32 devices in a mesh: ctx: 8 (over y, x, core), fsdp: 4 (over z).
Axes of the slice: x: 2, y: 2, z: 4, core: 2. Of those that a mesh axis runs over, the one named last changes fastest.
Arguments:
- tokens_in: bfloat16 [4, 1024, 1152], P('fsdp', 'ctx'), may hold values from -6 to 6
- doc_starts: int32 [4, 6], P('fsdp'), may hold values from 0 to 1023, as said below
- attn_gain: bfloat16 [1152], P('fsdp'), may hold values from 0.099609375 to 1.8984375
- query_weight: bfloat16 [1152, 1152], P('fsdp'), may hold values from -0.1875 to 0.1875
- key_weight: bfloat16 [1152, 384], P('fsdp'), may hold values from -0.1875 to 0.1875
- value_weight: bfloat16 [1152, 384], P('fsdp'), may hold values from -0.1875 to 0.1875
- output_weight: bfloat16 [1152, 1152], P('fsdp'), may hold values from -1.5 to 1.5
- ffn_gain: bfloat16 [1152], P('fsdp'), may hold values from 0.099609375 to 1.8984375
- gate_weight: bfloat16 [1152, 3072], P('fsdp'), may hold values from -0.1875 to 0.1875
- up_weight: bfloat16 [1152, 3072], P('fsdp'), may hold values from -0.1875 to 0.1875
- down_weight: bfloat16 [3072, 1152], P('fsdp'), may hold values from -0.109375 to 0.109375
- out_cotangent: bfloat16 [4, 1024, 1152], P('fsdp', 'ctx'), may hold values from -6 to 6
Outputs:
- layer_out: bfloat16 [4, 1024, 1152], P('fsdp', 'ctx')
- tokens_grad: bfloat16 [4, 1024, 1152], P('fsdp', 'ctx')
- attn_gain_grad: float32 [1152], P('fsdp')
- query_grad: float32 [1152, 1152], P('fsdp', 'ctx')
- key_grad: float32 [1152, 384], P('fsdp', 'ctx')
- value_grad: float32 [1152, 384], P('fsdp', 'ctx')
- output_grad: float32 [1152, 1152], P('fsdp', 'ctx')
- ffn_gain_grad: float32 [1152], P('fsdp')
- gate_grad: float32 [1152, 3072], P('fsdp', 'ctx')
- up_grad: float32 [1152, 3072], P('fsdp', 'ctx')
- down_grad: float32 [3072, 1152], P('fsdp', 'ctx')
The draws below stay inside these ranges and needn't reach their ends.
Inputs may be any that keep to these rules, and one draw needn't show every extreme that they name: doc_starts[s, 0] = 0; each row strictly increases.
All inputs are finite; a program needn't handle non-finite values.
Results may differ from the reference program's by a relative error of at most 0.017.
Values may be sent and summed in bfloat16 or wider, within the bound.
No kernel may reach another device: no remote copies, remote signals or barrier semaphores. Data moves between devices by JAX's collectives and lax.ppermute only.
A program may use at most 256 MiB of HBM per device.

```python
import math
import jax
import jax.numpy as jnp
from jax import lax

D = 1152
QUERY_HEADS = 18
KEY_VALUE_HEADS = 6
HEAD_SIZE = 64
FF = 3072
TOK_DEV = 128
DOCS = 6
QW = 1152
KW = 384
STREAM_TOKENS = 1024
STREAMS = 4
N_CTX = 8


def draw_doc_starts(key, part):
    half_len = TOK_DEV // 2
    middle = N_CTX * half_len
    rows_list = []
    for stream in range(STREAMS):
        sub_key = jax.random.fold_in(key, stream + 11)
        pick_key, second_key, tail_key = jax.random.split(sub_key, 3)
        long_index = jax.random.randint(pick_key, (), 0, 2).astype(jnp.int32)
        second = jax.random.randint(second_key, (1,), 1, half_len).astype(jnp.int32)
        chosen = jax.random.permutation(tail_key, STREAM_TOKENS - middle - 1)[:DOCS - 1].astype(jnp.int32)
        tail_starts = jnp.sort(chosen + (middle + 1)).astype(jnp.int32)
        with_second = jnp.concatenate([jnp.zeros((1,), jnp.int32), second, tail_starts[:DOCS - 2]])
        without_second = jnp.concatenate([jnp.zeros((1,), jnp.int32), tail_starts])
        rows_list.append(jnp.where(long_index == 1, with_second, without_second).astype(jnp.int32))
    return jnp.stack(rows_list).astype(jnp.int32)


def block_levels(stream_key, dims, cuts, least, largest):
    def one(axis_at, blocks):
        draws = jax.random.uniform(jax.random.fold_in(jax.random.fold_in(stream_key, 6), axis_at), (blocks,), jnp.float32, least / len(cuts), largest / len(cuts))
        return jnp.repeat(jnp.exp(draws), dims[axis_at] // blocks).reshape((-1,) + (1,) * (len(dims) - axis_at - 1))

    loudness = one(*cuts[0])
    for cut in cuts[1:]:
        loudness = loudness * one(*cut)
    return loudness


def gaussian(own_key, dims, spread, most, cuts=(), kind=jnp.bfloat16):
    array = spread * jax.random.normal(own_key, dims, jnp.float32)
    if cuts:
        array = array * block_levels(own_key, dims, cuts, -0.22, 0.18)
    return jnp.clip(array, -most, most).astype(kind)


def setup_inputs(seed: int = 0) -> dict:
    keys = jax.random.split(jax.random.key(seed), 13)
    return {
        "tokens_in": gaussian(keys[0], (STREAMS, STREAM_TOKENS, D), 1.0, 6.0, ((0, 4), (1, 8))),
        "doc_starts": draw_doc_starts(jax.random.fold_in(keys[12], 71), 0),
        "attn_gain": jnp.clip(1.0 + 0.18 * jax.random.normal(keys[2], (D,), jnp.float32), 0.099609375, 1.8984375).astype(jnp.bfloat16),
        "query_weight": gaussian(keys[3], (D, QW), D ** -0.5, 0.1875, ((0, 4),)),
        "key_weight": gaussian(keys[4], (D, KW), D ** -0.5, 0.1875, ((0, 4),)),
        "value_weight": gaussian(keys[5], (D, KW), D ** -0.5, 0.1875, ((0, 4),)),
        "output_weight": gaussian(keys[6], (QW, D), (QW // 64) ** -0.5, 1.5, ((0, 4),)),
        "ffn_gain": jnp.clip(1.0 + 0.18 * jax.random.normal(keys[7], (D,), jnp.float32), 0.099609375, 1.8984375).astype(jnp.bfloat16),
        "gate_weight": gaussian(keys[8], (D, FF), D ** -0.5, 0.1875, ((0, 4),)),
        "up_weight": gaussian(keys[9], (D, FF), D ** -0.5, 0.1875, ((0, 4),)),
        "down_weight": gaussian(keys[10], (FF, D), FF ** -0.5, 0.109375, ((0, 4),)),
        "out_cotangent": gaussian(keys[11], (STREAMS, STREAM_TOKENS, D), 1.0, 6.0, ((0, 4), (1, 8))),
    }


EPS = 1e-05
BASE = 10000.0
NEGATIVE_FILL = -1e+30

@jax.custom_vjp
def reduced_cast(v):
    return lax.optimization_barrier(v.astype(jnp.bfloat16)).astype(jnp.float32)

@jax.custom_vjp
def reduced_backward_cast(v):
    return v

def low_keep(v):
    return (reduced_cast(v), None)

def low_pass(kept, grad):
    return (grad,)

def back_keep(v):
    return (v, None)

def back_low(kept, grad):
    return (reduced_cast(grad),)
reduced_cast.defvjp(low_keep, low_pass)
reduced_backward_cast.defvjp(back_keep, back_low)

def matrix_product(left, right):
    return jnp.dot(left, right, precision=lax.Precision.HIGHEST, preferred_element_type=jnp.float32)

def rms_norm(values, gain):
    factor = lax.rsqrt(lax.optimization_barrier(jnp.mean(values * values, axis=-1, keepdims=True)) + EPS)
    return values * factor * gain

def stored_position(row_ids, rows_per_dev, devices_ctx):
    half_len = rows_per_dev // 2
    owner_dev = row_ids // rows_per_dev
    offset_in = row_ids % rows_per_dev
    early = owner_dev * half_len + offset_in
    later = (2 * devices_ctx - 1 - owner_dev) * half_len + offset_in - half_len
    return jnp.where(offset_in < half_len, early, later).astype(jnp.int32)

def rotate_half(values, cosine_table, sine_table, heads):
    count = values.shape[0]
    half = HEAD_SIZE // 2
    shaped = values.reshape(count, heads, HEAD_SIZE)
    first_half = shaped[..., :half]
    second_half = shaped[..., half:]
    cos_rows = cosine_table[:, None, :]
    sin_rows = sine_table[:, None, :]
    lower = first_half * cos_rows - second_half * sin_rows
    upper = second_half * cos_rows + first_half * sin_rows
    return jnp.concatenate([lower, upper], axis=-1).reshape(count, heads * HEAD_SIZE)

def stream_attention(rotated_queries, rotated_keys, reduced_values, doc_begin, positions):
    block_index = min(512, STREAM_TOKENS)
    block_count = STREAM_TOKENS // block_index
    group_size = QUERY_HEADS // KEY_VALUE_HEADS
    scale = HEAD_SIZE ** (-0.5)
    query_block_list = rotated_queries.reshape(block_count, block_index, KEY_VALUE_HEADS, group_size, HEAD_SIZE)
    begin_blocks = doc_begin.reshape(block_count, block_index)
    pos_blocks = positions.reshape(block_count, block_index)
    key_head_rows = rotated_keys.reshape(STREAM_TOKENS, KEY_VALUE_HEADS, HEAD_SIZE)
    value_head_rows = reduced_values.reshape(STREAM_TOKENS, KEY_VALUE_HEADS, HEAD_SIZE)
    key_pos = positions

    @jax.checkpoint
    def one_block(items):
        query_block, begin_block, pos_block = items
        raw = jnp.einsum('tkgd,skd->kgts', query_block, key_head_rows, precision=lax.Precision.HIGHEST)
        raw = reduced_backward_cast(raw)
        visible = (key_pos[None, :] >= begin_block[:, None]) & (key_pos[None, :] <= pos_block[:, None])
        scores = jnp.where(visible[None, None], raw * scale, NEGATIVE_FILL)
        probs = jax.nn.softmax(scores, axis=-1)
        mixed = jnp.einsum('kgts,skd->tkgd', reduced_cast(probs), value_head_rows, precision=lax.Precision.HIGHEST)
        return mixed.reshape(block_index, QUERY_HEADS * HEAD_SIZE)
    result = lax.map(one_block, (query_block_list, begin_blocks, pos_blocks))
    return result.reshape(STREAM_TOKENS, QUERY_HEADS * HEAD_SIZE)

def reference(tokens_in, doc_starts, attn_gain, query_weight, key_weight, value_weight, output_weight, ffn_gain, gate_weight, up_weight, down_weight, out_cotangent):
    row_ids = jnp.arange(STREAM_TOKENS, dtype=jnp.int32)
    positions = stored_position(row_ids, TOK_DEV, N_CTX)
    begins = lax.optimization_barrier(jnp.max(jnp.where(doc_starts[:, None, :] <= positions[None, :, None], doc_starts[:, None, :], 0), axis=-1))
    relative = (positions[None, :] - begins).astype(jnp.float32).reshape(-1)
    half = HEAD_SIZE // 2
    inv_freq = jnp.exp(-math.log(BASE) * 2.0 * jnp.arange(half, dtype=jnp.float32) / HEAD_SIZE)
    angles = relative[:, None] * inv_freq[None, :]
    cosine_table = jnp.cos(angles)
    sine_table = jnp.sin(angles)

    def forward(inputs_f, gain_one, query_w, key_projection, value_w, output_w, gain_two, gate_w, up_w, down_w):
        flat = inputs_f.reshape(-1, D)
        normalized_input = reduced_cast(rms_norm(flat, gain_one))
        rotated_queries = reduced_cast(rotate_half(reduced_backward_cast(matrix_product(normalized_input, query_w)), cosine_table, sine_table, QUERY_HEADS))
        rotated_keys = reduced_cast(rotate_half(reduced_backward_cast(matrix_product(normalized_input, key_projection)), cosine_table, sine_table, KEY_VALUE_HEADS))
        reduced_values = reduced_cast(reduced_backward_cast(matrix_product(normalized_input, value_w)))
        pieces = []
        for stream in range(STREAMS):
            lo_row = stream * STREAM_TOKENS
            pieces.append(stream_attention(rotated_queries[lo_row:lo_row + STREAM_TOKENS], rotated_keys[lo_row:lo_row + STREAM_TOKENS], reduced_values[lo_row:lo_row + STREAM_TOKENS], begins[stream], positions))
        attended = jnp.concatenate(pieces, axis=0)
        attended_low = reduced_cast(reduced_backward_cast(attended))
        hidden_in = flat + reduced_backward_cast(matrix_product(attended_low, output_w))
        ffn_in = reduced_cast(rms_norm(hidden_in, gain_two))
        gate = reduced_backward_cast(matrix_product(ffn_in, gate_w))
        upper = reduced_backward_cast(matrix_product(ffn_in, up_w))
        act_low = reduced_cast(jax.nn.silu(gate) * upper)
        result = hidden_in + matrix_product(act_low, down_w)
        return result.reshape(STREAMS, STREAM_TOKENS, D)
    primals = (tokens_in.astype(jnp.float32), attn_gain.astype(jnp.float32), query_weight.astype(jnp.float32), key_weight.astype(jnp.float32), value_weight.astype(jnp.float32), output_weight.astype(jnp.float32), ffn_gain.astype(jnp.float32), gate_weight.astype(jnp.float32), up_weight.astype(jnp.float32), down_weight.astype(jnp.float32))
    layer_out, pullback = jax.vjp(forward, *primals)
    grads = pullback(out_cotangent.astype(jnp.float32))
    return (layer_out.astype(jnp.bfloat16), grads[0].astype(jnp.bfloat16), grads[1], grads[2], grads[3], grads[4], grads[5], grads[6], grads[7], grads[8], grads[9])
```

```python
import functools
import math

import jax
import jax.numpy as jnp
import numpy as np
from jax import lax
from jax.experimental import pallas as pl
from jax.experimental.pallas import tpu as pltpu
from jax.sharding import PartitionSpec as P

QUERY_HEADS = 18
KEY_VALUE_HEADS = 6
HEAD_SIZE = 64
GROUP = QUERY_HEADS // KEY_VALUE_HEADS
HALF = HEAD_SIZE // 2

EPS = 1e-05
BASE = 10000.0
NEGATIVE_FILL = -1e30
BF = jnp.bfloat16
F32 = jnp.float32
VMEM_LIMIT = 56 * 1024 * 1024


def dot(left, right, left_dim, right_dim):
    return lax.dot_general(
        left, right, (((left_dim,), (right_dim,)), ((), ())), preferred_element_type=F32
    )


def rms_scale(values):
    return lax.rsqrt(jnp.mean(values * values, axis=-1, keepdims=True) + EPS)


def stored_position(row_ids, rows_per_dev, devices_ctx):
    half_len = rows_per_dev // 2
    owner_dev = row_ids // rows_per_dev
    offset_in = row_ids % rows_per_dev
    early = owner_dev * half_len + offset_in
    later = (2 * devices_ctx - 1 - owner_dev) * half_len + offset_in - half_len
    return jnp.where(offset_in < half_len, early, later)


def relative_ids(n):
    return np.array([2 * j + k for k in range(2) for j in range(n // 2)])


def hop(value, n, bits):
    return lax.ppermute(value, "ctx", [(i, i ^ bits) for i in range(n)])


def relative_index(bits, n):
    return (bits % 2) * (n // 2) + bits // 2


def blocks_at(values, indices, axis):
    picked = [lax.dynamic_slice_in_dim(values, i, 1, axis=axis) for i in indices]
    return jnp.concatenate(picked, axis=axis)


def absolute_of(rel_values, n, axis=0):
    me = lax.axis_index("ctx")
    return blocks_at(rel_values, [relative_index(me ^ d, n) for d in range(n)], axis)


def relative_of(values, n, axis=0):
    me = lax.axis_index("ctx")
    return blocks_at(values, [me ^ int(r) for r in relative_ids(n)], axis)


def gather_rel(value, n):
    if n > 8:
        return relative_of(lax.all_gather(value, "ctx"), n)
    same = jnp.stack([value] + [hop(value, n, 2 * j) for j in range(1, n // 2)])
    return jnp.concatenate([same, hop(same, n, 1)])


def scatter_rel(parts, n):
    if n > 8:
        return lax.psum_scatter(absolute_of(parts, n), "ctx", scatter_dimension=0)
    half = n // 2
    mine = parts[:half].astype(F32) + hop(parts[half:], n, 1).astype(F32)
    total = mine[0]
    sent = mine[1:].astype(parts.dtype)
    for j in range(1, half):
        total = total + hop(sent[j - 1], n, 2 * j).astype(F32)
    return total


def exchange_rel(parts, n):
    if n > 8:
        moved = lax.all_to_all(absolute_of(parts, n), "ctx", 0, 0, tiled=True)
        return relative_of(moved, n)
    half = n // 2
    both = jnp.stack([parts[:half], hop(parts[half:], n, 1)], axis=1)
    got = jnp.stack([both[0]] + [hop(both[j], n, 2 * j) for j in range(1, half)])
    return got.swapaxes(0, 1).reshape(parts.shape)


def turn(values, cosine, sine, sign):
    heads = values.shape[0] // HEAD_SIZE
    pieces = []
    for h in range(heads):
        first = values[HEAD_SIZE * h : HEAD_SIZE * h + HALF]
        second = values[HEAD_SIZE * h + HALF : HEAD_SIZE * (h + 1)]
        pieces.append(first * cosine - sign * (second * sine))
        pieces.append(second * cosine + sign * (first * sine))
    return jnp.concatenate(pieces, axis=0)


def mask_bias(kpos, qpos, qbeg):
    visible = (kpos >= qbeg) & (kpos <= qpos)
    return jnp.where(visible, 0.0, NEGATIVE_FILL).astype(F32)


def group_columns(ref, h):
    return jnp.concatenate(
        [ref[HEAD_SIZE * (GROUP * h + g) : HEAD_SIZE * (GROUP * h + g + 1), :] for g in range(GROUP)],
        axis=1,
    )


def attention_forward_kernel(
    q_ref, k_ref, v_ref, cosk_ref, sink_ref, kpos_ref, cosq_ref, sinq_ref, qpos_ref, qbeg_ref,
    att_ref, low_ref, lse_ref, qrot_ref, krot_ref,
    max_ref, sum_ref,
):
    step = pl.program_id(0)
    steps = pl.num_programs(0)
    tokens = q_ref.shape[1]

    @pl.when(step == 0)
    def _():
        turned = turn(q_ref[...].astype(F32), cosq_ref[...], sinq_ref[...], 1.0).astype(BF)
        qrot_ref[...] = turned * BF(HEAD_SIZE**-0.5)
        max_ref[...] = jnp.full(max_ref.shape, NEGATIVE_FILL, F32)
        sum_ref[...] = jnp.zeros(sum_ref.shape, F32)
        att_ref[...] = jnp.zeros(att_ref.shape, F32)

    krot_ref[...] = turn(k_ref[...].astype(F32), cosk_ref[...], sink_ref[...], 1.0).astype(BF)
    bias = mask_bias(kpos_ref[...], qpos_ref[...], qbeg_ref[...])
    bias = jnp.concatenate([bias] * GROUP, axis=1)
    for h in range(KEY_VALUE_HEADS):
        rows = slice(HEAD_SIZE * h, HEAD_SIZE * (h + 1))
        scores = dot(krot_ref[rows, :], group_columns(qrot_ref, h), 0, 0) + bias
        old_max = max_ref[h : h + 1, :]
        new_max = jnp.maximum(old_max, jnp.max(scores, axis=0, keepdims=True))
        weights = jnp.exp(scores - new_max)
        fade = jnp.exp(old_max - new_max)
        sum_ref[h : h + 1, :] = sum_ref[h : h + 1, :] * fade + jnp.sum(weights, axis=0, keepdims=True)
        max_ref[h : h + 1, :] = new_max
        mixed = dot(v_ref[rows, :], weights.astype(BF), 1, 0)
        for g in range(GROUP):
            at = slice(HEAD_SIZE * (GROUP * h + g), HEAD_SIZE * (GROUP * h + g + 1))
            lanes = slice(tokens * g, tokens * (g + 1))
            att_ref[at, :] = att_ref[at, :] * fade[:, lanes] + mixed[:, lanes]

    @pl.when(step == steps - 1)
    def _():
        for h in range(KEY_VALUE_HEADS):
            total = sum_ref[h : h + 1, :]
            lse_ref[h : h + 1, :] = max_ref[h : h + 1, :] + jnp.log(total)
            for g in range(GROUP):
                at = slice(HEAD_SIZE * (GROUP * h + g), HEAD_SIZE * (GROUP * h + g + 1))
                att_ref[at, :] = att_ref[at, :] / total[:, tokens * g : tokens * (g + 1)]
        low_ref[...] = att_ref[...].T.astype(BF)


def attention_backward_kernel(
    q_ref, k_ref, v_ref, do_ref, att_ref, lse_ref,
    cosk_ref, sink_ref, kpos_ref, cosq_ref, sinq_ref, qpos_ref, qbeg_ref,
    dq_ref, dk_ref, dv_ref,
    acc_ref,
):
    step = pl.program_id(0)
    steps = pl.num_programs(0)
    tokens = q_ref.shape[1]

    @pl.when(step == 0)
    def _():
        acc_ref[...] = jnp.zeros(acc_ref.shape, F32)

    bias = mask_bias(kpos_ref[...], qpos_ref[...], qbeg_ref[...])
    bias = jnp.concatenate([bias] * GROUP, axis=1)
    for h in range(KEY_VALUE_HEADS):
        rows = slice(HEAD_SIZE * h, HEAD_SIZE * (h + 1))
        queries = group_columns(q_ref, h)
        grads = group_columns(do_ref, h)
        delta = jnp.sum(grads.astype(F32) * group_columns(att_ref, h), axis=0, keepdims=True)
        scores = dot(k_ref[rows, :], queries, 0, 0) + bias
        probs = jnp.exp(scores - lse_ref[h : h + 1, :])
        d_probs = dot(v_ref[rows, :], grads, 0, 0)
        d_score = (probs * (d_probs - delta)).astype(BF)
        d_query = dot(k_ref[rows, :], d_score, 1, 0)
        for g in range(GROUP):
            at = slice(HEAD_SIZE * (GROUP * h + g), HEAD_SIZE * (GROUP * h + g + 1))
            acc_ref[at, :] += d_query[:, tokens * g : tokens * (g + 1)]
        d_key = dot(queries, d_score, 1, 1)
        dk_ref[rows, :] = turn(d_key, cosk_ref[...], sink_ref[...], -1.0).astype(BF)
        dv_ref[rows, :] = dot(grads, probs.astype(BF), 1, 1).astype(BF)

    @pl.when(step == steps - 1)
    def _():
        scaled = acc_ref[...] * (HEAD_SIZE**-0.5)
        dq_ref[...] = turn(scaled, cosq_ref[...], sinq_ref[...], -1.0).astype(BF)


def whole(shape):
    return pl.BlockSpec(shape, lambda g: (0,) * len(shape))


def key_columns(rows, block):
    return pl.BlockSpec((rows, block), lambda g: (0, g))


def attention_forward(q_raw, k_raw, v_low, tables):
    cosk, sink, kpos, cosq, sinq, qpos, qbeg = tables
    width, tokens = q_raw.shape
    key_width, length = k_raw.shape
    block = math.gcd(length, 1024)
    return pl.pallas_call(
        attention_forward_kernel,
        grid=(length // block,),
        in_specs=[
            whole(q_raw.shape), key_columns(key_width, block), key_columns(key_width, block),
            key_columns(HALF, block), key_columns(HALF, block),
            pl.BlockSpec((block, 1), lambda g: (g, 0)),
            whole(cosq.shape), whole(sinq.shape), whole(qpos.shape), whole(qbeg.shape),
        ],
        out_specs=[
            whole((width, tokens)), whole((tokens, width)), whole((KEY_VALUE_HEADS, GROUP * tokens)),
            whole((width, tokens)), key_columns(key_width, block),
        ],
        out_shape=[
            jax.ShapeDtypeStruct((width, tokens), F32),
            jax.ShapeDtypeStruct((tokens, width), BF),
            jax.ShapeDtypeStruct((KEY_VALUE_HEADS, GROUP * tokens), F32),
            jax.ShapeDtypeStruct((width, tokens), BF),
            jax.ShapeDtypeStruct((key_width, length), BF),
        ],
        scratch_shapes=[
            pltpu.VMEM((KEY_VALUE_HEADS, GROUP * tokens), F32),
            pltpu.VMEM((KEY_VALUE_HEADS, GROUP * tokens), F32),
        ],
        compiler_params=pltpu.CompilerParams(vmem_limit_bytes=VMEM_LIMIT),
        name="attention_forward",
    )(q_raw, k_raw, v_low, cosk, sink, kpos, cosq, sinq, qpos, qbeg)


def attention_backward(q_rot, k_rot, v_low, d_att, att, lse, tables):
    cosk, sink, kpos, cosq, sinq, qpos, qbeg = tables
    width, tokens = q_rot.shape
    key_width, length = k_rot.shape
    block = math.gcd(length, 1024)
    return pl.pallas_call(
        attention_backward_kernel,
        grid=(length // block,),
        in_specs=[
            whole(q_rot.shape), key_columns(key_width, block), key_columns(key_width, block),
            whole(d_att.shape), whole(att.shape), whole(lse.shape),
            key_columns(HALF, block), key_columns(HALF, block),
            pl.BlockSpec((block, 1), lambda g: (g, 0)),
            whole(cosq.shape), whole(sinq.shape), whole(qpos.shape), whole(qbeg.shape),
        ],
        out_specs=[
            whole((width, tokens)), key_columns(key_width, block), key_columns(key_width, block),
        ],
        out_shape=[
            jax.ShapeDtypeStruct((width, tokens), BF),
            jax.ShapeDtypeStruct((key_width, length), BF),
            jax.ShapeDtypeStruct((key_width, length), BF),
        ],
        scratch_shapes=[pltpu.VMEM((width, tokens), F32)],
        compiler_params=pltpu.CompilerParams(vmem_limit_bytes=VMEM_LIMIT),
        name="attention_backward",
    )(q_rot, k_rot, v_low, d_att, att, lse, cosk, sink, kpos, cosq, sinq, qpos, qbeg)


def assemble_kernel(me_ref, same_ref, other_ref, q_ref, k_ref, v_ref):
    half, flat_rows = same_ref.shape[:2]
    n = 2 * half
    tokens = same_ref.shape[2]
    qc, kc = q_ref.shape[0] // n, k_ref.shape[0] // n
    flat_rows = 2 * kc * n
    rel = relative_ids(n)
    inverse = np.argsort(rel)
    for i in range(n):
        device = me_ref[0] ^ int(rel[i])
        source, j = (same_ref, i) if i < half else (other_ref, i - half)
        at = flat_rows + (0 if i < half else qc)
        q_ref[pl.ds(pl.multiple_of(device * qc, 16), qc), :] = source[j, at : at + qc, :]
        to = pl.ds(pl.multiple_of(device * kc, 16), kc)
        for b in range(n):
            start = 2 * kc * int(inverse[rel[b] ^ rel[i]])
            lanes = slice(tokens * b, tokens * (b + 1))
            k_ref[to, lanes] = source[j, start : start + kc, :]
            v_ref[to, lanes] = source[j, start + kc : start + 2 * kc, :]


def assemble(me, same, other, query_width, key_width, length):
    vmem = pl.BlockSpec(memory_space=pltpu.VMEM)
    tokens = same.shape[2]
    return pl.pallas_call(
        assemble_kernel,
        in_specs=[pl.BlockSpec(memory_space=pltpu.SMEM), vmem, vmem],
        out_specs=[vmem] * 3,
        out_shape=[
            jax.ShapeDtypeStruct((query_width, tokens), BF),
            jax.ShapeDtypeStruct((key_width, length), BF),
            jax.ShapeDtypeStruct((key_width, length), BF),
        ],
        name="assemble",
    )(me, same, other)


def pack_kernel(me_ref, dq_ref, db_ref, dk_ref, dv_ref, out_ref):
    n = out_ref.shape[0]
    tokens = out_ref.shape[2]
    qc, dc, kc = dq_ref.shape[0] // n, db_ref.shape[0] // n, dk_ref.shape[0] // n
    flat_rows = 2 * kc * n
    rel = relative_ids(n)
    inverse = np.argsort(rel)
    for i in range(n):
        device = me_ref[0] ^ int(rel[i])
        out_ref[i, flat_rows : flat_rows + qc, :] = dq_ref[
            pl.ds(pl.multiple_of(device * qc, 16), qc), :
        ]
        out_ref[i, flat_rows + qc : flat_rows + qc + dc, :] = db_ref[
            pl.ds(pl.multiple_of(device * dc, 16), dc), :
        ]
        rows = pl.ds(pl.multiple_of(device * kc, 16), kc)
        for b in range(n):
            start = 2 * kc * int(inverse[rel[b] ^ rel[i]])
            lanes = slice(tokens * b, tokens * (b + 1))
            out_ref[i, start : start + kc, :] = dk_ref[rows, lanes]
            out_ref[i, start + kc : start + 2 * kc, :] = dv_ref[rows, lanes]


def pack(me, d_q, d_b, d_k, d_v, n):
    vmem = pl.BlockSpec(memory_space=pltpu.VMEM)
    rows = 2 * d_k.shape[0] + (d_q.shape[0] + d_b.shape[0]) // n
    return pl.pallas_call(
        pack_kernel,
        in_specs=[pl.BlockSpec(memory_space=pltpu.SMEM)] + [vmem] * 4,
        out_specs=vmem,
        out_shape=jax.ShapeDtypeStruct((n, rows, d_q.shape[1]), BF),
        name="pack",
    )(me, d_q, d_b, d_k, d_v)


def column_slice(weight, index, width):
    return lax.dynamic_slice_in_dim(weight, index * width, width, axis=1)


def local(
    tokens_in,
    doc_starts,
    attn_gain,
    query_weight,
    key_weight,
    value_weight,
    output_weight,
    ffn_gain,
    gate_weight,
    up_weight,
    down_weight,
    out_cotangent,
):
    n = lax.axis_size("ctx")
    operands = (
        tokens_in, doc_starts, attn_gain, query_weight, key_weight, value_weight, output_weight,
        ffn_gain, gate_weight, up_weight, down_weight, out_cotangent,
    )
    if n > 8:
        return local_gathered(*operands)
    depth = lax.axis_size("fsdp")
    me = lax.axis_index("ctx")
    level = lax.axis_index("fsdp")
    tokens, width = tokens_in.shape[1:]
    length = n * tokens
    query_width, key_width = query_weight.shape[1], key_weight.shape[1]
    qc, kc, dc = query_width // n, key_width // n, width // n
    hidden_units = gate_weight.shape[1]
    fc = hidden_units // n
    rows = query_weight.shape[0]
    rel = relative_ids(n)
    tiled = n <= 8 and qc % 16 == 0 and kc % 16 == 0 and dc % 16 == 0 and tokens % 128 == 0

    first_shard = jnp.concatenate(
        [
            column_slice(query_weight, me, qc),
            column_slice(key_weight, me, kc),
            column_slice(value_weight, me, kc),
            attn_gain[:, None],
            ffn_gain[:, None],
        ],
        axis=1,
    )
    first = lax.all_gather(first_shard, "fsdp", axis=0, tiled=True)
    qkv_weight = first[:, : qc + 2 * kc]
    gain_one = first[:, qc + 2 * kc].astype(F32)[None, :]
    gain_two = first[:, qc + 2 * kc + 1].astype(F32)[None, :]

    x_all = gather_rel(tokens_in[0], n).reshape(length, width)

    out_gate_shard = jnp.concatenate(
        [column_slice(output_weight, me, dc), column_slice(gate_weight, me, fc)], axis=1
    )
    out_gate = lax.all_gather(out_gate_shard, "fsdp", axis=0, tiled=True)
    down_rows = down_weight.shape[0] // n
    down_piece = lax.dynamic_slice_in_dim(down_weight, me * down_rows, down_rows, axis=0)
    per_row = width // fc if width % fc == 0 else 0
    if per_row and per_row * down_rows == rows:
        down_flat = jnp.concatenate(
            [down_piece[:, fc * i : fc * (i + 1)] for i in range(per_row)], axis=0
        )
        up_down_shard = jnp.concatenate([column_slice(up_weight, me, fc), down_flat], axis=1)
        up_down = lax.all_gather(up_down_shard, "fsdp", axis=0, tiled=True)
        up_columns = up_down[:, :fc]
        flat = up_down[:, fc:].reshape(depth, per_row, down_rows, fc)
        down_parts = jnp.concatenate([flat[:, i] for i in range(per_row)], axis=-1)
    else:
        up_columns = lax.all_gather(column_slice(up_weight, me, fc), "fsdp", axis=0, tiled=True)
        down_parts = lax.all_gather(down_piece, "fsdp")
    output_t = absolute_of(gather_rel(out_gate[:, :dc].T, n), n).reshape(width, query_width)
    gate_columns = out_gate[:, dc:]
    share = n // depth
    arrived = []
    for t in range(depth):
        chunk = lax.dynamic_index_in_dim(down_parts, (me % depth) ^ t, 0, keepdims=False)
        arrived.append(
            lax.ppermute(
                chunk, "ctx", [(i, ((i % depth) ^ t) * share + i // depth) for i in range(n)]
            )
        )
    down_own = blocks_at(jnp.stack(arrived), [(me // share) ^ i for i in range(depth)], 0)
    down_own = down_own.reshape(fc, width)

    devices = jnp.asarray(rel) ^ me
    row_ids = (devices[:, None] * tokens + jnp.arange(tokens)[None, :]).reshape(-1)
    positions = stored_position(row_ids.astype(jnp.int32), tokens, n)
    starts = doc_starts[0]
    begins = jnp.max(
        jnp.where(starts[None, :] <= positions[:, None], starts[None, :], 0), axis=1
    )
    inv_freq = jnp.exp(-math.log(BASE) * 2.0 * jnp.arange(HALF, dtype=F32) / HEAD_SIZE)
    angles = inv_freq[:, None] * (positions - begins).astype(F32)[None, :]
    cosine, sine = jnp.cos(angles), jnp.sin(angles)
    tables = (
        cosine, sine, positions[:, None], cosine[:, :tokens], sine[:, :tokens],
        positions[None, :tokens], begins[None, :tokens],
    )

    x_f = x_all.astype(F32)
    scale_one = rms_scale(x_f)
    normed_in = (x_f * scale_one * gain_one).astype(BF)
    qkv_t = dot(qkv_weight, normed_in, 0, 1).astype(BF)
    blocks = qkv_t.reshape(qc + 2 * kc, n, tokens).swapaxes(0, 1)
    q_parts = blocks[:, :qc]
    kv_parts = blocks[:, qc:]
    if tiled:
        half = n // 2
        kv_flat = kv_parts.reshape(n * 2 * kc, tokens)
        messages = [
            jnp.concatenate([kv_flat, q_parts[j], q_parts[half + j]]) for j in range(half)
        ]
        same = jnp.stack([messages[0]] + [hop(messages[j], n, 2 * j) for j in range(1, half)])
        other = hop(same, n, 1)
        q_raw, k_raw, v_low = assemble(me[None], same, other, query_width, key_width, length)
    else:
        q_raw = absolute_of(exchange_rel(q_parts, n), n).reshape(query_width, tokens)
        kv = absolute_of(gather_rel(absolute_of(kv_parts, n), n), n)
        kv = relative_of(kv, n, axis=1).swapaxes(1, 2)
        k_raw = kv[:, :kc].reshape(key_width, length)
        v_low = kv[:, kc:].reshape(key_width, length)

    att, attended_low, lse, q_rot, k_rot = attention_forward(q_raw, k_raw, v_low, tables)

    g_all = gather_rel(out_cotangent[0], n).reshape(length, width)

    attended_all = gather_rel(attended_low, n).reshape(length, query_width)
    hidden = x_f + dot(attended_all, output_t, 1, 1)
    scale_two = rms_scale(hidden)
    normed_two = hidden * scale_two
    ffn_in = (normed_two * gain_two).astype(BF)
    gate = dot(ffn_in, gate_columns, 1, 0)
    upper = dot(ffn_in, up_columns, 1, 0)
    sigma = jax.nn.sigmoid(gate)
    act_low = (gate * sigma * upper).astype(BF)
    d_act = dot(g_all, down_own, 1, 1)
    d_gate = (d_act * upper * sigma * (1.0 + gate * (1.0 - sigma))).astype(BF)
    d_up = (d_act * gate * sigma).astype(BF)
    d_ffn_part = dot(d_gate, gate_columns, 1, 1) + dot(d_up, up_columns, 1, 1)
    gain_two_part = jnp.sum(d_ffn_part * normed_two, axis=0)
    d_ffn_in = scatter_rel(d_ffn_part.astype(BF).reshape(n, tokens, width), n)
    down_part = dot(act_low, down_own, 1, 0)
    down_out = scatter_rel(down_part.astype(BF).reshape(n, tokens, width), n)
    hidden_own = hidden[:tokens]
    layer_out = (hidden_own + down_out).astype(BF)

    gate_up_grad = jnp.concatenate([dot(ffn_in, d_gate, 0, 0), dot(ffn_in, d_up, 0, 0)], axis=1)
    down_grad_t = dot(g_all, act_low, 0, 0).astype(BF).reshape(n, dc, fc)
    down_grad_t = absolute_of(exchange_rel(relative_of(down_grad_t, n), n), n)
    down_grad_t = down_grad_t.swapaxes(0, 1).reshape(dc, hidden_units)
    gate_up_sum = lax.psum_scatter(
        gate_up_grad.astype(BF), "fsdp", scatter_dimension=0, tiled=True
    ).astype(F32)
    down_sum = lax.psum_scatter(down_grad_t.T, "fsdp", scatter_dimension=0, tiled=True).astype(F32)

    g_own = out_cotangent[0].astype(F32)
    normed_two_own = normed_two[:tokens]
    scaled_two = d_ffn_in.astype(F32) * gain_two
    d_hidden = g_own + scale_two[:tokens] * (
        scaled_two - normed_two_own * jnp.mean(scaled_two * normed_two_own, axis=-1, keepdims=True)
    )
    d_branch = d_hidden.astype(BF)
    d_att = dot(output_t, d_branch, 0, 1).astype(BF)
    d_branch_t = d_branch.T.reshape(n, dc, tokens)

    d_q, d_k, d_v = attention_backward(q_rot, k_rot, v_low, d_att, att, lse, tables)
    if tiled:
        half = n // 2
        flat_rows = n * 2 * kc
        messages = pack(me[None], d_q, d_branch_t.reshape(width, tokens), d_k, d_v, n)
        other = hop(messages[half:], n, 1)
        kv_pair = messages[:half, :flat_rows].astype(F32) + other[:, :flat_rows].astype(F32)
        onward = jnp.concatenate(
            [kv_pair.astype(BF), messages[:half, flat_rows:], other[:, flat_rows:]], axis=1
        )
        got = [onward[0]] + [hop(onward[j], n, 2 * j) for j in range(1, half)]
        d_kv_own = kv_pair[0]
        for piece in got[1:]:
            d_kv_own = d_kv_own + piece[:flat_rows].astype(F32)
        d_kv_own = d_kv_own.reshape(n, 2 * kc, tokens)
        ends = [flat_rows, flat_rows + qc + dc]
        d_q_own = jnp.stack([piece[e : e + qc] for e in ends for piece in got])
        d_b_own = jnp.stack([piece[e + qc : e + qc + dc] for e in ends for piece in got])
    else:
        d_q_own = exchange_rel(relative_of(d_q.reshape(n, qc, tokens), n), n)
        d_b_own = exchange_rel(relative_of(d_branch_t, n), n)
        d_kv = jnp.concatenate([d_k.reshape(n, kc, length), d_v.reshape(n, kc, length)], axis=1)
        d_kv = absolute_of(d_kv.reshape(n, 2 * kc, n, tokens).swapaxes(1, 2), n, axis=1)
        d_kv_own = relative_of(scatter_rel(relative_of(d_kv, n), n), n)
    d_qkv = jnp.concatenate([d_q_own, d_kv_own.astype(BF)], axis=1)
    d_qkv = d_qkv.swapaxes(0, 1).reshape(qc + 2 * kc, length)
    d_b_own = d_b_own.swapaxes(0, 1).reshape(dc, length)

    qkv_grad = dot(normed_in, d_qkv, 0, 1)
    output_grad = dot(attended_all, d_b_own, 0, 1)
    d_normed_part = dot(d_qkv, qkv_weight, 0, 1)
    gain_one_part = jnp.sum(d_normed_part * (x_f * scale_one), axis=0)
    d_normed = scatter_rel(d_normed_part.astype(BF).reshape(n, tokens, width), n)
    normed_one = x_f[:tokens] * scale_one[:tokens]
    scaled_one = d_normed.astype(F32) * gain_one
    tokens_grad = d_hidden + scale_one[:tokens] * (
        scaled_one - normed_one * jnp.mean(scaled_one * normed_one, axis=-1, keepdims=True)
    )

    last = jnp.concatenate(
        [qkv_grad, output_grad, gain_one_part[:, None], gain_two_part[:, None]], axis=1
    ).reshape(depth, rows, -1)
    last_own = lax.dynamic_index_in_dim(last, level, 0, keepdims=False)
    low = last.astype(BF)
    for k in range(1, depth):
        sent = lax.dynamic_index_in_dim(low, level ^ k, 0, keepdims=False)
        last_own = last_own + lax.ppermute(
            sent, "fsdp", [(i, i ^ k) for i in range(depth)]
        ).astype(F32)
    gains = lax.psum(last_own[:, -2:], "ctx")
    at = qc + 2 * kc
    return (
        layer_out[None],
        tokens_grad.astype(BF)[None],
        gains[:, 0],
        last_own[:, :qc],
        last_own[:, qc : qc + kc],
        last_own[:, qc + kc : at],
        last_own[:, at : at + dc],
        gains[:, 1],
        gate_up_sum[:, :fc],
        gate_up_sum[:, fc:],
        down_sum,
    )


def rotate_half(values, cosine_table, sine_table, heads, forward):
    count = values.shape[0]
    half = HEAD_SIZE // 2
    shaped = values.reshape(count, heads, HEAD_SIZE)
    first_half = shaped[..., :half]
    second_half = shaped[..., half:]
    cos_rows = cosine_table[:, None, :]
    sin_rows = sine_table[:, None, :]
    if forward:
        lower = first_half * cos_rows - second_half * sin_rows
        upper = second_half * cos_rows + first_half * sin_rows
    else:
        lower = first_half * cos_rows + second_half * sin_rows
        upper = second_half * cos_rows - first_half * sin_rows
    return jnp.concatenate([lower, upper], axis=-1).reshape(count, heads * HEAD_SIZE)


def local_gathered(
    tokens_in,
    doc_starts,
    attn_gain,
    query_weight,
    key_weight,
    value_weight,
    output_weight,
    ffn_gain,
    gate_weight,
    up_weight,
    down_weight,
    out_cotangent,
):
    present_rows = tokens_in.shape[1]
    devices_ctx = lax.axis_size("ctx")
    group_size = QUERY_HEADS // KEY_VALUE_HEADS
    scale = HEAD_SIZE ** (-0.5)
    inputs_f = tokens_in[0].astype(jnp.float32)
    gain_one, query_full, key_full, value_full, output_full = (
        lax.all_gather(attn_gain, "fsdp", axis=0, tiled=True),
        lax.all_gather(query_weight, "fsdp", axis=0, tiled=True),
        lax.all_gather(key_weight, "fsdp", axis=0, tiled=True),
        lax.all_gather(value_weight, "fsdp", axis=0, tiled=True),
        lax.all_gather(output_weight, "fsdp", axis=0, tiled=True),
    )
    gain_one = gain_one.astype(jnp.float32)
    scale_one = rms_scale(inputs_f)
    normed_one = inputs_f * scale_one
    normalized_input = (normed_one * gain_one).astype(jnp.bfloat16)
    query_raw = jnp.dot(normalized_input, query_full, preferred_element_type=jnp.float32)
    key_unrotated = jnp.dot(normalized_input, key_full, preferred_element_type=jnp.float32)
    value_raw = jnp.dot(normalized_input, value_full, preferred_element_type=jnp.float32)
    local_rows = lax.axis_index("ctx") * present_rows + jnp.arange(present_rows, dtype=jnp.int32)
    token_pos = stored_position(local_rows, present_rows, devices_ctx)
    starts_row = doc_starts[0]
    doc_begin = jnp.max(
        jnp.where(starts_row[None, :] <= token_pos[:, None], starts_row[None, :], 0), axis=1
    )
    relative = (token_pos - doc_begin).astype(jnp.float32)
    inv_freq = jnp.exp(
        -math.log(BASE) * 2.0 * jnp.arange(HEAD_SIZE // 2, dtype=jnp.float32) / HEAD_SIZE
    )
    angles = relative[:, None] * inv_freq[None, :]
    cosine_table = jnp.cos(angles)
    sine_table = jnp.sin(angles)
    rotated_queries = rotate_half(query_raw, cosine_table, sine_table, QUERY_HEADS, True).astype(
        jnp.bfloat16
    )
    rotated_keys = rotate_half(
        key_unrotated, cosine_table, sine_table, KEY_VALUE_HEADS, True
    ).astype(jnp.bfloat16)
    reduced_values = value_raw.astype(jnp.bfloat16)
    key_gathered, value_gathered = (
        lax.all_gather(rotated_keys, "ctx", axis=0, tiled=True),
        lax.all_gather(reduced_values, "ctx", axis=0, tiled=True),
    )
    stream_len = key_gathered.shape[0]
    block_index = min(512, stream_len)
    block_count = stream_len // block_index
    key_block_list = key_gathered.reshape(block_count, block_index, KEY_VALUE_HEADS, HEAD_SIZE)
    value_block_list = value_gathered.reshape(block_count, block_index, KEY_VALUE_HEADS, HEAD_SIZE)
    key_positions = stored_position(
        jnp.arange(stream_len, dtype=jnp.int32), present_rows, devices_ctx
    )
    position_blocks = key_positions.reshape(block_count, block_index)
    grouped_queries = rotated_queries.reshape(present_rows, KEY_VALUE_HEADS, group_size, HEAD_SIZE)

    def scores_of(key_block, key_pos):
        raw = jnp.einsum(
            "tkgd,skd->kgts", grouped_queries, key_block, preferred_element_type=jnp.float32
        )
        visible = (key_pos[None, :] >= doc_begin[:, None]) & (
            key_pos[None, :] <= token_pos[:, None]
        )
        return (jnp.where(visible[None, None], raw * scale, NEGATIVE_FILL), visible)

    def stats_step(carry, items):
        running_max, running_sum = carry
        key_block, key_pos = items
        scores, visible = scores_of(key_block, key_pos)
        new_max = jnp.maximum(running_max, jnp.max(scores, axis=-1))
        weights = jnp.where(visible[None, None], jnp.exp(scores - new_max[..., None]), 0.0)
        running_sum = running_sum * jnp.exp(running_max - new_max) + jnp.sum(weights, axis=-1)
        return ((new_max, running_sum), None)

    stat_init = (
        jnp.full((KEY_VALUE_HEADS, group_size, present_rows), NEGATIVE_FILL, jnp.float32),
        jnp.zeros((KEY_VALUE_HEADS, group_size, present_rows), jnp.float32),
    )
    (row_max, row_sum), unused = lax.scan(stats_step, stat_init, (key_block_list, position_blocks))
    log_total = row_max + jnp.log(row_sum)

    def probs_of(key_block, key_pos):
        scores, visible = scores_of(key_block, key_pos)
        return jnp.where(visible[None, None], jnp.exp(scores - log_total[..., None]), 0.0)

    def value_step(carry, items):
        key_block, value_block, key_pos = items
        probs_low = probs_of(key_block, key_pos).astype(jnp.bfloat16)
        return (
            carry
            + jnp.einsum(
                "kgts,skd->tkgd", probs_low, value_block, preferred_element_type=jnp.float32
            ),
            None,
        )

    attn_rows, unused = lax.scan(
        value_step,
        jnp.zeros((present_rows, KEY_VALUE_HEADS, group_size, HEAD_SIZE), jnp.float32),
        (key_block_list, value_block_list, position_blocks),
    )
    query_width = rotated_queries.shape[1]
    attended_low = attn_rows.reshape(present_rows, query_width).astype(jnp.bfloat16)
    hidden_in = inputs_f + jnp.dot(attended_low, output_full, preferred_element_type=jnp.float32)
    gain_two, gate_full, up_full, down_full = (
        lax.all_gather(ffn_gain, "fsdp", axis=0, tiled=True),
        lax.all_gather(gate_weight, "fsdp", axis=0, tiled=True),
        lax.all_gather(up_weight, "fsdp", axis=0, tiled=True),
        lax.all_gather(down_weight, "fsdp", axis=0, tiled=True),
    )
    gain_two = gain_two.astype(jnp.float32)
    scale_two = rms_scale(hidden_in)
    normed_two = hidden_in * scale_two
    ffn_in = (normed_two * gain_two).astype(jnp.bfloat16)
    gate = jnp.dot(ffn_in, gate_full, preferred_element_type=jnp.float32)
    upper = jnp.dot(ffn_in, up_full, preferred_element_type=jnp.float32)
    sigma = jax.nn.sigmoid(gate)
    act_low = (gate * sigma * upper).astype(jnp.bfloat16)
    layer_out = (
        hidden_in + jnp.dot(act_low, down_full, preferred_element_type=jnp.float32)
    ).astype(jnp.bfloat16)
    cot_rows = out_cotangent[0]
    cot_f = cot_rows.astype(jnp.float32)
    down_local = jnp.dot(act_low.T, cot_rows, preferred_element_type=jnp.float32)
    d_act = jnp.dot(cot_rows, down_full.T, preferred_element_type=jnp.float32)
    d_gate = (d_act * upper * sigma * (1.0 + gate * (1.0 - sigma))).astype(jnp.bfloat16)
    d_up = (d_act * gate * sigma).astype(jnp.bfloat16)
    gate_local = jnp.dot(ffn_in.T, d_gate, preferred_element_type=jnp.float32)
    up_local = jnp.dot(ffn_in.T, d_up, preferred_element_type=jnp.float32)
    d_ffn_in = jnp.dot(d_gate, gate_full.T, preferred_element_type=jnp.float32) + jnp.dot(
        d_up, up_full.T, preferred_element_type=jnp.float32
    )
    gain_two_local = jnp.sum(d_ffn_in * normed_two, axis=0)
    scaled_two = d_ffn_in * gain_two
    d_hidden = cot_f + scale_two * (
        scaled_two - normed_two * jnp.mean(scaled_two * normed_two, axis=-1, keepdims=True)
    )
    d_branch = d_hidden.astype(jnp.bfloat16)
    output_local = jnp.dot(attended_low.T, d_branch, preferred_element_type=jnp.float32)
    attended_gradient = jnp.dot(d_branch, output_full.T, preferred_element_type=jnp.float32).astype(
        jnp.bfloat16
    )
    grouped_output_gradient = attended_gradient.reshape(
        present_rows, KEY_VALUE_HEADS, group_size, HEAD_SIZE
    )
    delta = jnp.einsum("tkgd,tkgd->kgt", grouped_output_gradient.astype(jnp.float32), attn_rows)

    def grad_step(carry, items):
        key_block, value_block, key_pos = items
        probs = probs_of(key_block, key_pos)
        d_probs = jnp.einsum(
            "tkgd,skd->kgts",
            grouped_output_gradient,
            value_block,
            preferred_element_type=jnp.float32,
        )
        d_score = (probs * (d_probs - delta[..., None]) * scale).astype(jnp.bfloat16)
        carry = carry + jnp.einsum(
            "kgts,skd->tkgd", d_score, key_block, preferred_element_type=jnp.float32
        )
        d_key_block = jnp.einsum(
            "kgts,tkgd->skd", d_score, grouped_queries, preferred_element_type=jnp.float32
        )
        d_value_block = jnp.einsum(
            "kgts,tkgd->skd",
            probs.astype(jnp.bfloat16),
            grouped_output_gradient,
            preferred_element_type=jnp.float32,
        )
        return (carry, (d_key_block, d_value_block))

    d_query_rot, (d_key_parts, d_value_parts) = lax.scan(
        grad_step,
        jnp.zeros((present_rows, KEY_VALUE_HEADS, group_size, HEAD_SIZE), jnp.float32),
        (key_block_list, value_block_list, position_blocks),
    )
    key_width = rotated_keys.shape[1]
    d_key_all = d_key_parts.reshape(stream_len, key_width)
    d_value_all = d_value_parts.reshape(stream_len, key_width)
    rotated_key_gradient, d_value = (
        lax.psum_scatter(d_key_all, "ctx", scatter_dimension=0, tiled=True),
        lax.psum_scatter(d_value_all, "ctx", scatter_dimension=0, tiled=True),
    )
    d_query = rotate_half(
        d_query_rot.reshape(present_rows, query_width), cosine_table, sine_table, QUERY_HEADS, False
    ).astype(jnp.bfloat16)
    key_gradient = rotate_half(
        rotated_key_gradient, cosine_table, sine_table, KEY_VALUE_HEADS, False
    ).astype(jnp.bfloat16)
    d_value_low = d_value.astype(jnp.bfloat16)
    query_local = jnp.dot(normalized_input.T, d_query, preferred_element_type=jnp.float32)
    key_local = jnp.dot(normalized_input.T, key_gradient, preferred_element_type=jnp.float32)
    value_local = jnp.dot(normalized_input.T, d_value_low, preferred_element_type=jnp.float32)
    d_normed = (
        jnp.dot(d_query, query_full.T, preferred_element_type=jnp.float32)
        + jnp.dot(key_gradient, key_full.T, preferred_element_type=jnp.float32)
        + jnp.dot(d_value_low, value_full.T, preferred_element_type=jnp.float32)
    )
    gain_one_local = jnp.sum(d_normed * normed_one, axis=0)
    scaled_one = d_normed * gain_one
    tokens_grad = d_hidden + scale_one * (
        scaled_one - normed_one * jnp.mean(scaled_one * normed_one, axis=-1, keepdims=True)
    )
    column_sums = (
        lax.psum_scatter(query_local, "ctx", scatter_dimension=1, tiled=True),
        lax.psum_scatter(key_local, "ctx", scatter_dimension=1, tiled=True),
        lax.psum_scatter(value_local, "ctx", scatter_dimension=1, tiled=True),
        lax.psum_scatter(output_local, "ctx", scatter_dimension=1, tiled=True),
        lax.psum_scatter(gate_local, "ctx", scatter_dimension=1, tiled=True),
        lax.psum_scatter(up_local, "ctx", scatter_dimension=1, tiled=True),
        lax.psum_scatter(down_local, "ctx", scatter_dimension=1, tiled=True),
    )
    gain_totals = lax.psum((gain_one_local, gain_two_local), "ctx")
    finals = (
        lax.psum_scatter(
            gain_totals[0].astype(jnp.bfloat16), "fsdp", scatter_dimension=0, tiled=True
        ).astype(jnp.float32),
        lax.psum_scatter(
            column_sums[0].astype(jnp.bfloat16), "fsdp", scatter_dimension=0, tiled=True
        ).astype(jnp.float32),
        lax.psum_scatter(
            column_sums[1].astype(jnp.bfloat16), "fsdp", scatter_dimension=0, tiled=True
        ).astype(jnp.float32),
        lax.psum_scatter(
            column_sums[2].astype(jnp.bfloat16), "fsdp", scatter_dimension=0, tiled=True
        ).astype(jnp.float32),
        lax.psum_scatter(
            column_sums[3].astype(jnp.bfloat16), "fsdp", scatter_dimension=0, tiled=True
        ).astype(jnp.float32),
        lax.psum_scatter(
            gain_totals[1].astype(jnp.bfloat16), "fsdp", scatter_dimension=0, tiled=True
        ).astype(jnp.float32),
        lax.psum_scatter(
            column_sums[4].astype(jnp.bfloat16), "fsdp", scatter_dimension=0, tiled=True
        ).astype(jnp.float32),
        lax.psum_scatter(
            column_sums[5].astype(jnp.bfloat16), "fsdp", scatter_dimension=0, tiled=True
        ).astype(jnp.float32),
        lax.psum_scatter(
            column_sums[6].astype(jnp.bfloat16), "fsdp", scatter_dimension=0, tiled=True
        ).astype(jnp.float32),
    )
    gain_one_grad = finals[0]
    gain_two_grad = finals[5]
    matrices = (finals[1], finals[2], finals[3], finals[4], finals[6], finals[7], finals[8])
    return (
        layer_out[None],
        tokens_grad.astype(jnp.bfloat16)[None],
        gain_one_grad,
        matrices[0],
        matrices[1],
        matrices[2],
        matrices[3],
        gain_two_grad,
        matrices[4],
        matrices[5],
        matrices[6],
    )


def solution(mesh):
    return jax.shard_map(
        local,
        mesh=mesh,
        in_specs=(
            P("fsdp", "ctx", None),
            P("fsdp", None),
            P("fsdp"),
            P("fsdp", None),
            P("fsdp", None),
            P("fsdp", None),
            P("fsdp", None),
            P("fsdp"),
            P("fsdp", None),
            P("fsdp", None),
            P("fsdp", None),
            P("fsdp", "ctx", None),
        ),
        out_specs=(
            P("fsdp", "ctx", None),
            P("fsdp", "ctx", None),
            P("fsdp"),
            P("fsdp", "ctx"),
            P("fsdp", "ctx"),
            P("fsdp", "ctx"),
            P("fsdp", "ctx"),
            P("fsdp"),
            P("fsdp", "ctx"),
            P("fsdp", "ctx"),
            P("fsdp", "ctx"),
        ),
        check_vma=False,
    )
```

```python
import math

import jax
import jax.numpy as jnp
import numpy as np
from jax import lax
from jax.experimental import pallas as pl
from jax.experimental.pallas import tpu as pltpu
from jax.sharding import PartitionSpec as P

QUERY_HEADS = 18
KEY_VALUE_HEADS = 6
HEAD_SIZE = 64
GROUP = QUERY_HEADS // KEY_VALUE_HEADS
HALF = HEAD_SIZE // 2
LANES = 128

EPS = 1e-05
BASE = 10000.0
NEGATIVE_FILL = -1e30
BF = jnp.bfloat16
F32 = jnp.float32
MIB = 1024 * 1024


def dot(left, right, left_dim, right_dim):
    return lax.dot_general(
        left, right, (((left_dim,), (right_dim,)), ((), ())), preferred_element_type=F32
    )


def rms_scale(values):
    return lax.rsqrt(jnp.mean(values * values, axis=-1, keepdims=True) + EPS)


def stored_position(row_ids, rows_per_dev, devices_ctx):
    half_len = rows_per_dev // 2
    owner_dev = row_ids // rows_per_dev
    offset_in = row_ids % rows_per_dev
    early = owner_dev * half_len + offset_in
    later = (2 * devices_ctx - 1 - owner_dev) * half_len + offset_in - half_len
    return jnp.where(offset_in < half_len, early, later)


def relative_ids(n):
    return [2 * j + k for k in range(2) for j in range(n // 2)]


def moved_block(n, i, b):
    rel = relative_ids(n)
    return rel.index(rel[b] ^ rel[i])


def hop(value, axis, bits):
    n = lax.axis_size(axis)
    return lax.ppermute(value, axis, [(i, i ^ bits) for i in range(n)])


def after(value, *others):
    return lax.optimization_barrier((value, *others))[0]


def gather_blocks(value, n):
    same = [value] + [hop(value, "ctx", 2 * j) for j in range(1, n // 2)]
    return same + [hop(block, "ctx", 1) for block in same]


def aligned(index, size):
    return pl.ds(pl.multiple_of(index * size, 16), size)


def turn(values, cosine, sine, sign):
    pieces = []
    for at in range(0, values.shape[0], HEAD_SIZE):
        first = values[at : at + HALF]
        second = values[at + HALF : at + HEAD_SIZE]
        pieces.append(first * cosine - sign * (second * sine))
        pieces.append(second * cosine + sign * (first * sine))
    return jnp.concatenate(pieces, axis=0)


def head_rows(h, g):
    return slice(HEAD_SIZE * (GROUP * h + g), HEAD_SIZE * (GROUP * h + g + 1))


def group_columns(ref, h):
    return jnp.concatenate([ref[head_rows(h, g), :] for g in range(GROUP)], axis=1)


def mask_bias(me, starts_ref, n, tokens):
    shape = (tokens, tokens)
    half_len = tokens // 2

    def position(device, offset):
        early = device * half_len + offset
        return jnp.where(offset < half_len, early, (2 * n - 2 - device) * half_len + offset)

    q_pos = position(me, lax.broadcasted_iota(jnp.int32, shape, 1))
    begin = jnp.zeros(shape, jnp.int32)
    for d in range(starts_ref.shape[1]):
        start = starts_ref[0, d]
        begin = jnp.where(q_pos >= start, jnp.maximum(begin, start), begin)
    blocks = []
    for bits in relative_ids(n):
        k_pos = position(me ^ bits, lax.broadcasted_iota(jnp.int32, shape, 0))
        visible = (k_pos >= begin) & (k_pos <= q_pos)
        blocks.append(jnp.where(visible, 0.0, NEGATIVE_FILL).astype(F32))
    return jnp.concatenate(blocks, axis=0)


SMEM = pl.BlockSpec(memory_space=pltpu.SMEM)


def kernel_call(body, name, outs, args, scratch=(), scalars=0, limit=60):
    shapes = [jax.ShapeDtypeStruct(shape, dtype) for shape, dtype in outs]

    def whole(value):
        return pl.BlockSpec(value.shape, lambda g: (0,) * len(value.shape))

    return pl.pallas_call(
        body,
        grid=(1,),
        in_specs=[SMEM] * scalars + [whole(a) for a in args[scalars:]],
        out_specs=[whole(s) for s in shapes],
        out_shape=shapes,
        scratch_shapes=[pltpu.VMEM(shape, dtype) for shape, dtype in scratch],
        compiler_params=pltpu.CompilerParams(vmem_limit_bytes=limit * MIB),
        cost_estimate=pl.CostEstimate(flops=1, bytes_accessed=1, transcendentals=0),
        name=name,
    )(*args)


def project_kernel(level_ref, *refs, n, depth, cols):
    qc, kc = cols
    half = n // 2
    x_refs, w_refs = refs[:n], refs[n : n + depth]
    normed_ref, weight_t_ref, out_t_ref, gains_ref = refs[n + depth : n + depth + 4]
    message_refs = refs[n + depth + 4 : n + depth + 4 + half]
    weight_ref, raw_ref, row_ref = refs[n + depth + 4 + half :]
    rows = row_ref.shape[2]
    tokens = x_refs[0].shape[0]
    width = qc + 2 * kc
    for k in range(depth):
        weight_ref[aligned(level_ref[0] ^ k, rows), :] = w_refs[k][:rows, :]
        row_ref[level_ref[0] ^ k] = w_refs[k][rows:, :rows].astype(F32)
    turned = weight_ref[...].astype(F32).T.astype(BF)
    weight_t_ref[...] = turned[:width]
    out_t_ref[...] = turned[width:]
    gains = jnp.concatenate([row_ref[t] for t in range(depth)], axis=1)
    gains_ref[...] = gains[:8]
    for i in range(n):
        values = x_refs[i][...].astype(F32)
        normed = (values * rms_scale(values) * gains[:1]).astype(BF)
        normed_ref[tokens * i : tokens * (i + 1), :] = normed
        raw_ref[i] = dot(weight_t_ref[...], normed, 1, 1).astype(BF)
    for j in range(half):
        for b in range(n):
            message_refs[j][2 * kc * b : 2 * kc * (b + 1), :] = raw_ref[b, qc:, :]
        at = 2 * kc * n
        message_refs[j][at : at + qc, :] = raw_ref[j, :qc, :]
        message_refs[j][at + qc : at + 2 * qc, :] = raw_ref[half + j, :qc, :]


def project(level, x_blocks, w_pieces, n, depth, qc, kc):
    tokens, width = x_blocks[0].shape
    rows = width // depth
    cols = qc + 2 * kc
    spare = w_pieces[0].shape[0] - rows
    length = n * tokens
    all_cols = w_pieces[0].shape[1]

    def body(*refs):
        project_kernel(*refs, n=n, depth=depth, cols=(qc, kc))

    return kernel_call(
        body,
        "project",
        [((length, width), BF), ((cols, width), BF), ((all_cols - cols, width), BF), ((8, width), F32)]
        + [((2 * kc * n + 2 * qc, tokens), BF)] * (n // 2),
        [level, *x_blocks, *w_pieces],
        scratch=[((width, all_cols), BF), ((n, cols, tokens), BF), ((depth, spare, rows), F32)],
        scalars=1,
    )


def attention_forward_kernel(me_ref, starts_ref, *refs, n):
    half = n // 2
    same, other = refs[:half], refs[half:n]
    cos_ref, sin_ref = refs[n : n + 2]
    low_ref, att_ref, lse_ref, qrot_ref, krot_ref, v_ref = refs[n + 2 : n + 8]
    q_ref, k_ref, bias_ref = refs[n + 8 :]
    tokens = q_ref.shape[1]
    qc, kc = q_ref.shape[0] // n, k_ref.shape[0] // n
    rel = relative_ids(n)
    for i in range(n):
        device = me_ref[0] ^ rel[i]
        source = same[i] if i < half else other[i - half]
        at = 2 * kc * n + (0 if i < half else qc)
        q_ref[aligned(device, qc), :] = source[at : at + qc, :]
        to = aligned(device, kc)
        for b in range(n):
            start = 2 * kc * moved_block(n, i, b)
            lanes = slice(tokens * b, tokens * (b + 1))
            k_ref[to, lanes] = source[start : start + kc, :]
            v_ref[to, lanes] = source[start + kc : start + 2 * kc, :]
    bias_ref[...] = mask_bias(me_ref[0], starts_ref, n, tokens)
    for h in range(KEY_VALUE_HEADS):
        rows = slice(HEAD_SIZE * h, HEAD_SIZE * (h + 1))
        krot_ref[rows, :] = turn(k_ref[rows, :].astype(F32), cos_ref[...], sin_ref[...], 1.0).astype(BF)
        for g in range(GROUP):
            at = head_rows(h, g)
            turned = turn(
                q_ref[at, :].astype(F32), cos_ref[:, :tokens], sin_ref[:, :tokens], 1.0
            ).astype(BF)
            qrot_ref[at, :] = turned * BF(HEAD_SIZE**-0.5)
    for h in range(KEY_VALUE_HEADS):
        rows = slice(HEAD_SIZE * h, HEAD_SIZE * (h + 1))
        bias = jnp.concatenate([bias_ref[...]] * GROUP, axis=1)
        scores = dot(krot_ref[rows, :], group_columns(qrot_ref, h), 0, 0) + bias
        top = jnp.max(scores, axis=0, keepdims=True)
        weights = jnp.exp(scores - top)
        total = jnp.sum(weights, axis=0, keepdims=True)
        lse_ref[h : h + 1, :] = top + jnp.log(total)
        mixed = dot(v_ref[rows, :], weights.astype(BF), 1, 0) / total
        for g in range(GROUP):
            att_ref[head_rows(h, g), :] = mixed[:, tokens * g : tokens * (g + 1)]
    low_ref[...] = att_ref[...].T.astype(BF)


def attention_forward(me, starts, same, other, cosine, sine, n, query_width, key_width):
    tokens = same[0].shape[1]
    length = n * tokens

    def body(*refs):
        attention_forward_kernel(*refs, n=n)

    return kernel_call(
        body,
        "attention_forward",
        [
            ((tokens, query_width), BF),
            ((query_width, tokens), F32),
            ((KEY_VALUE_HEADS, GROUP * tokens), F32),
            ((query_width, tokens), BF),
            ((key_width, length), BF),
            ((key_width, length), BF),
        ],
        [me, starts, *same, *other, cosine, sine],
        scratch=[((query_width, tokens), BF), ((key_width, length), BF), ((length, tokens), F32)],
        scalars=2,
    )


def feed_forward_kernel(me_ref, *refs, n, depth):
    half = n // 2
    out_pieces, downs, (w_ref, gains_ref) = refs[:n], refs[n : n + depth], refs[n + depth : n + depth + 2]
    at = n + depth + 2
    x_refs, a_refs, g_refs = (refs[at + n * i : at + n * (i + 1)] for i in range(3))
    at += 3 * n
    d_same = refs[at : at + half]
    (
        d_other_ref, y_same_ref, y_other_ref, ffn_ref, act_ref, dgu_ref, part_ref, own_ref, wo_ref, wd_ref,
    ) = refs[at + half :]
    tokens, width = x_refs[0].shape
    fc = act_ref.shape[1]
    rel = relative_ids(n)
    for i in range(n):
        wo_ref[aligned(me_ref[0] ^ rel[i], out_pieces[i].shape[0]), :] = out_pieces[i][...]
    share, down_rows = n // depth, wd_ref.shape[0] // depth
    part = jnp.zeros((1, width), F32)
    for j in range(half):
        rows = slice(2 * tokens * j, 2 * tokens * (j + 1))
        values, attended = (
            jnp.concatenate([some[j][...], some[half + j][...]], axis=0) for some in (x_refs, a_refs)
        )
        hidden = values.astype(F32) + dot(attended, wo_ref[...], 1, 1)
        if j == 0:
            own_ref[...] = hidden[:tokens]
        normed = hidden * rms_scale(hidden)
        ffn_in = (normed * gains_ref[1:2, :]).astype(BF)
        ffn_ref[rows, :] = ffn_in
        gate = dot(ffn_in, w_ref[:, :fc], 1, 0)
        upper = dot(ffn_in, w_ref[:, fc : 2 * fc], 1, 0)
        if j == 0:
            for t in range(depth):
                to = aligned((me_ref[0] // share) ^ t, down_rows)
                for i in range(width // fc):
                    wd_ref[to, fc * i : fc * (i + 1)] = downs[t][down_rows * i : down_rows * (i + 1), :]
        cot = jnp.concatenate([g_refs[j][...], g_refs[half + j][...]], axis=0)
        d_act = dot(cot, wd_ref[...], 1, 1)
        sigma = jax.nn.sigmoid(gate)
        silu = gate * sigma
        act = (silu * upper).astype(BF)
        act_ref[rows, :] = act
        d_gate = (d_act * upper * sigma * (1.0 + gate * (1.0 - sigma))).astype(BF)
        d_up = (d_act * silu).astype(BF)
        dgu_ref[rows, :fc] = d_gate
        dgu_ref[rows, fc:] = d_up
        d_in = dot(d_gate, w_ref[:, :fc], 1, 1) + dot(d_up, w_ref[:, fc : 2 * fc], 1, 1)
        part = part + jnp.sum(d_in * normed, axis=0, keepdims=True)
        d_same[j][...] = d_in[:tokens].astype(BF)
        d_other_ref[j] = d_in[tokens:].astype(BF)
        out = dot(act, wd_ref[...], 1, 0)
        y_same_ref[j] = out[:tokens].astype(BF)
        y_other_ref[j] = out[tokens:].astype(BF)
    part_ref[...] = jnp.broadcast_to(part, part_ref.shape)


def feed_forward(me, out_pieces, downs, ffn_weights, gains, x_blocks, a_blocks, g_blocks, n, depth):
    tokens, width = x_blocks[0].shape
    fc = downs[0].shape[1]
    half, rows = n // 2, n * tokens
    by_chip = [some[side + j] for some in (x_blocks, a_blocks, g_blocks) for side in (0, half) for j in range(half)]

    def body(*refs):
        feed_forward_kernel(*refs, n=n, depth=depth)

    outs = kernel_call(
        body,
        "feed_forward",
        [((tokens, width), BF)] * half
        + [((half, tokens, width), BF)] * 3
        + [((rows, width), BF), ((rows, fc), BF), ((rows, 2 * fc), BF), ((8, width), F32)]
        + [((tokens, width), F32)],
        [me, *out_pieces, *downs, ffn_weights, gains, *by_chip],
        scratch=[((width, out_pieces[0].shape[1]), BF), ((fc, width), BF)],
        scalars=1,
    )
    return outs[:half], *outs[half:]


def ffn_grads_kernel(me_ref, *refs, n):
    half = n // 2
    ffn_ref, act_ref, dgu_ref = refs[:3]
    g_refs = refs[3 : 3 + n]
    gu_ref, same_ref = refs[3 + n : 5 + n]
    other_refs, down_ref = refs[5 + n : 5 + n + half], refs[5 + n + half]
    gu_ref[...] = dot(ffn_ref[...], dgu_ref[...], 0, 0).astype(BF)
    g_all = jnp.concatenate([g_refs[side + j][...] for j in range(half) for side in (0, half)], axis=0)
    down_ref[...] = dot(g_all, act_ref[...], 0, 0).astype(BF)
    dc = down_ref.shape[0] // n
    rel = relative_ids(n)
    for i in range(n):
        piece = down_ref[aligned(me_ref[0] ^ rel[i], dc), :]
        if i < half:
            same_ref[i] = piece
        else:
            other_refs[i - half][...] = piece


def ffn_grads(me, ffn, act, dgu, g_blocks, n):
    half = n // 2
    width, fc = ffn.shape[1], act.shape[1]
    dc = width // n

    def body(*refs):
        ffn_grads_kernel(*refs, n=n)

    return kernel_call(
        body,
        "ffn_grads",
        [((width, 2 * fc), BF), ((half, dc, fc), BF)] + [((dc, fc), BF)] * half,
        [me, ffn, act, dgu, *g_blocks],
        scratch=[((width, fc), BF)],
        scalars=1,
    )


def pack_out_kernel(*refs, half):
    y_same_ref, y_far_ref, d_same_ref = refs[:3]
    d_far_refs, own_ref, out_refs = refs[3 : 3 + half], refs[3 + half], refs[4 + half :]
    tokens, width = own_ref.shape
    dc, fc = d_same_ref.shape[1:]
    rows = 2 * dc * fc // width
    for j in range(half):
        both = y_same_ref[j].astype(F32) + y_far_ref[j].astype(F32)
        if j == 0:
            own_ref[...] = both
        out_refs[j][:tokens, :] = both.astype(BF)
        pair_rows = jnp.concatenate([d_same_ref[j], d_far_refs[j][...]], axis=0)
        for i in range(width // fc):
            out_refs[j][tokens:, fc * i : fc * (i + 1)] = pair_rows[rows * i : rows * (i + 1)]


def pack_out(y_same, y_far, d_same, d_far):
    half, tokens, width = y_same.shape
    dc, fc = d_same.shape[1:]

    def body(*refs):
        pack_out_kernel(*refs, half=half)

    return kernel_call(
        body,
        "pack_out",
        [((tokens, width), F32)] + [((tokens + 2 * dc * fc // width, width), BF)] * half,
        [y_same, y_far, d_same, *d_far],
    )


def unpack_out_kernel(me_ref, level_ref, *refs, n, depth):
    half = n // 2
    packed, (own_ref, hidden_ref, out_ref) = refs[:half], refs[half : half + 3]
    grad_refs, grad_ref = refs[half + 3 : half + 3 + depth], refs[half + 3 + depth]
    tokens, width = own_ref.shape
    dc = grad_ref.shape[1]
    share = n // depth
    fc = grad_ref.shape[2] // share
    for j in range(half):
        pair_rows = jnp.concatenate(
            [packed[j][tokens:, fc * i : fc * (i + 1)] for i in range(width // fc)], axis=0
        )
        for side in range(2):
            device = me_ref[0] ^ (2 * j + side)
            lanes = pl.ds(pl.multiple_of((device % share) * fc, LANES), fc)
            grad_ref[device // share, :, lanes] = pair_rows[dc * side : dc * (side + 1)]
    for k in range(depth):
        grad_refs[k][...] = grad_ref[level_ref[0] ^ k]
    total = hidden_ref[...] + own_ref[...]
    for r in packed[1:]:
        total = total + r[:tokens, :].astype(F32)
    out_ref[...] = total.astype(BF)


def unpack_out(me, level, own, hidden, packed, n, depth, dc, fc):
    def body(*refs):
        unpack_out_kernel(*refs, n=n, depth=depth)

    piece = (dc, fc * n // depth)
    return kernel_call(
        body,
        "unpack_out",
        [(own.shape, BF)] + [(piece, BF)] * depth,
        [me, level, *packed, own, hidden],
        scratch=[((depth, *piece), BF)],
        scalars=2,
    )


def attention_backward_kernel(me_ref, starts_ref, *refs, n):
    half = n // 2
    sums = refs[: half + 1]
    (g_ref, hidden_ref, gains_ref, q_ref, k_ref, v_ref, att_ref, lse_ref, cos_ref, sin_ref) = refs[
        half + 1 : half + 11
    ]
    out_pieces = refs[half + 11 : half + 11 + n]
    dh_ref, same_ref = refs[half + 11 + n : half + 13 + n]
    other_refs = refs[half + 13 + n : n + n + 13]
    do_ref, db_ref, dq_ref, dk_ref, dv_ref, bias_ref, message_ref, wo_ref = refs[2 * n + 13 :]
    rel = relative_ids(n)
    bias_ref[...] = mask_bias(me_ref[0], starts_ref, n, q_ref.shape[1])
    tokens = q_ref.shape[1]
    d_in = sums[0][...].astype(F32) + sums[1][0].astype(F32)
    for r in sums[2:]:
        d_in = d_in + r[...].astype(F32)
    hidden = hidden_ref[...]
    scale = rms_scale(hidden)
    normed = hidden * scale
    scaled = d_in * gains_ref[1:2, :]
    d_hidden = g_ref[...].astype(F32) + scale * (
        scaled - normed * jnp.mean(scaled * normed, axis=-1, keepdims=True)
    )
    dh_ref[...] = d_hidden
    db_ref[...] = d_hidden.T.astype(BF)
    for i in range(n):
        wo_ref[aligned(me_ref[0] ^ rel[i], out_pieces[i].shape[0]), :] = out_pieces[i][...]
    do_ref[...] = dot(wo_ref[...], db_ref[...], 0, 0).astype(BF)
    for h in range(KEY_VALUE_HEADS):
        rows = slice(HEAD_SIZE * h, HEAD_SIZE * (h + 1))
        queries = group_columns(q_ref, h)
        grads = group_columns(do_ref, h)
        delta = jnp.sum(grads.astype(F32) * group_columns(att_ref, h), axis=0, keepdims=True)
        bias = jnp.concatenate([bias_ref[...]] * GROUP, axis=1)
        scores = dot(k_ref[rows, :], queries, 0, 0) + bias
        probs = jnp.exp(scores - lse_ref[h : h + 1, :])
        d_probs = dot(v_ref[rows, :], grads, 0, 0)
        d_score = (probs * (d_probs - delta)).astype(BF)
        d_query = dot(k_ref[rows, :], d_score, 1, 0) * (HEAD_SIZE**-0.5)
        for g in range(GROUP):
            dq_ref[head_rows(h, g), :] = turn(
                d_query[:, tokens * g : tokens * (g + 1)], cos_ref[:, :tokens], sin_ref[:, :tokens], -1.0
            ).astype(BF)
        d_key = dot(queries, d_score, 1, 1)
        dk_ref[rows, :] = turn(d_key, cos_ref[...], sin_ref[...], -1.0).astype(BF)
        dv_ref[rows, :] = dot(grads, probs.astype(BF), 1, 1).astype(BF)
    qc, dc, kc = dq_ref.shape[0] // n, db_ref.shape[0] // n, dk_ref.shape[0] // n
    flat = 2 * kc * n
    for i in (*range(half, n), *range(half)):
        if i == 0:
            for j in range(half):
                other_refs[j][...] = message_ref[j]
        device = me_ref[0] ^ rel[i]
        to = same_ref if i < half else message_ref
        j = i % half
        to[j, flat : flat + qc, :] = dq_ref[aligned(device, qc), :]
        to[j, flat + qc : flat + qc + dc, :] = db_ref[aligned(device, dc), :]
        at = aligned(device, kc)
        for b in range(n):
            start = 2 * kc * moved_block(n, i, b)
            lanes = slice(tokens * b, tokens * (b + 1))
            to[j, start : start + kc, :] = dk_ref[at, lanes]
            to[j, start + kc : start + 2 * kc, :] = dv_ref[at, lanes]


def attention_backward(me, starts, sums, g, hidden, gains, out_pieces, saved, cosine, sine, n):
    q_rot, k_rot, v_low, att, lse = saved
    query_width, tokens = q_rot.shape
    width = hidden.shape[1]
    key_width, length = k_rot.shape
    rows = 2 * key_width + (query_width + width) // n

    def body(*refs):
        attention_backward_kernel(*refs, n=n)

    return kernel_call(
        body,
        "attention_backward",
        [((tokens, width), F32), ((n // 2, rows, tokens), BF)] + [((rows, tokens), BF)] * (n // 2),
        [me, starts, *sums, g, hidden, gains, q_rot, k_rot, v_low, att, lse, cosine, sine, *out_pieces],
        scratch=[
            ((query_width, tokens), BF), ((width, tokens), BF), ((query_width, tokens), BF),
            ((key_width, length), BF), ((key_width, length), BF), ((length, tokens), F32),
            ((n // 2, rows, tokens), BF), ((width, query_width), BF),
        ],
        scalars=2,
    )


def pair_kernel(same_ref, *refs, flat):
    half, rows = same_ref.shape[:2]
    others, outs = refs[:half], refs[half:]
    more = rows - flat
    for j in reversed(range(half)):
        other = others[j][...]
        both = same_ref[j, :flat, :].astype(F32) + other[:flat].astype(F32)
        outs[j][:flat, :] = both.astype(BF)
        outs[j][flat : flat + more, :] = same_ref[j, flat:, :]
        outs[j][flat + more :, :] = other[flat:]


def pair(same, others, flat):
    half, rows, tokens = same.shape

    def body(*refs):
        pair_kernel(*refs, flat=flat)

    return kernel_call(
        body, "pair", [((2 * rows - flat, tokens), BF)] * half, [same, *others]
    )


def input_grads_kernel(level_ref, *refs, n, depth, cols):
    qc, kc, dc = cols
    half = n // 2
    got, a_refs, x_refs = refs[:half], refs[half : half + n], refs[half + n : half + 2 * n]
    normed_ref, weight_t_ref = refs[half + 2 * n : half + 2 * n + 2]
    at = half + 2 * n + 2
    part_two_ref, other_ref = refs[at : at + 2]
    same_refs = refs[at + 2 : at + 2 + half]
    level_refs = refs[at + 2 + half : at + 2 + half + depth]
    d_ref, b_ref, last_ref, row_ref = refs[at + 2 + half + depth :]
    tokens = x_refs[0].shape[0]
    flat = 2 * kc * n
    total = got[0][:flat, :].astype(F32)
    for r in got[1:]:
        total = total + r[:flat, :].astype(F32)
    total = total.astype(BF)
    for i in range(n):
        lanes = slice(tokens * i, tokens * (i + 1))
        start = flat + (qc + dc) * (i // half)
        source = got[i % half]
        d_ref[:qc, lanes] = source[start : start + qc, :]
        d_ref[qc:, lanes] = total[2 * kc * i : 2 * kc * (i + 1)]
        b_ref[:, lanes] = source[start + qc : start + qc + dc, :]
    width = x_refs[0].shape[1]
    part = jnp.zeros((1, width), F32)
    for i in (*range(half, n), *range(half)):
        lanes = slice(tokens * i, tokens * (i + 1))
        d_normed = dot(d_ref[:, lanes], weight_t_ref[...], 0, 0)
        values = x_refs[i][...].astype(F32)
        part = part + jnp.sum(d_normed * (values * rms_scale(values)), axis=0, keepdims=True)
        if i < half:
            same_refs[i][...] = d_normed.astype(BF)
        else:
            other_ref[i - half] = d_normed.astype(BF)
    cut = qc + 2 * kc
    last_ref[:, :cut] = dot(normed_ref[...], d_ref[...], 0, 1).astype(BF)
    attended = jnp.concatenate([r[...] for r in a_refs], axis=0)
    last_ref[:, cut:] = dot(attended, b_ref[...], 0, 1).astype(BF)
    rows, wide = width // depth, row_ref.shape[2]
    both = jnp.concatenate([part, part_two_ref[:1, :], jnp.zeros((14, width), F32)], axis=0)
    for t in range(depth):
        row_ref[t, :, :rows] = both[:, rows * t : rows * (t + 1)]
        row_ref[t, :, rows:] = jnp.zeros((16, wide - rows), F32)
    for k in range(depth):
        level_refs[k][:rows, :] = last_ref[aligned(level_ref[0] ^ k, rows), :]
        level_refs[k][rows:, :] = row_ref[level_ref[0] ^ k].astype(BF)


def input_grads(level, got, attended, x_blocks, normed_in, weight_t, part_two, n, depth, qc, kc, dc):
    half = n // 2
    tokens, width = x_blocks[0].shape
    length = n * tokens
    cols = qc + 2 * kc + dc

    def body(*refs):
        input_grads_kernel(*refs, n=n, depth=depth, cols=(qc, kc, dc))

    return kernel_call(
        body,
        "input_grads",
        [((half, tokens, width), BF)]
        + [((tokens, width), BF)] * half
        + [((width // depth + 16, cols), BF)] * depth,
        [level, *got, *attended, *x_blocks, normed_in, weight_t, part_two],
        scratch=[
            ((qc + 2 * kc, length), BF), ((dc, length), BF), ((width, cols), BF), ((depth, 16, cols), F32),
        ],
        scalars=1,
    )


def finish_kernel(*refs, half, depth, cuts):
    sums, pieces = refs[: half + 1], refs[half + 1 : half + 1 + depth]
    downs = refs[half + 1 + depth : half + 1 + 2 * depth]
    at = half + 1 + 2 * depth
    dh_ref, x_ref, gains_ref, out_ref, rows_ref, down_ref = refs[at : at + 6]
    total = pieces[0][...].astype(F32)
    for r in pieces[1:]:
        total = total + r[...].astype(F32)
    rows = total.shape[0] - 16
    rows_ref[...] = total[rows : rows + 8]
    turned = total[:rows].T
    for grad_ref, start, stop in zip(refs[at + 6 :], cuts[:-1], cuts[1:]):
        grad_ref[...] = turned[start:stop]
    total = downs[0][...].astype(F32)
    for r in downs[1:]:
        total = total + r[...].astype(F32)
    down_ref[...] = total
    d_normed = sums[0][...].astype(F32) + sums[1][0].astype(F32)
    for r in sums[2:]:
        d_normed = d_normed + r[...].astype(F32)
    values = x_ref[...].astype(F32)
    scale = rms_scale(values)
    normed = values * scale
    scaled = d_normed * gains_ref[0:1, :]
    out_ref[...] = (
        dh_ref[...]
        + scale * (scaled - normed * jnp.mean(scaled * normed, axis=-1, keepdims=True))
    ).astype(BF)


def finish(sums, pieces, downs, d_hidden, x, gains, cuts):
    height, wide = pieces[0].shape

    def body(*refs):
        finish_kernel(*refs, half=len(sums) - 1, depth=len(pieces), cuts=cuts)

    return kernel_call(
        body,
        "finish",
        [(x.shape, BF), ((8, wide), F32), (downs[0].shape, F32)]
        + [((stop - start, height - 16), F32) for start, stop in zip(cuts[:-1], cuts[1:])],
        [*sums, *pieces, *downs, d_hidden, x, gains],
    )


def pair_sums(same, far):
    return [
        (same[j].astype(F32) + far[j].astype(F32)).astype(BF) for j in range(1, len(same))
    ]


def column_slice(weight, index, width):
    return lax.dynamic_slice_in_dim(weight, index * width, width, axis=1)


def local(
    tokens_in,
    doc_starts,
    attn_gain,
    query_weight,
    key_weight,
    value_weight,
    output_weight,
    ffn_gain,
    gate_weight,
    up_weight,
    down_weight,
    out_cotangent,
):
    n = lax.axis_size("ctx")
    depth = lax.axis_size("fsdp")
    tokens, width = tokens_in.shape[1:]
    query_width, key_width = query_weight.shape[1], key_weight.shape[1]
    qc, kc, dc = query_width // n, key_width // n, width // n
    rows = query_weight.shape[0]
    hidden_units = gate_weight.shape[1]
    fc = hidden_units // n
    down_rows = down_weight.shape[0] // n
    per_row = width // fc
    operands = (
        tokens_in, doc_starts, attn_gain, query_weight, key_weight, value_weight, output_weight,
        ffn_gain, gate_weight, up_weight, down_weight, out_cotangent,
    )
    if n > 8 or tokens != LANES or any(size % 16 for size in (qc, kc, dc, rows, down_rows)):
        return local_gathered(*operands)
    half = n // 2
    me = lax.axis_index("ctx")
    level = lax.axis_index("fsdp")
    me_1, level_1 = me[None], level[None]
    x, g = tokens_in[0], out_cotangent[0]

    x_blocks = gather_blocks(x, n)

    columns = jnp.concatenate(
        [
            column_slice(query_weight, me, qc),
            column_slice(key_weight, me, kc),
            column_slice(value_weight, me, kc),
            column_slice(output_weight, me, dc),
        ],
        axis=1,
    )
    gain_rows = jnp.pad(
        jnp.stack([attn_gain, ffn_gain]), ((0, 14), (0, columns.shape[1] - rows))
    )
    first = jnp.concatenate([columns, gain_rows], axis=0)
    first_pieces = [first] + [hop(first, "fsdp", k) for k in range(1, depth)]
    down_piece = lax.dynamic_slice_in_dim(down_weight, me * down_rows, down_rows, axis=0)
    shard = jnp.concatenate(
        [
            column_slice(gate_weight, me, fc),
            column_slice(up_weight, me, fc),
            jnp.concatenate(
                [down_piece[:, fc * i : fc * (i + 1)] for i in range(per_row)], axis=0
            ),
        ],
        axis=1,
    )
    ffn_weights = lax.all_gather(after(shard, *first_pieces[1:], *x_blocks[1:half]), "fsdp", axis=0, tiled=True)

    devices = jnp.asarray(np.array(relative_ids(n), np.int32)) ^ me
    row_ids = (devices[:, None] * tokens + jnp.arange(tokens, dtype=jnp.int32)[None, :]).reshape(1, -1)
    positions = stored_position(row_ids, tokens, n)
    starts = doc_starts[0][:, None]
    begins = jnp.max(jnp.where(starts <= positions, starts, 0), axis=0, keepdims=True)
    inv_freq = jnp.exp(-math.log(BASE) * 2.0 * jnp.arange(HALF, dtype=F32) / HEAD_SIZE)
    angles = inv_freq[:, None] * (positions - begins).astype(F32)
    cosine, sine = jnp.cos(angles), jnp.sin(angles)

    normed_in, weight_t, out_t_own, gains, *messages = project(
        level_1, x_blocks, first_pieces, n, depth, qc, kc
    )
    same = [messages[0]] + [hop(messages[j], "ctx", 2 * j) for j in range(1, half)]
    other = [hop(message, "ctx", 1) for message in same]
    g_blocks = gather_blocks(after(g, x_blocks[half - 1]), n)
    attended, att, lse, q_rot, k_rot, v_low = attention_forward(
        me_1, after(doc_starts, *g_blocks[:half]), same, other, cosine, sine,
        n, query_width, key_width,
    )

    out_same = [out_t_own] + [
        hop(after(out_t_own, same[1]), "ctx", 2 * j) for j in range(1, half)
    ]
    out_other = [hop(after(piece, attended), "ctx", 1) for piece in out_same]
    share = n // depth
    downs = []
    for t in range(depth):
        chunk = lax.dynamic_slice(
            ffn_weights, (((me % depth) ^ t) * rows, 2 * fc), (rows, fc)
        )
        downs.append(
            lax.ppermute(
                chunk, "ctx", [(i, ((i % depth) ^ t) * share + i // depth) for i in range(n)]
            )
        )

    a_same = [attended] + [hop(attended, "ctx", 2 * j) for j in range(1, half)]
    a_blocks = a_same + [hop(after(block, *downs), "ctx", 1) for block in a_same]
    d_same, d_other, y_same, y_other, ffn_in, act, d_gate_up, gain_part, hidden = feed_forward(
        me_1, out_same + out_other, downs, ffn_weights, gains, x_blocks, a_blocks, g_blocks, n, depth
    )
    d_far = hop(d_other, "ctx", 1)
    d_pairs = pair_sums(d_same, d_far)
    sums = [d_same[0], d_far] + [hop(d_pairs[j - 1], "ctx", 2 * j) for j in range(1, half)]
    gate_up_grad, down_same, *down_other = ffn_grads(
        me_1, after(ffn_in, *d_pairs), act, d_gate_up, g_blocks, n
    )
    gate_up_sum = lax.psum_scatter(gate_up_grad, "fsdp", scatter_dimension=0, tiled=True)
    y_own, *packed = pack_out(
        y_same, hop(y_other, "ctx", 1), down_same, [hop(piece, "ctx", 1) for piece in down_other]
    )

    d_hidden, own_messages, *other_messages = attention_backward(
        me_1, after(doc_starts, y_own), sums, g, hidden, gains, out_same + out_other,
        (q_rot, k_rot, v_low, att, lse), cosine, sine, n,
    )

    packed = [packed[0]] + [
        hop(after(packed[j], *sums[2:]), "ctx", 2 * j) for j in range(1, half)
    ]
    onward = pair(
        after(own_messages, *packed), [hop(m, "ctx", 1) for m in other_messages], 2 * kc * n
    )
    layer_out, *down_pieces = unpack_out(me_1, level_1, y_own, hidden, packed, n, depth, dc, fc)
    down_pieces = [down_pieces[0]] + [hop(down_pieces[k], "fsdp", k) for k in range(1, depth)]
    normed_in = after(normed_in, layer_out, *down_pieces[1:])

    got = [onward[0]] + [hop(onward[j], "ctx", 2 * j) for j in range(1, half)]
    n_other, *rest = input_grads(
        level_1, got, a_blocks, x_blocks, normed_in, weight_t, gain_part, n, depth, qc, kc, dc
    )
    n_same, level_pieces = rest[:half], rest[half:]
    pieces = [level_pieces[0]] + [hop(level_pieces[k], "fsdp", k) for k in range(1, depth)]
    n_far = hop(n_other, "ctx", 1)
    n_pairs = pair_sums(n_same, n_far)
    n_sums = [n_same[0], n_far] + [hop(n_pairs[j - 1], "ctx", 2 * j) for j in range(1, half)]
    gate_grad, up_grad = (
        gate_up_sum[:, fc * i : fc * (i + 1)].astype(F32) for i in range(2)
    )
    cuts = [0, qc, qc + kc, qc + 2 * kc, qc + 2 * kc + dc]
    tokens_grad, gain_rows, down_sum, query_grad, key_grad, value_grad, output_grad = finish(
        n_sums, pieces, down_pieces, d_hidden, x, after(gains, gate_grad, up_grad), cuts
    )
    gain_rows = gain_rows + hop(gain_rows, "ctx", 1)
    gain_rows = gain_rows + sum(hop(gain_rows, "ctx", 2 * j) for j in range(1, half))
    gain_own = gain_rows[:2, :rows]
    return (
        layer_out[None],
        tokens_grad[None],
        gain_own[0],
        query_grad.T,
        key_grad.T,
        value_grad.T,
        output_grad.T,
        gain_own[1],
        gate_grad,
        up_grad,
        down_sum.T,
    )


def rotate_half(values, cosine_table, sine_table, heads, forward):
    count = values.shape[0]
    half = HEAD_SIZE // 2
    shaped = values.reshape(count, heads, HEAD_SIZE)
    first_half = shaped[..., :half]
    second_half = shaped[..., half:]
    cos_rows = cosine_table[:, None, :]
    sin_rows = sine_table[:, None, :]
    if forward:
        lower = first_half * cos_rows - second_half * sin_rows
        upper = second_half * cos_rows + first_half * sin_rows
    else:
        lower = first_half * cos_rows + second_half * sin_rows
        upper = second_half * cos_rows - first_half * sin_rows
    return jnp.concatenate([lower, upper], axis=-1).reshape(count, heads * HEAD_SIZE)


def local_gathered(
    tokens_in,
    doc_starts,
    attn_gain,
    query_weight,
    key_weight,
    value_weight,
    output_weight,
    ffn_gain,
    gate_weight,
    up_weight,
    down_weight,
    out_cotangent,
):
    present_rows = tokens_in.shape[1]
    devices_ctx = lax.axis_size("ctx")
    group_size = QUERY_HEADS // KEY_VALUE_HEADS
    scale = HEAD_SIZE ** (-0.5)
    inputs_f = tokens_in[0].astype(jnp.float32)
    gain_one, query_full, key_full, value_full, output_full = (
        lax.all_gather(attn_gain, "fsdp", axis=0, tiled=True),
        lax.all_gather(query_weight, "fsdp", axis=0, tiled=True),
        lax.all_gather(key_weight, "fsdp", axis=0, tiled=True),
        lax.all_gather(value_weight, "fsdp", axis=0, tiled=True),
        lax.all_gather(output_weight, "fsdp", axis=0, tiled=True),
    )
    gain_one = gain_one.astype(jnp.float32)
    scale_one = rms_scale(inputs_f)
    normed_one = inputs_f * scale_one
    normalized_input = (normed_one * gain_one).astype(jnp.bfloat16)
    query_raw = jnp.dot(normalized_input, query_full, preferred_element_type=jnp.float32)
    key_unrotated = jnp.dot(normalized_input, key_full, preferred_element_type=jnp.float32)
    value_raw = jnp.dot(normalized_input, value_full, preferred_element_type=jnp.float32)
    local_rows = lax.axis_index("ctx") * present_rows + jnp.arange(present_rows, dtype=jnp.int32)
    token_pos = stored_position(local_rows, present_rows, devices_ctx)
    starts_row = doc_starts[0]
    doc_begin = jnp.max(
        jnp.where(starts_row[None, :] <= token_pos[:, None], starts_row[None, :], 0), axis=1
    )
    relative = (token_pos - doc_begin).astype(jnp.float32)
    inv_freq = jnp.exp(
        -math.log(BASE) * 2.0 * jnp.arange(HEAD_SIZE // 2, dtype=jnp.float32) / HEAD_SIZE
    )
    angles = relative[:, None] * inv_freq[None, :]
    cosine_table = jnp.cos(angles)
    sine_table = jnp.sin(angles)
    rotated_queries = rotate_half(query_raw, cosine_table, sine_table, QUERY_HEADS, True).astype(
        jnp.bfloat16
    )
    rotated_keys = rotate_half(
        key_unrotated, cosine_table, sine_table, KEY_VALUE_HEADS, True
    ).astype(jnp.bfloat16)
    reduced_values = value_raw.astype(jnp.bfloat16)
    key_gathered, value_gathered = (
        lax.all_gather(rotated_keys, "ctx", axis=0, tiled=True),
        lax.all_gather(reduced_values, "ctx", axis=0, tiled=True),
    )
    stream_len = key_gathered.shape[0]
    block_index = min(512, stream_len)
    block_count = stream_len // block_index
    key_block_list = key_gathered.reshape(block_count, block_index, KEY_VALUE_HEADS, HEAD_SIZE)
    value_block_list = value_gathered.reshape(block_count, block_index, KEY_VALUE_HEADS, HEAD_SIZE)
    key_positions = stored_position(
        jnp.arange(stream_len, dtype=jnp.int32), present_rows, devices_ctx
    )
    position_blocks = key_positions.reshape(block_count, block_index)
    grouped_queries = rotated_queries.reshape(present_rows, KEY_VALUE_HEADS, group_size, HEAD_SIZE)

    def scores_of(key_block, key_pos):
        raw = jnp.einsum(
            "tkgd,skd->kgts", grouped_queries, key_block, preferred_element_type=jnp.float32
        )
        visible = (key_pos[None, :] >= doc_begin[:, None]) & (
            key_pos[None, :] <= token_pos[:, None]
        )
        return (jnp.where(visible[None, None], raw * scale, NEGATIVE_FILL), visible)

    def stats_step(carry, items):
        running_max, running_sum = carry
        key_block, key_pos = items
        scores, visible = scores_of(key_block, key_pos)
        new_max = jnp.maximum(running_max, jnp.max(scores, axis=-1))
        weights = jnp.where(visible[None, None], jnp.exp(scores - new_max[..., None]), 0.0)
        running_sum = running_sum * jnp.exp(running_max - new_max) + jnp.sum(weights, axis=-1)
        return ((new_max, running_sum), None)

    stat_init = (
        jnp.full((KEY_VALUE_HEADS, group_size, present_rows), NEGATIVE_FILL, jnp.float32),
        jnp.zeros((KEY_VALUE_HEADS, group_size, present_rows), jnp.float32),
    )
    (row_max, row_sum), unused = lax.scan(stats_step, stat_init, (key_block_list, position_blocks))
    log_total = row_max + jnp.log(row_sum)

    def probs_of(key_block, key_pos):
        scores, visible = scores_of(key_block, key_pos)
        return jnp.where(visible[None, None], jnp.exp(scores - log_total[..., None]), 0.0)

    def value_step(carry, items):
        key_block, value_block, key_pos = items
        probs_low = probs_of(key_block, key_pos).astype(jnp.bfloat16)
        return (
            carry
            + jnp.einsum(
                "kgts,skd->tkgd", probs_low, value_block, preferred_element_type=jnp.float32
            ),
            None,
        )

    attn_rows, unused = lax.scan(
        value_step,
        jnp.zeros((present_rows, KEY_VALUE_HEADS, group_size, HEAD_SIZE), jnp.float32),
        (key_block_list, value_block_list, position_blocks),
    )
    query_width = rotated_queries.shape[1]
    attended_low = attn_rows.reshape(present_rows, query_width).astype(jnp.bfloat16)
    hidden_in = inputs_f + jnp.dot(attended_low, output_full, preferred_element_type=jnp.float32)
    gain_two, gate_full, up_full, down_full = (
        lax.all_gather(ffn_gain, "fsdp", axis=0, tiled=True),
        lax.all_gather(gate_weight, "fsdp", axis=0, tiled=True),
        lax.all_gather(up_weight, "fsdp", axis=0, tiled=True),
        lax.all_gather(down_weight, "fsdp", axis=0, tiled=True),
    )
    gain_two = gain_two.astype(jnp.float32)
    scale_two = rms_scale(hidden_in)
    normed_two = hidden_in * scale_two
    ffn_in = (normed_two * gain_two).astype(jnp.bfloat16)
    gate = jnp.dot(ffn_in, gate_full, preferred_element_type=jnp.float32)
    upper = jnp.dot(ffn_in, up_full, preferred_element_type=jnp.float32)
    sigma = jax.nn.sigmoid(gate)
    act_low = (gate * sigma * upper).astype(jnp.bfloat16)
    layer_out = (
        hidden_in + jnp.dot(act_low, down_full, preferred_element_type=jnp.float32)
    ).astype(jnp.bfloat16)
    cot_rows = out_cotangent[0]
    cot_f = cot_rows.astype(jnp.float32)
    down_local = jnp.dot(act_low.T, cot_rows, preferred_element_type=jnp.float32)
    d_act = jnp.dot(cot_rows, down_full.T, preferred_element_type=jnp.float32)
    d_gate = (d_act * upper * sigma * (1.0 + gate * (1.0 - sigma))).astype(jnp.bfloat16)
    d_up = (d_act * gate * sigma).astype(jnp.bfloat16)
    gate_local = jnp.dot(ffn_in.T, d_gate, preferred_element_type=jnp.float32)
    up_local = jnp.dot(ffn_in.T, d_up, preferred_element_type=jnp.float32)
    d_ffn_in = jnp.dot(d_gate, gate_full.T, preferred_element_type=jnp.float32) + jnp.dot(
        d_up, up_full.T, preferred_element_type=jnp.float32
    )
    gain_two_local = jnp.sum(d_ffn_in * normed_two, axis=0)
    scaled_two = d_ffn_in * gain_two
    d_hidden = cot_f + scale_two * (
        scaled_two - normed_two * jnp.mean(scaled_two * normed_two, axis=-1, keepdims=True)
    )
    d_branch = d_hidden.astype(jnp.bfloat16)
    output_local = jnp.dot(attended_low.T, d_branch, preferred_element_type=jnp.float32)
    attended_gradient = jnp.dot(d_branch, output_full.T, preferred_element_type=jnp.float32).astype(
        jnp.bfloat16
    )
    grouped_output_gradient = attended_gradient.reshape(
        present_rows, KEY_VALUE_HEADS, group_size, HEAD_SIZE
    )
    delta = jnp.einsum("tkgd,tkgd->kgt", grouped_output_gradient.astype(jnp.float32), attn_rows)

    def grad_step(carry, items):
        key_block, value_block, key_pos = items
        probs = probs_of(key_block, key_pos)
        d_probs = jnp.einsum(
            "tkgd,skd->kgts",
            grouped_output_gradient,
            value_block,
            preferred_element_type=jnp.float32,
        )
        d_score = (probs * (d_probs - delta[..., None]) * scale).astype(jnp.bfloat16)
        carry = carry + jnp.einsum(
            "kgts,skd->tkgd", d_score, key_block, preferred_element_type=jnp.float32
        )
        d_key_block = jnp.einsum(
            "kgts,tkgd->skd", d_score, grouped_queries, preferred_element_type=jnp.float32
        )
        d_value_block = jnp.einsum(
            "kgts,tkgd->skd",
            probs.astype(jnp.bfloat16),
            grouped_output_gradient,
            preferred_element_type=jnp.float32,
        )
        return (carry, (d_key_block, d_value_block))

    d_query_rot, (d_key_parts, d_value_parts) = lax.scan(
        grad_step,
        jnp.zeros((present_rows, KEY_VALUE_HEADS, group_size, HEAD_SIZE), jnp.float32),
        (key_block_list, value_block_list, position_blocks),
    )
    key_width = rotated_keys.shape[1]
    d_key_all = d_key_parts.reshape(stream_len, key_width)
    d_value_all = d_value_parts.reshape(stream_len, key_width)
    rotated_key_gradient, d_value = (
        lax.psum_scatter(d_key_all, "ctx", scatter_dimension=0, tiled=True),
        lax.psum_scatter(d_value_all, "ctx", scatter_dimension=0, tiled=True),
    )
    d_query = rotate_half(
        d_query_rot.reshape(present_rows, query_width), cosine_table, sine_table, QUERY_HEADS, False
    ).astype(jnp.bfloat16)
    key_gradient = rotate_half(
        rotated_key_gradient, cosine_table, sine_table, KEY_VALUE_HEADS, False
    ).astype(jnp.bfloat16)
    d_value_low = d_value.astype(jnp.bfloat16)
    query_local = jnp.dot(normalized_input.T, d_query, preferred_element_type=jnp.float32)
    key_local = jnp.dot(normalized_input.T, key_gradient, preferred_element_type=jnp.float32)
    value_local = jnp.dot(normalized_input.T, d_value_low, preferred_element_type=jnp.float32)
    d_normed = (
        jnp.dot(d_query, query_full.T, preferred_element_type=jnp.float32)
        + jnp.dot(key_gradient, key_full.T, preferred_element_type=jnp.float32)
        + jnp.dot(d_value_low, value_full.T, preferred_element_type=jnp.float32)
    )
    gain_one_local = jnp.sum(d_normed * normed_one, axis=0)
    scaled_one = d_normed * gain_one
    tokens_grad = d_hidden + scale_one * (
        scaled_one - normed_one * jnp.mean(scaled_one * normed_one, axis=-1, keepdims=True)
    )
    column_sums = (
        lax.psum_scatter(query_local, "ctx", scatter_dimension=1, tiled=True),
        lax.psum_scatter(key_local, "ctx", scatter_dimension=1, tiled=True),
        lax.psum_scatter(value_local, "ctx", scatter_dimension=1, tiled=True),
        lax.psum_scatter(output_local, "ctx", scatter_dimension=1, tiled=True),
        lax.psum_scatter(gate_local, "ctx", scatter_dimension=1, tiled=True),
        lax.psum_scatter(up_local, "ctx", scatter_dimension=1, tiled=True),
        lax.psum_scatter(down_local, "ctx", scatter_dimension=1, tiled=True),
    )
    gain_totals = lax.psum((gain_one_local, gain_two_local), "ctx")
    finals = (
        lax.psum_scatter(
            gain_totals[0].astype(jnp.bfloat16), "fsdp", scatter_dimension=0, tiled=True
        ).astype(jnp.float32),
        lax.psum_scatter(
            column_sums[0].astype(jnp.bfloat16), "fsdp", scatter_dimension=0, tiled=True
        ).astype(jnp.float32),
        lax.psum_scatter(
            column_sums[1].astype(jnp.bfloat16), "fsdp", scatter_dimension=0, tiled=True
        ).astype(jnp.float32),
        lax.psum_scatter(
            column_sums[2].astype(jnp.bfloat16), "fsdp", scatter_dimension=0, tiled=True
        ).astype(jnp.float32),
        lax.psum_scatter(
            column_sums[3].astype(jnp.bfloat16), "fsdp", scatter_dimension=0, tiled=True
        ).astype(jnp.float32),
        lax.psum_scatter(
            gain_totals[1].astype(jnp.bfloat16), "fsdp", scatter_dimension=0, tiled=True
        ).astype(jnp.float32),
        lax.psum_scatter(
            column_sums[4].astype(jnp.bfloat16), "fsdp", scatter_dimension=0, tiled=True
        ).astype(jnp.float32),
        lax.psum_scatter(
            column_sums[5].astype(jnp.bfloat16), "fsdp", scatter_dimension=0, tiled=True
        ).astype(jnp.float32),
        lax.psum_scatter(
            column_sums[6].astype(jnp.bfloat16), "fsdp", scatter_dimension=0, tiled=True
        ).astype(jnp.float32),
    )
    gain_one_grad = finals[0]
    gain_two_grad = finals[5]
    matrices = (finals[1], finals[2], finals[3], finals[4], finals[6], finals[7], finals[8])
    return (
        layer_out[None],
        tokens_grad.astype(jnp.bfloat16)[None],
        gain_one_grad,
        matrices[0],
        matrices[1],
        matrices[2],
        matrices[3],
        gain_two_grad,
        matrices[4],
        matrices[5],
        matrices[6],
    )


def solution(mesh):
    return jax.shard_map(
        local,
        mesh=mesh,
        in_specs=(
            P("fsdp", "ctx", None),
            P("fsdp", None),
            P("fsdp"),
            P("fsdp", None),
            P("fsdp", None),
            P("fsdp", None),
            P("fsdp", None),
            P("fsdp"),
            P("fsdp", None),
            P("fsdp", None),
            P("fsdp", None),
            P("fsdp", "ctx", None),
        ),
        out_specs=(
            P("fsdp", "ctx", None),
            P("fsdp", "ctx", None),
            P("fsdp"),
            P("fsdp", "ctx"),
            P("fsdp", "ctx"),
            P("fsdp", "ctx"),
            P("fsdp", "ctx"),
            P("fsdp"),
            P("fsdp", "ctx"),
            P("fsdp", "ctx"),
            P("fsdp", "ctx"),
        ),
        check_vma=False,
    )
```

```python
import math

import jax
import jax.numpy as jnp
import numpy as np
from jax import lax
from jax.experimental import pallas as pl
from jax.experimental.pallas import tpu as pltpu
from jax.sharding import PartitionSpec as P

QUERY_HEADS = 18
KEY_VALUE_HEADS = 6
HEAD_SIZE = 64
GROUP = QUERY_HEADS // KEY_VALUE_HEADS
HALF = HEAD_SIZE // 2
LANES = 128

EPS = 1e-05
BASE = 10000.0
NEGATIVE_FILL = -1e30
BF = jnp.bfloat16
F32 = jnp.float32
MIB = 1024 * 1024


def dot(left, right, left_dim, right_dim):
    return lax.dot_general(
        left, right, (((left_dim,), (right_dim,)), ((), ())), preferred_element_type=F32
    )


def rms_scale(values):
    return lax.rsqrt(jnp.mean(values * values, axis=-1, keepdims=True) + EPS)


def stored_position(row_ids, rows_per_dev, devices_ctx):
    half_len = rows_per_dev // 2
    owner_dev = row_ids // rows_per_dev
    offset_in = row_ids % rows_per_dev
    early = owner_dev * half_len + offset_in
    later = (2 * devices_ctx - 1 - owner_dev) * half_len + offset_in - half_len
    return jnp.where(offset_in < half_len, early, later)


def relative_ids(n):
    return [2 * j + k for k in range(2) for j in range(n // 2)]


def moved_block(n, i, b):
    rel = relative_ids(n)
    return rel.index(rel[b] ^ rel[i])


def hop(value, axis, bits):
    n = lax.axis_size(axis)
    return lax.ppermute(value, axis, [(i, i ^ bits) for i in range(n)])


def after(value, *others):
    return lax.optimization_barrier((value, *others))[0]


def gather_blocks(value, n):
    same = [value] + [hop(value, "ctx", 2 * j) for j in range(1, n // 2)]
    return same + [hop(block, "ctx", 1) for block in same]


def gather_chips(value, n):
    blocks = [value]
    for j in range(1, n // 2):
        sent = after(value, blocks[1]) if j == 3 else value
        blocks.append(hop(sent, "ctx", 2 * j))
    return blocks


def aligned(index, size):
    return pl.ds(pl.multiple_of(index * size, 16), size)


def turn(values, cosine, sine, sign):
    pieces = []
    for at in range(0, values.shape[0], HEAD_SIZE):
        first = values[at : at + HALF]
        second = values[at + HALF : at + HEAD_SIZE]
        pieces.append(first * cosine - sign * (second * sine))
        pieces.append(second * cosine + sign * (first * sine))
    return jnp.concatenate(pieces, axis=0)


def head_rows(h, g):
    return slice(HEAD_SIZE * (GROUP * h + g), HEAD_SIZE * (GROUP * h + g + 1))


def group_columns(ref, h):
    return jnp.concatenate([ref[head_rows(h, g), :] for g in range(GROUP)], axis=1)


def mask_bias(me, starts_ref, n, tokens):
    shape = (tokens, tokens)
    half_len = tokens // 2

    def position(device, offset):
        early = device * half_len + offset
        return jnp.where(offset < half_len, early, (2 * n - 2 - device) * half_len + offset)

    q_pos = position(me, lax.broadcasted_iota(jnp.int32, shape, 1))
    begin = jnp.zeros(shape, jnp.int32)
    for d in range(starts_ref.shape[1]):
        start = starts_ref[0, d]
        begin = jnp.where(q_pos >= start, jnp.maximum(begin, start), begin)
    blocks = []
    for bits in relative_ids(n):
        k_pos = position(me ^ bits, lax.broadcasted_iota(jnp.int32, shape, 0))
        visible = (k_pos >= begin) & (k_pos <= q_pos)
        blocks.append(jnp.where(visible, 0.0, NEGATIVE_FILL).astype(F32))
    return jnp.concatenate(blocks, axis=0)


SMEM = pl.BlockSpec(memory_space=pltpu.SMEM)


def kernel_call(body, name, outs, args, scratch=(), scalars=0, limit=60):
    shapes = [jax.ShapeDtypeStruct(shape, dtype) for shape, dtype in outs]

    def whole(value):
        return pl.BlockSpec(value.shape, lambda g: (0,) * len(value.shape))

    return pl.pallas_call(
        body,
        grid=(1,),
        in_specs=[SMEM] * scalars + [whole(a) for a in args[scalars:]],
        out_specs=[whole(s) for s in shapes],
        out_shape=shapes,
        scratch_shapes=[pltpu.VMEM(shape, dtype) for shape, dtype in scratch],
        compiler_params=pltpu.CompilerParams(vmem_limit_bytes=limit * MIB),
        cost_estimate=pl.CostEstimate(flops=1, bytes_accessed=1, transcendentals=0),
        name=name,
    )(*args)


def project_kernel(level_ref, *refs, n, depth, cols):
    qc, kc = cols
    half = n // 2
    x_refs, w_refs = refs[:n], refs[n : n + depth]
    normed_ref, weight_t_ref, out_t_ref, gains_ref = refs[n + depth : n + depth + 4]
    message_refs = refs[n + depth + 4 : n + depth + 4 + half]
    weight_ref, raw_ref, row_ref = refs[n + depth + 4 + half :]
    rows = row_ref.shape[2]
    tokens = x_refs[0].shape[0]
    width = qc + 2 * kc
    for k in range(depth):
        weight_ref[aligned(level_ref[0] ^ k, rows), :] = w_refs[k][:rows, :]
        row_ref[level_ref[0] ^ k] = w_refs[k][rows:, :rows].astype(F32)
    turned = weight_ref[...].astype(F32).T.astype(BF)
    weight_t_ref[...] = turned[:width]
    out_t_ref[...] = turned[width:]
    gains = jnp.concatenate([row_ref[t] for t in range(depth)], axis=1)
    gains_ref[...] = gains[:8]
    for i in range(n):
        values = x_refs[i][...].astype(F32)
        normed = (values * rms_scale(values) * gains[:1]).astype(BF)
        normed_ref[tokens * i : tokens * (i + 1), :] = normed
        raw_ref[i] = dot(weight_t_ref[...], normed, 1, 1).astype(BF)
    for j in range(half):
        for b in range(n):
            message_refs[j][2 * kc * b : 2 * kc * (b + 1), :] = raw_ref[b, qc:, :]
        at = 2 * kc * n
        message_refs[j][at : at + qc, :] = raw_ref[j, :qc, :]
        message_refs[j][at + qc : at + 2 * qc, :] = raw_ref[half + j, :qc, :]


def project(level, x_blocks, w_pieces, n, depth, qc, kc):
    tokens, width = x_blocks[0].shape
    rows = width // depth
    cols = qc + 2 * kc
    spare = w_pieces[0].shape[0] - rows
    length = n * tokens
    all_cols = w_pieces[0].shape[1]

    def body(*refs):
        project_kernel(*refs, n=n, depth=depth, cols=(qc, kc))

    return kernel_call(
        body,
        "project",
        [((length, width), BF), ((cols, width), BF), ((all_cols - cols, width), BF), ((8, width), F32)]
        + [((2 * kc * n + 2 * qc, tokens), BF)] * (n // 2),
        [level, *x_blocks, *w_pieces],
        scratch=[((width, all_cols), BF), ((n, cols, tokens), BF), ((depth, spare, rows), F32)],
        scalars=1,
    )


def attention_forward_kernel(me_ref, starts_ref, *refs, n):
    half = n // 2
    same, other = refs[:half], refs[half:n]
    cos_ref, sin_ref = refs[n : n + 2]
    low_ref, att_ref, lse_ref, qrot_ref, krot_ref, v_ref = refs[n + 2 : n + 8]
    q_ref, k_ref, bias_ref = refs[n + 8 :]
    tokens = q_ref.shape[1]
    qc, kc = q_ref.shape[0] // n, k_ref.shape[0] // n
    rel = relative_ids(n)
    for i in range(n):
        device = me_ref[0] ^ rel[i]
        source = same[i] if i < half else other[i - half]
        at = 2 * kc * n + (0 if i < half else qc)
        q_ref[aligned(device, qc), :] = source[at : at + qc, :]
        to = aligned(device, kc)
        for b in range(n):
            start = 2 * kc * moved_block(n, i, b)
            lanes = slice(tokens * b, tokens * (b + 1))
            k_ref[to, lanes] = source[start : start + kc, :]
            v_ref[to, lanes] = source[start + kc : start + 2 * kc, :]
    bias_ref[...] = mask_bias(me_ref[0], starts_ref, n, tokens)
    for h in range(KEY_VALUE_HEADS):
        rows = slice(HEAD_SIZE * h, HEAD_SIZE * (h + 1))
        krot_ref[rows, :] = turn(k_ref[rows, :].astype(F32), cos_ref[...], sin_ref[...], 1.0).astype(BF)
        for g in range(GROUP):
            at = head_rows(h, g)
            turned = turn(
                q_ref[at, :].astype(F32), cos_ref[:, :tokens], sin_ref[:, :tokens], 1.0
            ).astype(BF)
            qrot_ref[at, :] = turned * BF(HEAD_SIZE**-0.5)
    for h in range(KEY_VALUE_HEADS):
        rows = slice(HEAD_SIZE * h, HEAD_SIZE * (h + 1))
        bias = jnp.concatenate([bias_ref[...]] * GROUP, axis=1)
        scores = dot(krot_ref[rows, :], group_columns(qrot_ref, h), 0, 0) + bias
        top = jnp.max(scores, axis=0, keepdims=True)
        weights = jnp.exp(scores - top)
        total = jnp.sum(weights, axis=0, keepdims=True)
        lse_ref[h : h + 1, :] = top + jnp.log(total)
        mixed = dot(v_ref[rows, :], weights.astype(BF), 1, 0) / total
        for g in range(GROUP):
            att_ref[head_rows(h, g), :] = mixed[:, tokens * g : tokens * (g + 1)]
    low_ref[...] = att_ref[...].T.astype(BF)


def attention_forward(me, starts, same, other, cosine, sine, n, query_width, key_width):
    tokens = same[0].shape[1]
    length = n * tokens

    def body(*refs):
        attention_forward_kernel(*refs, n=n)

    return kernel_call(
        body,
        "attention_forward",
        [
            ((tokens, query_width), BF),
            ((query_width, tokens), F32),
            ((KEY_VALUE_HEADS, GROUP * tokens), F32),
            ((query_width, tokens), BF),
            ((key_width, length), BF),
            ((key_width, length), BF),
        ],
        [me, starts, *same, *other, cosine, sine],
        scratch=[((query_width, tokens), BF), ((key_width, length), BF), ((length, tokens), F32)],
        scalars=2,
    )


def feed_forward_kernel(me_ref, *refs, n, depth):
    half = n // 2
    out_pieces, downs, (w_ref, gains_ref) = refs[:n], refs[n : n + depth], refs[n + depth : n + depth + 2]
    at = n + depth + 2
    x_refs, a_refs, g_refs = (refs[at + n * i : at + n * (i + 1)] for i in range(3))
    at += 3 * n
    d_same = refs[at : at + half]
    (
        d_other_ref, y_same_ref, y_other_ref, ffn_ref, act_ref, dgu_ref, part_ref, own_ref, wo_ref, wd_ref,
    ) = refs[at + half :]
    tokens, width = x_refs[0].shape
    fc = act_ref.shape[1]
    rel = relative_ids(n)
    for i in range(n):
        wo_ref[aligned(me_ref[0] ^ rel[i], out_pieces[i].shape[0]), :] = out_pieces[i][...]
    share, down_rows = n // depth, wd_ref.shape[0] // depth
    part = jnp.zeros((1, width), F32)
    for j in range(half):
        rows = slice(2 * tokens * j, 2 * tokens * (j + 1))
        values, attended = (
            jnp.concatenate([some[j][...], some[half + j][...]], axis=0) for some in (x_refs, a_refs)
        )
        hidden = values.astype(F32) + dot(attended, wo_ref[...], 1, 1)
        if j == 0:
            own_ref[...] = hidden[:tokens]
        normed = hidden * rms_scale(hidden)
        ffn_in = (normed * gains_ref[1:2, :]).astype(BF)
        ffn_ref[rows, :] = ffn_in
        gate = dot(ffn_in, w_ref[:, :fc], 1, 0)
        upper = dot(ffn_in, w_ref[:, fc : 2 * fc], 1, 0)
        if j == 0:
            for t in range(depth):
                to = aligned((me_ref[0] // share) ^ t, down_rows)
                for i in range(width // fc):
                    wd_ref[to, fc * i : fc * (i + 1)] = downs[t][down_rows * i : down_rows * (i + 1), :]
        cot = jnp.concatenate([g_refs[j][...], g_refs[half + j][...]], axis=0)
        d_act = dot(cot, wd_ref[...], 1, 1)
        sigma = jax.nn.sigmoid(gate)
        silu = gate * sigma
        act = (silu * upper).astype(BF)
        act_ref[rows, :] = act
        d_gate = (d_act * upper * sigma * (1.0 + gate * (1.0 - sigma))).astype(BF)
        d_up = (d_act * silu).astype(BF)
        dgu_ref[rows, :fc] = d_gate
        dgu_ref[rows, fc:] = d_up
        d_in = dot(d_gate, w_ref[:, :fc], 1, 1) + dot(d_up, w_ref[:, fc : 2 * fc], 1, 1)
        part = part + jnp.sum(d_in * normed, axis=0, keepdims=True)
        d_same[j][...] = d_in[:tokens].astype(BF)
        d_other_ref[j] = d_in[tokens:].astype(BF)
        out = dot(act, wd_ref[...], 1, 0)
        y_same_ref[j] = out[:tokens].astype(BF)
        y_other_ref[j] = out[tokens:].astype(BF)
    part_ref[...] = jnp.broadcast_to(part, part_ref.shape)


def feed_forward(me, out_pieces, downs, ffn_weights, gains, x_blocks, a_blocks, g_blocks, n, depth):
    tokens, width = x_blocks[0].shape
    fc = downs[0].shape[1]
    half, rows = n // 2, n * tokens
    by_chip = [some[side + j] for some in (x_blocks, a_blocks, g_blocks) for side in (0, half) for j in range(half)]

    def body(*refs):
        feed_forward_kernel(*refs, n=n, depth=depth)

    outs = kernel_call(
        body,
        "feed_forward",
        [((tokens, width), BF)] * half
        + [((half, tokens, width), BF)] * 3
        + [((rows, width), BF), ((rows, fc), BF), ((rows, 2 * fc), BF), ((8, width), F32)]
        + [((tokens, width), F32)],
        [me, *out_pieces, *downs, ffn_weights, gains, *by_chip],
        scratch=[((width, out_pieces[0].shape[1]), BF), ((fc, width), BF)],
        scalars=1,
    )
    return outs[:half], *outs[half:]


def ffn_grads_kernel(me_ref, *refs, n):
    half = n // 2
    ffn_ref, act_ref, dgu_ref = refs[:3]
    g_refs = refs[3 : 3 + n]
    gu_ref, packed_refs, down_ref = refs[3 + n], refs[4 + n : 4 + n + half], refs[4 + n + half]
    gu_ref[...] = dot(ffn_ref[...], dgu_ref[...], 0, 0).astype(BF)
    g_all = jnp.concatenate([g_refs[side + j][...] for j in range(half) for side in (0, half)], axis=0)
    down_ref[...] = dot(g_all, act_ref[...], 0, 0).astype(BF)
    dc = down_ref.shape[0] // n
    rel = relative_ids(n)
    for i in range(n):
        side = dc * (i // half)
        packed_refs[i % half][side : side + dc, :] = down_ref[aligned(me_ref[0] ^ rel[i], dc), :]


def ffn_grads(me, ffn, act, dgu, g_blocks, n):
    half = n // 2
    width, fc = ffn.shape[1], act.shape[1]
    dc = width // n

    def body(*refs):
        ffn_grads_kernel(*refs, n=n)

    return kernel_call(
        body,
        "ffn_grads",
        [((width, 2 * fc), BF)] + [((2 * dc, fc), BF)] * half,
        [me, ffn, act, dgu, *g_blocks],
        scratch=[((width, fc), BF)],
        scalars=1,
    )


def level_shapes(shape, depth):
    return [(shape, BF)] * (depth // 2) + [((depth // 2, *shape), BF)]


def store_level(refs, k, value):
    if k % 2:
        refs[-1][k // 2] = value
    else:
        refs[k // 2][...] = value


def sum_levels(pieces):
    near, far = pieces[:-1], pieces[-1]
    got = hop(far, "fsdp", 1)
    if len(near) == 1:
        return [near[0], got[0]]
    both = [(piece.astype(F32) + got[k].astype(F32)).astype(BF) for k, piece in enumerate(near)]
    return [both[0]] + [hop(both[k], "fsdp", 2 * k) for k in range(1, len(both))]


def unpack_down_kernel(me_ref, level_ref, *refs, n, depth):
    half = n // 2
    same, far = refs[:half], refs[half:n]
    grad_refs, grad_ref = refs[n:-1], refs[-1]
    dc = grad_ref.shape[1]
    share = n // depth
    fc = grad_ref.shape[2] // share
    for j in range(half):
        for side, piece in enumerate((same[j][:dc, :], far[j][dc:, :])):
            device = me_ref[0] ^ (2 * j + side)
            lanes = pl.ds(pl.multiple_of((device % share) * fc, LANES), fc)
            grad_ref[device // share, :, lanes] = piece
    for k in range(depth):
        grad_refs[k][...] = grad_ref[level_ref[0] ^ k]


def unpack_down(me, level, same, far, n, depth):
    rows, fc = same[0].shape

    def body(*refs):
        unpack_down_kernel(*refs, n=n, depth=depth)

    piece = (rows // 2, fc * n // depth)
    return kernel_call(
        body,
        "unpack_down",
        [(piece, BF)] * depth,
        [me, level, *same, *far],
        scratch=[((depth, *piece), BF)],
        scalars=2,
    )


def attention_backward_kernel(me_ref, starts_ref, *refs, n):
    half = n // 2
    sums = refs[: half + 1]
    (g_ref, hidden_ref, gains_ref, q_ref, k_ref, v_ref, att_ref, lse_ref, cos_ref, sin_ref) = refs[
        half + 1 : half + 11
    ]
    out_pieces = refs[half + 11 : half + 11 + n]
    dh_ref, same_ref = refs[half + 11 + n : half + 13 + n]
    other_refs = refs[half + 13 + n : n + n + 13]
    do_ref, db_ref, dq_ref, dk_ref, dv_ref, bias_ref, message_ref, wo_ref = refs[2 * n + 13 :]
    rel = relative_ids(n)
    bias_ref[...] = mask_bias(me_ref[0], starts_ref, n, q_ref.shape[1])
    tokens = q_ref.shape[1]
    d_in = sums[0][...].astype(F32) + sums[1][0].astype(F32)
    for r in sums[2:]:
        d_in = d_in + r[...].astype(F32)
    hidden = hidden_ref[...]
    scale = rms_scale(hidden)
    normed = hidden * scale
    scaled = d_in * gains_ref[1:2, :]
    d_hidden = g_ref[...].astype(F32) + scale * (
        scaled - normed * jnp.mean(scaled * normed, axis=-1, keepdims=True)
    )
    dh_ref[...] = d_hidden
    db_ref[...] = d_hidden.T.astype(BF)
    for i in range(n):
        wo_ref[aligned(me_ref[0] ^ rel[i], out_pieces[i].shape[0]), :] = out_pieces[i][...]
    do_ref[...] = dot(wo_ref[...], db_ref[...], 0, 0).astype(BF)
    for h in range(KEY_VALUE_HEADS):
        rows = slice(HEAD_SIZE * h, HEAD_SIZE * (h + 1))
        queries = group_columns(q_ref, h)
        grads = group_columns(do_ref, h)
        delta = jnp.sum(grads.astype(F32) * group_columns(att_ref, h), axis=0, keepdims=True)
        bias = jnp.concatenate([bias_ref[...]] * GROUP, axis=1)
        scores = dot(k_ref[rows, :], queries, 0, 0) + bias
        probs = jnp.exp(scores - lse_ref[h : h + 1, :])
        d_probs = dot(v_ref[rows, :], grads, 0, 0)
        d_score = (probs * (d_probs - delta)).astype(BF)
        d_query = dot(k_ref[rows, :], d_score, 1, 0) * (HEAD_SIZE**-0.5)
        for g in range(GROUP):
            dq_ref[head_rows(h, g), :] = turn(
                d_query[:, tokens * g : tokens * (g + 1)], cos_ref[:, :tokens], sin_ref[:, :tokens], -1.0
            ).astype(BF)
        d_key = dot(queries, d_score, 1, 1)
        dk_ref[rows, :] = turn(d_key, cos_ref[...], sin_ref[...], -1.0).astype(BF)
        dv_ref[rows, :] = dot(grads, probs.astype(BF), 1, 1).astype(BF)
    qc, dc, kc = dq_ref.shape[0] // n, db_ref.shape[0] // n, dk_ref.shape[0] // n
    flat = 2 * kc * n
    for i in (*range(half, n), *range(half)):
        if i == 0:
            for j in range(half):
                other_refs[j][...] = message_ref[j]
        device = me_ref[0] ^ rel[i]
        to = same_ref if i < half else message_ref
        j = i % half
        to[j, flat : flat + qc, :] = dq_ref[aligned(device, qc), :]
        to[j, flat + qc : flat + qc + dc, :] = db_ref[aligned(device, dc), :]
        at = aligned(device, kc)
        for b in range(n):
            start = 2 * kc * moved_block(n, i, b)
            lanes = slice(tokens * b, tokens * (b + 1))
            to[j, start : start + kc, :] = dk_ref[at, lanes]
            to[j, start + kc : start + 2 * kc, :] = dv_ref[at, lanes]


def attention_backward(me, starts, sums, g, hidden, gains, out_pieces, saved, cosine, sine, n):
    q_rot, k_rot, v_low, att, lse = saved
    query_width, tokens = q_rot.shape
    width = hidden.shape[1]
    key_width, length = k_rot.shape
    rows = 2 * key_width + (query_width + width) // n

    def body(*refs):
        attention_backward_kernel(*refs, n=n)

    return kernel_call(
        body,
        "attention_backward",
        [((tokens, width), F32), ((n // 2, rows, tokens), BF)] + [((rows, tokens), BF)] * (n // 2),
        [me, starts, *sums, g, hidden, gains, q_rot, k_rot, v_low, att, lse, cosine, sine, *out_pieces],
        scratch=[
            ((query_width, tokens), BF), ((width, tokens), BF), ((query_width, tokens), BF),
            ((key_width, length), BF), ((key_width, length), BF), ((length, tokens), F32),
            ((n // 2, rows, tokens), BF), ((width, query_width), BF),
        ],
        scalars=2,
    )


def pair_kernel(same_ref, *refs, flat):
    half, rows = same_ref.shape[:2]
    others, outs = refs[:half], refs[half:]
    more = rows - flat
    for j in reversed(range(half)):
        other = others[j][...]
        both = same_ref[j, :flat, :].astype(F32) + other[:flat].astype(F32)
        outs[j][:flat, :] = both.astype(BF)
        outs[j][flat : flat + more, :] = same_ref[j, flat:, :]
        outs[j][flat + more :, :] = other[flat:]


def pair(same, others, flat):
    half, rows, tokens = same.shape

    def body(*refs):
        pair_kernel(*refs, flat=flat)

    return kernel_call(
        body, "pair", [((2 * rows - flat, tokens), BF)] * half, [same, *others]
    )


def input_grads_kernel(level_ref, *refs, n, depth, cols):
    qc, kc, dc = cols
    half = n // 2
    got, a_refs, x_refs = refs[:half], refs[half : half + n], refs[half + n : half + 2 * n]
    normed_ref, weight_t_ref = refs[half + 2 * n : half + 2 * n + 2]
    at = half + 2 * n + 2
    part_two_ref, other_ref = refs[at : at + 2]
    same_refs = refs[at + 2 : at + 2 + half]
    level_refs = refs[at + 2 + half : -4]
    d_ref, b_ref, last_ref, row_ref = refs[-4:]
    tokens = x_refs[0].shape[0]
    flat = 2 * kc * n
    total = got[0][:flat, :].astype(F32)
    for r in got[1:]:
        total = total + r[:flat, :].astype(F32)
    total = total.astype(BF)
    for i in range(n):
        lanes = slice(tokens * i, tokens * (i + 1))
        start = flat + (qc + dc) * (i // half)
        source = got[i % half]
        d_ref[:qc, lanes] = source[start : start + qc, :]
        d_ref[qc:, lanes] = total[2 * kc * i : 2 * kc * (i + 1)]
        b_ref[:, lanes] = source[start + qc : start + qc + dc, :]
    width = x_refs[0].shape[1]
    part = jnp.zeros((1, width), F32)
    for i in (*range(half, n), *range(half)):
        lanes = slice(tokens * i, tokens * (i + 1))
        d_normed = dot(d_ref[:, lanes], weight_t_ref[...], 0, 0)
        values = x_refs[i][...].astype(F32)
        part = part + jnp.sum(d_normed * (values * rms_scale(values)), axis=0, keepdims=True)
        if i < half:
            same_refs[i][...] = d_normed.astype(BF)
        else:
            other_ref[i - half] = d_normed.astype(BF)
    cut = qc + 2 * kc
    last_ref[:, :cut] = dot(normed_ref[...], d_ref[...], 0, 1).astype(BF)
    attended = jnp.concatenate([r[...] for r in a_refs], axis=0)
    last_ref[:, cut:] = dot(attended, b_ref[...], 0, 1).astype(BF)
    rows, wide = width // depth, row_ref.shape[2]
    both = jnp.concatenate([part, part_two_ref[:1, :], jnp.zeros((14, width), F32)], axis=0)
    for t in range(depth):
        row_ref[t, :, :rows] = both[:, rows * t : rows * (t + 1)]
        row_ref[t, :, rows:] = jnp.zeros((16, wide - rows), F32)
    for k in range(depth):
        piece = [last_ref[aligned(level_ref[0] ^ k, rows), :], row_ref[level_ref[0] ^ k].astype(BF)]
        store_level(level_refs, k, jnp.concatenate(piece, axis=0))


def input_grads(level, got, attended, x_blocks, normed_in, weight_t, part_two, n, depth, qc, kc, dc):
    half = n // 2
    tokens, width = x_blocks[0].shape
    length = n * tokens
    cols = qc + 2 * kc + dc

    def body(*refs):
        input_grads_kernel(*refs, n=n, depth=depth, cols=(qc, kc, dc))

    return kernel_call(
        body,
        "input_grads",
        [((half, tokens, width), BF)]
        + [((tokens, width), BF)] * half
        + level_shapes((width // depth + 16, cols), depth),
        [level, *got, *attended, *x_blocks, normed_in, weight_t, part_two],
        scratch=[
            ((qc + 2 * kc, length), BF), ((dc, length), BF), ((width, cols), BF), ((depth, 16, cols), F32),
        ],
        scalars=1,
    )


def summed(parts, tokens):
    total = parts[0].astype(F32)
    for part in parts[1:]:
        total = total + part[:tokens].astype(F32)
    return total


def finish_kernel(*refs, half, terms, cuts):
    sums, y_sums = refs[: half + 1], refs[half + 1 : 2 * half + 2]
    at = 2 * half + 2
    pieces, downs = refs[at : at + terms[0]], refs[at + terms[0] : at + sum(terms)]
    at += sum(terms)
    gu_ref, hidden_ref, dh_ref, x_ref, gains_ref = refs[at : at + 5]
    y_ref, out_ref, down_ref, gate_ref, up_ref = refs[at + 5 : at + 10]
    fc = gate_ref.shape[1]
    gate_ref[...] = gu_ref[:, :fc].astype(F32)
    up_ref[...] = gu_ref[:, fc:].astype(F32)
    y_ref[...] = (
        hidden_ref[...]
        + summed([y_sums[0][0], y_sums[1][0], *(r[...] for r in y_sums[2:])], x_ref.shape[0])
    ).astype(BF)
    total = downs[0][...].astype(F32)
    for r in downs[1:]:
        total = total + r[...].astype(F32)
    down_ref[...] = total
    d_normed = summed([sums[0][...], sums[1][0], *(r[...] for r in sums[2:])], x_ref.shape[0])
    values = x_ref[...].astype(F32)
    scale = rms_scale(values)
    normed = values * scale
    scaled = d_normed * gains_ref[0:1, :]
    out_ref[...] = (
        dh_ref[...]
        + scale * (scaled - normed * jnp.mean(scaled * normed, axis=-1, keepdims=True))
    ).astype(BF)
    total = pieces[0][...].astype(F32)
    for r in pieces[1:]:
        total = total + r[...].astype(F32)
    turned = total[: total.shape[0] - 16].T
    for grad_ref, start, stop in zip(refs[at + 10 :], cuts[:-1], cuts[1:]):
        grad_ref[...] = turned[start:stop]


def finish(sums, y_sums, pieces, downs, gate_up, hidden, d_hidden, x, gains, cuts):
    height = pieces[0].shape[0]

    def body(*refs):
        finish_kernel(*refs, half=len(sums) - 1, terms=(len(pieces), len(downs)), cuts=cuts)

    return kernel_call(
        body,
        "finish",
        [(x.shape, BF), (x.shape, BF), (downs[0].shape, F32)]
        + [((gate_up.shape[0], gate_up.shape[1] // 2), F32)] * 2
        + [((stop - start, height - 16), F32) for start, stop in zip(cuts[:-1], cuts[1:])],
        [*sums, *y_sums, *pieces, *downs, gate_up, hidden, d_hidden, x, gains],
    )


def pair_sums(same, far):
    return [
        (same[j].astype(F32) + far[j].astype(F32)).astype(BF) for j in range(1, far.shape[0])
    ]


def column_slice(weight, index, width):
    return lax.dynamic_slice_in_dim(weight, index * width, width, axis=1)


def local(
    tokens_in,
    doc_starts,
    attn_gain,
    query_weight,
    key_weight,
    value_weight,
    output_weight,
    ffn_gain,
    gate_weight,
    up_weight,
    down_weight,
    out_cotangent,
):
    n = lax.axis_size("ctx")
    depth = lax.axis_size("fsdp")
    tokens, width = tokens_in.shape[1:]
    query_width, key_width = query_weight.shape[1], key_weight.shape[1]
    qc, kc, dc = query_width // n, key_width // n, width // n
    rows = query_weight.shape[0]
    hidden_units = gate_weight.shape[1]
    fc = hidden_units // n
    down_rows = down_weight.shape[0] // n
    per_row = width // fc
    operands = (
        tokens_in, doc_starts, attn_gain, query_weight, key_weight, value_weight, output_weight,
        ffn_gain, gate_weight, up_weight, down_weight, out_cotangent,
    )
    if n > 8 or tokens != LANES or any(size % 16 for size in (qc, kc, dc, rows, down_rows)):
        return local_gathered(*operands)
    half = n // 2
    me = lax.axis_index("ctx")
    level = lax.axis_index("fsdp")
    me_1, level_1 = me[None], level[None]
    x, g = tokens_in[0], out_cotangent[0]

    x_same = gather_chips(x, n)
    x_blocks = x_same + [hop(after(block, x_same[1]), "ctx", 1) for block in x_same]

    columns = jnp.concatenate(
        [
            column_slice(query_weight, me, qc),
            column_slice(key_weight, me, kc),
            column_slice(value_weight, me, kc),
            column_slice(output_weight, me, dc),
        ],
        axis=1,
    )
    gain_rows = jnp.pad(
        jnp.stack([attn_gain, ffn_gain]), ((0, 14), (0, columns.shape[1] - rows))
    )
    first = jnp.concatenate([columns, gain_rows], axis=0)
    first_pieces = [first] + [hop(first, "fsdp", k) for k in range(1, depth)]
    down_piece = lax.dynamic_slice_in_dim(down_weight, me * down_rows, down_rows, axis=0)
    shard = jnp.concatenate(
        [
            column_slice(gate_weight, me, fc),
            column_slice(up_weight, me, fc),
            jnp.concatenate(
                [down_piece[:, fc * i : fc * (i + 1)] for i in range(per_row)], axis=0
            ),
        ],
        axis=1,
    )
    ffn_weights = lax.all_gather(after(shard, *first_pieces[1:], *x_blocks[1:half]), "fsdp", axis=0, tiled=True)

    devices = jnp.asarray(np.array(relative_ids(n), np.int32)) ^ me
    row_ids = (devices[:, None] * tokens + jnp.arange(tokens, dtype=jnp.int32)[None, :]).reshape(1, -1)
    positions = stored_position(row_ids, tokens, n)
    starts = doc_starts[0][:, None]
    begins = jnp.max(jnp.where(starts <= positions, starts, 0), axis=0, keepdims=True)
    inv_freq = jnp.exp(-math.log(BASE) * 2.0 * jnp.arange(HALF, dtype=F32) / HEAD_SIZE)
    angles = inv_freq[:, None] * (positions - begins).astype(F32)
    cosine, sine = jnp.cos(angles), jnp.sin(angles)

    normed_in, weight_t, out_t_own, gains, *messages = project(
        level_1, x_blocks, first_pieces, n, depth, qc, kc
    )
    same = [messages[0]] + [hop(messages[j], "ctx", 2 * j) for j in range(1, half)]
    other = [hop(message, "ctx", 1) for message in same]
    g_blocks = gather_blocks(after(g, x_blocks[half - 1]), n)
    attended, att, lse, q_rot, k_rot, v_low = attention_forward(
        me_1, after(doc_starts, *g_blocks[:half]), same, other, cosine, sine,
        n, query_width, key_width,
    )

    out_same = [out_t_own] + [
        hop(after(out_t_own, same[1]), "ctx", 2 * j) for j in range(1, half)
    ]
    out_other = [hop(after(piece, attended), "ctx", 1) for piece in out_same]
    share = n // depth
    downs = []
    for t in range(depth):
        chunk = lax.dynamic_slice(
            ffn_weights, (((me % depth) ^ t) * rows, 2 * fc), (rows, fc)
        )
        downs.append(
            lax.ppermute(
                chunk, "ctx", [(i, ((i % depth) ^ t) * share + i // depth) for i in range(n)]
            )
        )

    a_same = [attended] + [hop(attended, "ctx", 2 * j) for j in range(1, half)]
    a_blocks = a_same + [hop(after(block, *downs), "ctx", 1) for block in a_same]
    d_same, d_other, y_same, y_other, ffn_in, act, d_gate_up, gain_part, hidden = feed_forward(
        me_1, out_same + out_other, downs, ffn_weights, gains, x_blocks, a_blocks, g_blocks, n, depth
    )
    d_far = hop(d_other, "ctx", 1)
    d_pairs = pair_sums(d_same, d_far)
    gate_up_grad, *packed = ffn_grads(
        me_1, after(ffn_in, *d_pairs), act, d_gate_up, g_blocks, n
    )
    sums = [d_same[0], d_far]
    for j in range(1, half):
        sums.append(hop(d_pairs[j - 1], "ctx", 2 * j))
    gate_up_sum = lax.psum_scatter(gate_up_grad, "fsdp", scatter_dimension=0, tiled=True)
    y_far = hop(y_other, "ctx", 1)
    y_pairs = [jnp.pad(block, ((0, 16), (0, 0))) for block in pair_sums(y_same, y_far)]

    d_hidden, own_messages, *other_messages = attention_backward(
        me_1, after(doc_starts, *packed, *y_pairs), sums, g, hidden, gains, out_same + out_other,
        (q_rot, k_rot, v_low, att, lse), cosine, sine, n,
    )

    packed = [packed[0]] + [
        hop(after(packed[j], *sums[2:]), "ctx", 2 * j) for j in range(1, half)
    ]
    y_sums = [y_same, y_far] + [
        hop(after(y_pairs[j - 1], packed[0], *sums[2:]), "ctx", 2 * j)
        for j in range(1, min(half, 3))
    ]
    down_far = [hop(after(piece, d_hidden, *y_sums[2:]), "ctx", 1) for piece in packed]
    onward = pair(
        after(own_messages, *down_far), [hop(m, "ctx", 1) for m in other_messages], 2 * kc * n
    )
    down_pieces = unpack_down(me_1, level_1, packed, down_far, n, depth)
    onward = [after(block, down_pieces[0]) for block in onward]
    down_terms = [down_pieces[0]] + [hop(down_pieces[k], "fsdp", k) for k in range(1, depth)]
    normed_in = after(normed_in, *down_terms[1:])

    got = [onward[0]] + [hop(onward[j], "ctx", 2 * j) for j in range(1, half)]
    rest = input_grads(
        level_1, got, a_blocks, x_blocks, normed_in, weight_t, gain_part, n, depth, qc, kc, dc
    )
    n_other, n_same, level_pieces = rest[0], rest[1 : half + 1], rest[half + 1 :]
    pieces = sum_levels(level_pieces)
    n_far = hop(n_other, "ctx", 1)
    n_pairs = [
        (n_same[j].astype(F32) + n_far[j].astype(F32)).astype(BF) for j in range(1, half)
    ]
    n_sums = [n_same[0], n_far]
    for j in range(1, half):
        sent = after(n_pairs[j - 1], n_sums[2], gate_up_sum) if j == 3 else n_pairs[j - 1]
        n_sums.append(hop(sent, "ctx", 2 * j))
    y_sums += [hop(after(y_pairs[j - 1], n_sums[2]), "ctx", 2 * j) for j in range(3, half)]
    cuts = [0, qc, qc + kc, qc + 2 * kc, qc + 2 * kc + dc]
    (
        layer_out, tokens_grad, down_sum, gate_grad, up_grad,
        query_grad, key_grad, value_grad, output_grad,
    ) = finish(n_sums, y_sums, pieces, down_terms, gate_up_sum, hidden, d_hidden, x, gains, cuts)
    gain_rows = sum(piece[rows : rows + 2].astype(F32) for piece in after(pieces, *n_sums[2:]))
    gain_rows = gain_rows + hop(gain_rows, "ctx", 1)
    gain_rows = gain_rows + sum(
        after(hop(gain_rows, "ctx", 2 * j), tokens_grad) for j in range(1, half)
    )
    gain_own = gain_rows[:2, :rows]
    return (
        layer_out[None],
        tokens_grad[None],
        gain_own[0],
        query_grad.T,
        key_grad.T,
        value_grad.T,
        output_grad.T,
        gain_own[1],
        gate_grad,
        up_grad,
        down_sum.T,
    )


def rotate_half(values, cosine_table, sine_table, heads, forward):
    count = values.shape[0]
    half = HEAD_SIZE // 2
    shaped = values.reshape(count, heads, HEAD_SIZE)
    first_half = shaped[..., :half]
    second_half = shaped[..., half:]
    cos_rows = cosine_table[:, None, :]
    sin_rows = sine_table[:, None, :]
    if forward:
        lower = first_half * cos_rows - second_half * sin_rows
        upper = second_half * cos_rows + first_half * sin_rows
    else:
        lower = first_half * cos_rows + second_half * sin_rows
        upper = second_half * cos_rows - first_half * sin_rows
    return jnp.concatenate([lower, upper], axis=-1).reshape(count, heads * HEAD_SIZE)


def local_gathered(
    tokens_in,
    doc_starts,
    attn_gain,
    query_weight,
    key_weight,
    value_weight,
    output_weight,
    ffn_gain,
    gate_weight,
    up_weight,
    down_weight,
    out_cotangent,
):
    present_rows = tokens_in.shape[1]
    devices_ctx = lax.axis_size("ctx")
    group_size = QUERY_HEADS // KEY_VALUE_HEADS
    scale = HEAD_SIZE ** (-0.5)
    inputs_f = tokens_in[0].astype(jnp.float32)
    gain_one, query_full, key_full, value_full, output_full = (
        lax.all_gather(attn_gain, "fsdp", axis=0, tiled=True),
        lax.all_gather(query_weight, "fsdp", axis=0, tiled=True),
        lax.all_gather(key_weight, "fsdp", axis=0, tiled=True),
        lax.all_gather(value_weight, "fsdp", axis=0, tiled=True),
        lax.all_gather(output_weight, "fsdp", axis=0, tiled=True),
    )
    gain_one = gain_one.astype(jnp.float32)
    scale_one = rms_scale(inputs_f)
    normed_one = inputs_f * scale_one
    normalized_input = (normed_one * gain_one).astype(jnp.bfloat16)
    query_raw = jnp.dot(normalized_input, query_full, preferred_element_type=jnp.float32)
    key_unrotated = jnp.dot(normalized_input, key_full, preferred_element_type=jnp.float32)
    value_raw = jnp.dot(normalized_input, value_full, preferred_element_type=jnp.float32)
    local_rows = lax.axis_index("ctx") * present_rows + jnp.arange(present_rows, dtype=jnp.int32)
    token_pos = stored_position(local_rows, present_rows, devices_ctx)
    starts_row = doc_starts[0]
    doc_begin = jnp.max(
        jnp.where(starts_row[None, :] <= token_pos[:, None], starts_row[None, :], 0), axis=1
    )
    relative = (token_pos - doc_begin).astype(jnp.float32)
    inv_freq = jnp.exp(
        -math.log(BASE) * 2.0 * jnp.arange(HEAD_SIZE // 2, dtype=jnp.float32) / HEAD_SIZE
    )
    angles = relative[:, None] * inv_freq[None, :]
    cosine_table = jnp.cos(angles)
    sine_table = jnp.sin(angles)
    rotated_queries = rotate_half(query_raw, cosine_table, sine_table, QUERY_HEADS, True).astype(
        jnp.bfloat16
    )
    rotated_keys = rotate_half(
        key_unrotated, cosine_table, sine_table, KEY_VALUE_HEADS, True
    ).astype(jnp.bfloat16)
    reduced_values = value_raw.astype(jnp.bfloat16)
    key_gathered, value_gathered = (
        lax.all_gather(rotated_keys, "ctx", axis=0, tiled=True),
        lax.all_gather(reduced_values, "ctx", axis=0, tiled=True),
    )
    stream_len = key_gathered.shape[0]
    block_index = min(512, stream_len)
    block_count = stream_len // block_index
    key_block_list = key_gathered.reshape(block_count, block_index, KEY_VALUE_HEADS, HEAD_SIZE)
    value_block_list = value_gathered.reshape(block_count, block_index, KEY_VALUE_HEADS, HEAD_SIZE)
    key_positions = stored_position(
        jnp.arange(stream_len, dtype=jnp.int32), present_rows, devices_ctx
    )
    position_blocks = key_positions.reshape(block_count, block_index)
    grouped_queries = rotated_queries.reshape(present_rows, KEY_VALUE_HEADS, group_size, HEAD_SIZE)

    def scores_of(key_block, key_pos):
        raw = jnp.einsum(
            "tkgd,skd->kgts", grouped_queries, key_block, preferred_element_type=jnp.float32
        )
        visible = (key_pos[None, :] >= doc_begin[:, None]) & (
            key_pos[None, :] <= token_pos[:, None]
        )
        return (jnp.where(visible[None, None], raw * scale, NEGATIVE_FILL), visible)

    def stats_step(carry, items):
        running_max, running_sum = carry
        key_block, key_pos = items
        scores, visible = scores_of(key_block, key_pos)
        new_max = jnp.maximum(running_max, jnp.max(scores, axis=-1))
        weights = jnp.where(visible[None, None], jnp.exp(scores - new_max[..., None]), 0.0)
        running_sum = running_sum * jnp.exp(running_max - new_max) + jnp.sum(weights, axis=-1)
        return ((new_max, running_sum), None)

    stat_init = (
        jnp.full((KEY_VALUE_HEADS, group_size, present_rows), NEGATIVE_FILL, jnp.float32),
        jnp.zeros((KEY_VALUE_HEADS, group_size, present_rows), jnp.float32),
    )
    (row_max, row_sum), unused = lax.scan(stats_step, stat_init, (key_block_list, position_blocks))
    log_total = row_max + jnp.log(row_sum)

    def probs_of(key_block, key_pos):
        scores, visible = scores_of(key_block, key_pos)
        return jnp.where(visible[None, None], jnp.exp(scores - log_total[..., None]), 0.0)

    def value_step(carry, items):
        key_block, value_block, key_pos = items
        probs_low = probs_of(key_block, key_pos).astype(jnp.bfloat16)
        return (
            carry
            + jnp.einsum(
                "kgts,skd->tkgd", probs_low, value_block, preferred_element_type=jnp.float32
            ),
            None,
        )

    attn_rows, unused = lax.scan(
        value_step,
        jnp.zeros((present_rows, KEY_VALUE_HEADS, group_size, HEAD_SIZE), jnp.float32),
        (key_block_list, value_block_list, position_blocks),
    )
    query_width = rotated_queries.shape[1]
    attended_low = attn_rows.reshape(present_rows, query_width).astype(jnp.bfloat16)
    hidden_in = inputs_f + jnp.dot(attended_low, output_full, preferred_element_type=jnp.float32)
    gain_two, gate_full, up_full, down_full = (
        lax.all_gather(ffn_gain, "fsdp", axis=0, tiled=True),
        lax.all_gather(gate_weight, "fsdp", axis=0, tiled=True),
        lax.all_gather(up_weight, "fsdp", axis=0, tiled=True),
        lax.all_gather(down_weight, "fsdp", axis=0, tiled=True),
    )
    gain_two = gain_two.astype(jnp.float32)
    scale_two = rms_scale(hidden_in)
    normed_two = hidden_in * scale_two
    ffn_in = (normed_two * gain_two).astype(jnp.bfloat16)
    gate = jnp.dot(ffn_in, gate_full, preferred_element_type=jnp.float32)
    upper = jnp.dot(ffn_in, up_full, preferred_element_type=jnp.float32)
    sigma = jax.nn.sigmoid(gate)
    act_low = (gate * sigma * upper).astype(jnp.bfloat16)
    layer_out = (
        hidden_in + jnp.dot(act_low, down_full, preferred_element_type=jnp.float32)
    ).astype(jnp.bfloat16)
    cot_rows = out_cotangent[0]
    cot_f = cot_rows.astype(jnp.float32)
    down_local = jnp.dot(act_low.T, cot_rows, preferred_element_type=jnp.float32)
    d_act = jnp.dot(cot_rows, down_full.T, preferred_element_type=jnp.float32)
    d_gate = (d_act * upper * sigma * (1.0 + gate * (1.0 - sigma))).astype(jnp.bfloat16)
    d_up = (d_act * gate * sigma).astype(jnp.bfloat16)
    gate_local = jnp.dot(ffn_in.T, d_gate, preferred_element_type=jnp.float32)
    up_local = jnp.dot(ffn_in.T, d_up, preferred_element_type=jnp.float32)
    d_ffn_in = jnp.dot(d_gate, gate_full.T, preferred_element_type=jnp.float32) + jnp.dot(
        d_up, up_full.T, preferred_element_type=jnp.float32
    )
    gain_two_local = jnp.sum(d_ffn_in * normed_two, axis=0)
    scaled_two = d_ffn_in * gain_two
    d_hidden = cot_f + scale_two * (
        scaled_two - normed_two * jnp.mean(scaled_two * normed_two, axis=-1, keepdims=True)
    )
    d_branch = d_hidden.astype(jnp.bfloat16)
    output_local = jnp.dot(attended_low.T, d_branch, preferred_element_type=jnp.float32)
    attended_gradient = jnp.dot(d_branch, output_full.T, preferred_element_type=jnp.float32).astype(
        jnp.bfloat16
    )
    grouped_output_gradient = attended_gradient.reshape(
        present_rows, KEY_VALUE_HEADS, group_size, HEAD_SIZE
    )
    delta = jnp.einsum("tkgd,tkgd->kgt", grouped_output_gradient.astype(jnp.float32), attn_rows)

    def grad_step(carry, items):
        key_block, value_block, key_pos = items
        probs = probs_of(key_block, key_pos)
        d_probs = jnp.einsum(
            "tkgd,skd->kgts",
            grouped_output_gradient,
            value_block,
            preferred_element_type=jnp.float32,
        )
        d_score = (probs * (d_probs - delta[..., None]) * scale).astype(jnp.bfloat16)
        carry = carry + jnp.einsum(
            "kgts,skd->tkgd", d_score, key_block, preferred_element_type=jnp.float32
        )
        d_key_block = jnp.einsum(
            "kgts,tkgd->skd", d_score, grouped_queries, preferred_element_type=jnp.float32
        )
        d_value_block = jnp.einsum(
            "kgts,tkgd->skd",
            probs.astype(jnp.bfloat16),
            grouped_output_gradient,
            preferred_element_type=jnp.float32,
        )
        return (carry, (d_key_block, d_value_block))

    d_query_rot, (d_key_parts, d_value_parts) = lax.scan(
        grad_step,
        jnp.zeros((present_rows, KEY_VALUE_HEADS, group_size, HEAD_SIZE), jnp.float32),
        (key_block_list, value_block_list, position_blocks),
    )
    key_width = rotated_keys.shape[1]
    d_key_all = d_key_parts.reshape(stream_len, key_width)
    d_value_all = d_value_parts.reshape(stream_len, key_width)
    rotated_key_gradient, d_value = (
        lax.psum_scatter(d_key_all, "ctx", scatter_dimension=0, tiled=True),
        lax.psum_scatter(d_value_all, "ctx", scatter_dimension=0, tiled=True),
    )
    d_query = rotate_half(
        d_query_rot.reshape(present_rows, query_width), cosine_table, sine_table, QUERY_HEADS, False
    ).astype(jnp.bfloat16)
    key_gradient = rotate_half(
        rotated_key_gradient, cosine_table, sine_table, KEY_VALUE_HEADS, False
    ).astype(jnp.bfloat16)
    d_value_low = d_value.astype(jnp.bfloat16)
    query_local = jnp.dot(normalized_input.T, d_query, preferred_element_type=jnp.float32)
    key_local = jnp.dot(normalized_input.T, key_gradient, preferred_element_type=jnp.float32)
    value_local = jnp.dot(normalized_input.T, d_value_low, preferred_element_type=jnp.float32)
    d_normed = (
        jnp.dot(d_query, query_full.T, preferred_element_type=jnp.float32)
        + jnp.dot(key_gradient, key_full.T, preferred_element_type=jnp.float32)
        + jnp.dot(d_value_low, value_full.T, preferred_element_type=jnp.float32)
    )
    gain_one_local = jnp.sum(d_normed * normed_one, axis=0)
    scaled_one = d_normed * gain_one
    tokens_grad = d_hidden + scale_one * (
        scaled_one - normed_one * jnp.mean(scaled_one * normed_one, axis=-1, keepdims=True)
    )
    column_sums = (
        lax.psum_scatter(query_local, "ctx", scatter_dimension=1, tiled=True),
        lax.psum_scatter(key_local, "ctx", scatter_dimension=1, tiled=True),
        lax.psum_scatter(value_local, "ctx", scatter_dimension=1, tiled=True),
        lax.psum_scatter(output_local, "ctx", scatter_dimension=1, tiled=True),
        lax.psum_scatter(gate_local, "ctx", scatter_dimension=1, tiled=True),
        lax.psum_scatter(up_local, "ctx", scatter_dimension=1, tiled=True),
        lax.psum_scatter(down_local, "ctx", scatter_dimension=1, tiled=True),
    )
    gain_totals = lax.psum((gain_one_local, gain_two_local), "ctx")
    finals = (
        lax.psum_scatter(
            gain_totals[0].astype(jnp.bfloat16), "fsdp", scatter_dimension=0, tiled=True
        ).astype(jnp.float32),
        lax.psum_scatter(
            column_sums[0].astype(jnp.bfloat16), "fsdp", scatter_dimension=0, tiled=True
        ).astype(jnp.float32),
        lax.psum_scatter(
            column_sums[1].astype(jnp.bfloat16), "fsdp", scatter_dimension=0, tiled=True
        ).astype(jnp.float32),
        lax.psum_scatter(
            column_sums[2].astype(jnp.bfloat16), "fsdp", scatter_dimension=0, tiled=True
        ).astype(jnp.float32),
        lax.psum_scatter(
            column_sums[3].astype(jnp.bfloat16), "fsdp", scatter_dimension=0, tiled=True
        ).astype(jnp.float32),
        lax.psum_scatter(
            gain_totals[1].astype(jnp.bfloat16), "fsdp", scatter_dimension=0, tiled=True
        ).astype(jnp.float32),
        lax.psum_scatter(
            column_sums[4].astype(jnp.bfloat16), "fsdp", scatter_dimension=0, tiled=True
        ).astype(jnp.float32),
        lax.psum_scatter(
            column_sums[5].astype(jnp.bfloat16), "fsdp", scatter_dimension=0, tiled=True
        ).astype(jnp.float32),
        lax.psum_scatter(
            column_sums[6].astype(jnp.bfloat16), "fsdp", scatter_dimension=0, tiled=True
        ).astype(jnp.float32),
    )
    gain_one_grad = finals[0]
    gain_two_grad = finals[5]
    matrices = (finals[1], finals[2], finals[3], finals[4], finals[6], finals[7], finals[8])
    return (
        layer_out[None],
        tokens_grad.astype(jnp.bfloat16)[None],
        gain_one_grad,
        matrices[0],
        matrices[1],
        matrices[2],
        matrices[3],
        gain_two_grad,
        matrices[4],
        matrices[5],
        matrices[6],
    )


def solution(mesh):
    return jax.shard_map(
        local,
        mesh=mesh,
        in_specs=(
            P("fsdp", "ctx", None),
            P("fsdp", None),
            P("fsdp"),
            P("fsdp", None),
            P("fsdp", None),
            P("fsdp", None),
            P("fsdp", None),
            P("fsdp"),
            P("fsdp", None),
            P("fsdp", None),
            P("fsdp", None),
            P("fsdp", "ctx", None),
        ),
        out_specs=(
            P("fsdp", "ctx", None),
            P("fsdp", "ctx", None),
            P("fsdp"),
            P("fsdp", "ctx"),
            P("fsdp", "ctx"),
            P("fsdp", "ctx"),
            P("fsdp", "ctx"),
            P("fsdp"),
            P("fsdp", "ctx"),
            P("fsdp", "ctx"),
            P("fsdp", "ctx"),
        ),
        check_vma=False,
    )
```

```python
import math

import jax
import jax.numpy as jnp
import numpy as np
from jax import lax
from jax.experimental import pallas as pl
from jax.experimental.pallas import tpu as pltpu
from jax.sharding import PartitionSpec as P

QUERY_HEADS = 18
KEY_VALUE_HEADS = 6
HEAD_SIZE = 64
GROUP = QUERY_HEADS // KEY_VALUE_HEADS
HALF = HEAD_SIZE // 2
LANES = 128

EPS = 1e-05
BASE = 10000.0
NEGATIVE_FILL = -1e30
BF = jnp.bfloat16
F32 = jnp.float32
MIB = 1024 * 1024


def dot(left, right, left_dim, right_dim):
    return lax.dot_general(
        left, right, (((left_dim,), (right_dim,)), ((), ())), preferred_element_type=F32
    )


def rms_scale(values):
    return lax.rsqrt(jnp.mean(values * values, axis=-1, keepdims=True) + EPS)


def stored_position(row_ids, rows_per_dev, devices_ctx):
    half_len = rows_per_dev // 2
    owner_dev = row_ids // rows_per_dev
    offset_in = row_ids % rows_per_dev
    early = owner_dev * half_len + offset_in
    later = (2 * devices_ctx - 1 - owner_dev) * half_len + offset_in - half_len
    return jnp.where(offset_in < half_len, early, later)


def relative_ids(n):
    return [2 * j + k for k in range(2) for j in range(n // 2)]


def moved_block(n, i, b):
    rel = relative_ids(n)
    return rel.index(rel[b] ^ rel[i])


def hop(value, axis, bits):
    n = lax.axis_size(axis)
    return lax.ppermute(value, axis, [(i, i ^ bits) for i in range(n)])


def after(value, *others):
    return lax.optimization_barrier((value, *others))[0]


def gather_blocks(value, n):
    same = [value] + [hop(value, "ctx", 2 * j) for j in range(1, n // 2)]
    return same + [hop(block, "ctx", 1) for block in same]


def gather_chips(value, n):
    blocks = [value]
    for j in range(1, n // 2):
        sent = after(value, blocks[1]) if j == 3 else value
        blocks.append(hop(sent, "ctx", 2 * j))
    return blocks


def aligned(index, size):
    return pl.ds(pl.multiple_of(index * size, 16), size)


def turn(values, cosine, sine, sign):
    pieces = []
    for at in range(0, values.shape[0], HEAD_SIZE):
        first = values[at : at + HALF]
        second = values[at + HALF : at + HEAD_SIZE]
        pieces.append(first * cosine - sign * (second * sine))
        pieces.append(second * cosine + sign * (first * sine))
    return jnp.concatenate(pieces, axis=0)


def head_rows(h, g):
    return slice(HEAD_SIZE * (GROUP * h + g), HEAD_SIZE * (GROUP * h + g + 1))


def group_columns(ref, h):
    return jnp.concatenate([ref[head_rows(h, g), :] for g in range(GROUP)], axis=1)


def mask_bias(me, starts_ref, n, tokens):
    shape = (tokens, tokens)
    half_len = tokens // 2

    def position(device, offset):
        early = device * half_len + offset
        return jnp.where(offset < half_len, early, (2 * n - 2 - device) * half_len + offset)

    q_pos = position(me, lax.broadcasted_iota(jnp.int32, shape, 1))
    begin = jnp.zeros(shape, jnp.int32)
    for d in range(starts_ref.shape[1]):
        start = starts_ref[0, d]
        begin = jnp.where(q_pos >= start, jnp.maximum(begin, start), begin)
    blocks = []
    for bits in relative_ids(n):
        k_pos = position(me ^ bits, lax.broadcasted_iota(jnp.int32, shape, 0))
        visible = (k_pos >= begin) & (k_pos <= q_pos)
        blocks.append(jnp.where(visible, 0.0, NEGATIVE_FILL).astype(F32))
    return jnp.concatenate(blocks, axis=0)


SMEM = pl.BlockSpec(memory_space=pltpu.SMEM)


def kernel_call(body, name, outs, args, scratch=(), scalars=0, limit=60):
    shapes = [jax.ShapeDtypeStruct(shape, dtype) for shape, dtype in outs]

    def whole(value):
        return pl.BlockSpec(value.shape, lambda g: (0,) * len(value.shape))

    return pl.pallas_call(
        body,
        grid=(1,),
        in_specs=[SMEM] * scalars + [whole(a) for a in args[scalars:]],
        out_specs=[whole(s) for s in shapes],
        out_shape=shapes,
        scratch_shapes=[pltpu.VMEM(shape, dtype) for shape, dtype in scratch],
        compiler_params=pltpu.CompilerParams(vmem_limit_bytes=limit * MIB),
        cost_estimate=pl.CostEstimate(flops=1, bytes_accessed=1, transcendentals=0),
        name=name,
    )(*args)


def project_kernel(level_ref, *refs, n, depth, cols):
    qc, kc = cols
    half = n // 2
    x_refs, w_refs = refs[:n], refs[n : n + depth]
    weight_t_ref, out_t_ref, gains_ref = refs[n + depth : n + depth + 3]
    message_refs = refs[n + depth + 3 : n + depth + 3 + half]
    weight_ref, raw_ref, row_ref = refs[n + depth + 3 + half :]
    rows = row_ref.shape[2]
    tokens = x_refs[0].shape[0]
    width = qc + 2 * kc
    for k in range(depth):
        weight_ref[aligned(level_ref[0] ^ k, rows), :] = w_refs[k][:rows, :]
        row_ref[level_ref[0] ^ k] = w_refs[k][rows:, :rows].astype(F32)
    turned = weight_ref[...].astype(F32).T.astype(BF)
    weight_t_ref[...] = turned[:width]
    out_t_ref[...] = turned[width:]
    gains = jnp.concatenate([row_ref[t] for t in range(depth)], axis=1)
    gains_ref[...] = gains[:8]
    for i in range(n):
        values = x_refs[i][...].astype(F32)
        normed = (values * rms_scale(values) * gains[:1]).astype(BF)
        raw_ref[i] = dot(weight_t_ref[...], normed, 1, 1).astype(BF)
    for j in range(half):
        for b in range(n):
            message_refs[j][2 * kc * b : 2 * kc * (b + 1), :] = raw_ref[b, qc:, :]
        at = 2 * kc * n
        message_refs[j][at : at + qc, :] = raw_ref[j, :qc, :]
        message_refs[j][at + qc : at + 2 * qc, :] = raw_ref[half + j, :qc, :]


def project(level, x_blocks, w_pieces, n, depth, qc, kc):
    tokens, width = x_blocks[0].shape
    rows = width // depth
    cols = qc + 2 * kc
    spare = w_pieces[0].shape[0] - rows
    all_cols = w_pieces[0].shape[1]

    def body(*refs):
        project_kernel(*refs, n=n, depth=depth, cols=(qc, kc))

    return kernel_call(
        body,
        "project",
        [((cols, width), BF), ((all_cols - cols, width), BF), ((8, width), F32)]
        + [((2 * kc * n + 2 * qc, tokens), BF)] * (n // 2),
        [level, *x_blocks, *w_pieces],
        scratch=[((width, all_cols), BF), ((n, cols, tokens), BF), ((depth, spare, rows), F32)],
        scalars=1,
    )


def attention_forward_kernel(me_ref, starts_ref, *refs, n):
    half = n // 2
    same, other = refs[:half], refs[half:n]
    cos_ref, sin_ref = refs[n : n + 2]
    low_ref, att_ref, lse_ref, qrot_ref, krot_ref, v_ref = refs[n + 2 : n + 8]
    q_ref, k_ref, bias_ref = refs[n + 8 :]
    tokens = q_ref.shape[1]
    qc, kc = q_ref.shape[0] // n, k_ref.shape[0] // n
    rel = relative_ids(n)
    for i in range(n):
        device = me_ref[0] ^ rel[i]
        source = same[i] if i < half else other[i - half]
        at = 2 * kc * n + (0 if i < half else qc)
        q_ref[aligned(device, qc), :] = source[at : at + qc, :]
        to = aligned(device, kc)
        for b in range(n):
            start = 2 * kc * moved_block(n, i, b)
            lanes = slice(tokens * b, tokens * (b + 1))
            k_ref[to, lanes] = source[start : start + kc, :]
            v_ref[to, lanes] = source[start + kc : start + 2 * kc, :]
    bias_ref[...] = mask_bias(me_ref[0], starts_ref, n, tokens)
    for h in range(KEY_VALUE_HEADS):
        rows = slice(HEAD_SIZE * h, HEAD_SIZE * (h + 1))
        krot_ref[rows, :] = turn(k_ref[rows, :].astype(F32), cos_ref[...], sin_ref[...], 1.0).astype(BF)
        for g in range(GROUP):
            at = head_rows(h, g)
            turned = turn(
                q_ref[at, :].astype(F32), cos_ref[:, :tokens], sin_ref[:, :tokens], 1.0
            ).astype(BF)
            qrot_ref[at, :] = turned * BF(HEAD_SIZE**-0.5)
    for h in range(KEY_VALUE_HEADS):
        rows = slice(HEAD_SIZE * h, HEAD_SIZE * (h + 1))
        bias = jnp.concatenate([bias_ref[...]] * GROUP, axis=1)
        scores = dot(krot_ref[rows, :], group_columns(qrot_ref, h), 0, 0) + bias
        top = jnp.max(scores, axis=0, keepdims=True)
        weights = jnp.exp(scores - top)
        total = jnp.sum(weights, axis=0, keepdims=True)
        lse_ref[h : h + 1, :] = top + jnp.log(total)
        mixed = dot(v_ref[rows, :], weights.astype(BF), 1, 0) / total
        for g in range(GROUP):
            att_ref[head_rows(h, g), :] = mixed[:, tokens * g : tokens * (g + 1)]
    low_ref[...] = att_ref[...].T.astype(BF)


def attention_forward(me, starts, same, other, cosine, sine, n, query_width, key_width):
    tokens = same[0].shape[1]
    length = n * tokens

    def body(*refs):
        attention_forward_kernel(*refs, n=n)

    return kernel_call(
        body,
        "attention_forward",
        [
            ((tokens, query_width), BF),
            ((query_width, tokens), F32),
            ((KEY_VALUE_HEADS, GROUP * tokens), F32),
            ((query_width, tokens), BF),
            ((key_width, length), BF),
            ((key_width, length), BF),
        ],
        [me, starts, *same, *other, cosine, sine],
        scratch=[((query_width, tokens), BF), ((key_width, length), BF), ((length, tokens), F32)],
        scalars=2,
    )


def feed_forward_kernel(me_ref, *refs, n, depth):
    half = n // 2
    out_pieces, downs, (w_ref, gains_ref) = refs[:n], refs[n : n + depth], refs[n + depth : n + depth + 2]
    at = n + depth + 2
    x_refs, a_refs, g_refs = (refs[at + n * i : at + n * (i + 1)] for i in range(3))
    at += 3 * n
    d_same = refs[at : at + half]
    (
        d_other_ref, y_same_ref, y_other_ref, ffn_ref, act_ref, dgu_ref, part_ref, own_ref, wo_ref, wd_ref,
    ) = refs[at + half :]
    tokens, width = x_refs[0].shape
    fc = act_ref.shape[1]
    rel = relative_ids(n)
    for i in range(n):
        wo_ref[aligned(me_ref[0] ^ rel[i], out_pieces[i].shape[0]), :] = out_pieces[i][...]
    share, down_rows = n // depth, wd_ref.shape[0] // depth
    part = jnp.zeros((1, width), F32)
    for j in range(half):
        rows = slice(2 * tokens * j, 2 * tokens * (j + 1))
        values, attended = (
            jnp.concatenate([some[j][...], some[half + j][...]], axis=0) for some in (x_refs, a_refs)
        )
        hidden = values.astype(F32) + dot(attended, wo_ref[...], 1, 1)
        if j == 0:
            own_ref[...] = hidden[:tokens]
        normed = hidden * rms_scale(hidden)
        ffn_in = (normed * gains_ref[1:2, :]).astype(BF)
        ffn_ref[rows, :] = ffn_in
        gate = dot(ffn_in, w_ref[:, :fc], 1, 0)
        upper = dot(ffn_in, w_ref[:, fc : 2 * fc], 1, 0)
        if j == 0:
            for t in range(depth):
                to = aligned((me_ref[0] // share) ^ t, down_rows)
                for i in range(width // fc):
                    wd_ref[to, fc * i : fc * (i + 1)] = downs[t][down_rows * i : down_rows * (i + 1), :]
        cot = jnp.concatenate([g_refs[j][...], g_refs[half + j][...]], axis=0)
        d_act = dot(cot, wd_ref[...], 1, 1)
        sigma = jax.nn.sigmoid(gate)
        silu = gate * sigma
        act = (silu * upper).astype(BF)
        act_ref[rows, :] = act
        d_gate = (d_act * upper * sigma * (1.0 + gate * (1.0 - sigma))).astype(BF)
        d_up = (d_act * silu).astype(BF)
        dgu_ref[rows, :fc] = d_gate
        dgu_ref[rows, fc:] = d_up
        d_in = dot(d_gate, w_ref[:, :fc], 1, 1) + dot(d_up, w_ref[:, fc : 2 * fc], 1, 1)
        part = part + jnp.sum(d_in * normed, axis=0, keepdims=True)
        d_same[j][...] = d_in[:tokens].astype(BF)
        d_other_ref[j] = d_in[tokens:].astype(BF)
        out = dot(act, wd_ref[...], 1, 0)
        y_same_ref[j] = out[:tokens].astype(BF)
        y_other_ref[j] = out[tokens:].astype(BF)
    part_ref[...] = jnp.broadcast_to(part, part_ref.shape)


def feed_forward(me, out_pieces, downs, ffn_weights, gains, x_blocks, a_blocks, g_blocks, n, depth):
    tokens, width = x_blocks[0].shape
    fc = downs[0].shape[1]
    half, rows = n // 2, n * tokens
    by_chip = [some[side + j] for some in (x_blocks, a_blocks, g_blocks) for side in (0, half) for j in range(half)]

    def body(*refs):
        feed_forward_kernel(*refs, n=n, depth=depth)

    outs = kernel_call(
        body,
        "feed_forward",
        [((tokens, width), BF)] * half
        + [((half, tokens, width), BF)] * 3
        + [((rows, width), BF), ((rows, fc), BF), ((rows, 2 * fc), BF), ((8, width), F32)]
        + [((tokens, width), F32)],
        [me, *out_pieces, *downs, ffn_weights, gains, *by_chip],
        scratch=[((width, out_pieces[0].shape[1]), BF), ((fc, width), BF)],
        scalars=1,
    )
    return outs[:half], *outs[half:]


def ffn_grads_kernel(me_ref, *refs, n):
    half = n // 2
    ffn_ref, act_ref, dgu_ref = refs[:3]
    g_refs = refs[3 : 3 + n]
    gu_ref, packed_refs, down_ref = refs[3 + n], refs[4 + n : 4 + n + half], refs[4 + n + half]
    gu_ref[...] = dot(ffn_ref[...], dgu_ref[...], 0, 0).astype(BF)
    g_all = jnp.concatenate([g_refs[side + j][...] for j in range(half) for side in (0, half)], axis=0)
    down_ref[...] = dot(g_all, act_ref[...], 0, 0).astype(BF)
    dc = down_ref.shape[0] // n
    rel = relative_ids(n)
    for i in range(n):
        side = dc * (i // half)
        packed_refs[i % half][side : side + dc, :] = down_ref[aligned(me_ref[0] ^ rel[i], dc), :]


def ffn_grads(me, ffn, act, dgu, g_blocks, n):
    half = n // 2
    width, fc = ffn.shape[1], act.shape[1]
    dc = width // n

    def body(*refs):
        ffn_grads_kernel(*refs, n=n)

    return kernel_call(
        body,
        "ffn_grads",
        [((width, 2 * fc), BF)] + [((2 * dc, fc), BF)] * half,
        [me, ffn, act, dgu, *g_blocks],
        scratch=[((width, fc), BF)],
        scalars=1,
    )


def level_shapes(shape, depth):
    return [(shape, BF)] * (depth // 2) + [((depth // 2, *shape), BF)]


def store_level(refs, k, value):
    if k % 2:
        refs[-1][k // 2] = value
    else:
        refs[k // 2][...] = value


def sum_levels(pieces):
    near, far = pieces[:-1], pieces[-1]
    got = hop(far, "fsdp", 1)
    if len(near) == 1:
        return [near[0], got[0]]
    both = [(piece.astype(F32) + got[k].astype(F32)).astype(BF) for k, piece in enumerate(near)]
    return [both[0]] + [hop(both[k], "fsdp", 2 * k) for k in range(1, len(both))]


def unpack_down_kernel(me_ref, level_ref, *refs, n, depth):
    half = n // 2
    same, far = refs[:half], refs[half:n]
    grad_refs, grad_ref = refs[n:-1], refs[-1]
    dc = grad_ref.shape[1]
    share = n // depth
    fc = grad_ref.shape[2] // share
    for j in range(half):
        for side, piece in enumerate((same[j][:dc, :], far[j][dc:, :])):
            device = me_ref[0] ^ (2 * j + side)
            lanes = pl.ds(pl.multiple_of((device % share) * fc, LANES), fc)
            grad_ref[device // share, :, lanes] = piece
    for k in range(depth):
        grad_refs[k][...] = grad_ref[level_ref[0] ^ k]


def unpack_down(me, level, same, far, n, depth):
    rows, fc = same[0].shape

    def body(*refs):
        unpack_down_kernel(*refs, n=n, depth=depth)

    piece = (rows // 2, fc * n // depth)
    return kernel_call(
        body,
        "unpack_down",
        [(piece, BF)] * depth,
        [me, level, *same, *far],
        scratch=[((depth, *piece), BF)],
        scalars=2,
    )


def attention_backward_kernel(me_ref, starts_ref, *refs, n):
    half = n // 2
    sums = refs[: half + 1]
    (g_ref, hidden_ref, gains_ref, q_ref, k_ref, v_ref, att_ref, lse_ref, cos_ref, sin_ref) = refs[
        half + 1 : half + 11
    ]
    out_pieces = refs[half + 11 : half + 11 + n]
    dh_ref, same_ref = refs[half + 11 + n : half + 13 + n]
    other_refs = refs[half + 13 + n : n + n + 13]
    do_ref, db_ref, dq_ref, dk_ref, dv_ref, bias_ref, message_ref, wo_ref = refs[2 * n + 13 :]
    rel = relative_ids(n)
    bias_ref[...] = mask_bias(me_ref[0], starts_ref, n, q_ref.shape[1])
    tokens = q_ref.shape[1]
    d_in = sums[0][...].astype(F32) + sums[1][0].astype(F32)
    for r in sums[2:]:
        d_in = d_in + r[...].astype(F32)
    hidden = hidden_ref[...]
    scale = rms_scale(hidden)
    normed = hidden * scale
    scaled = d_in * gains_ref[1:2, :]
    d_hidden = g_ref[...].astype(F32) + scale * (
        scaled - normed * jnp.mean(scaled * normed, axis=-1, keepdims=True)
    )
    dh_ref[...] = d_hidden
    db_ref[...] = d_hidden.T.astype(BF)
    for i in range(n):
        wo_ref[aligned(me_ref[0] ^ rel[i], out_pieces[i].shape[0]), :] = out_pieces[i][...]
    do_ref[...] = dot(wo_ref[...], db_ref[...], 0, 0).astype(BF)
    for h in range(KEY_VALUE_HEADS):
        rows = slice(HEAD_SIZE * h, HEAD_SIZE * (h + 1))
        queries = group_columns(q_ref, h)
        grads = group_columns(do_ref, h)
        delta = jnp.sum(grads.astype(F32) * group_columns(att_ref, h), axis=0, keepdims=True)
        bias = jnp.concatenate([bias_ref[...]] * GROUP, axis=1)
        scores = dot(k_ref[rows, :], queries, 0, 0) + bias
        probs = jnp.exp(scores - lse_ref[h : h + 1, :])
        d_probs = dot(v_ref[rows, :], grads, 0, 0)
        d_score = (probs * (d_probs - delta)).astype(BF)
        d_query = dot(k_ref[rows, :], d_score, 1, 0) * (HEAD_SIZE**-0.5)
        for g in range(GROUP):
            dq_ref[head_rows(h, g), :] = turn(
                d_query[:, tokens * g : tokens * (g + 1)], cos_ref[:, :tokens], sin_ref[:, :tokens], -1.0
            ).astype(BF)
        d_key = dot(queries, d_score, 1, 1)
        dk_ref[rows, :] = turn(d_key, cos_ref[...], sin_ref[...], -1.0).astype(BF)
        dv_ref[rows, :] = dot(grads, probs.astype(BF), 1, 1).astype(BF)
    qc, dc, kc = dq_ref.shape[0] // n, db_ref.shape[0] // n, dk_ref.shape[0] // n
    flat = 2 * kc * n
    for i in (*range(half, n), *range(half)):
        if i == 0:
            for j in range(half):
                other_refs[j][...] = message_ref[j]
        device = me_ref[0] ^ rel[i]
        to = same_ref if i < half else message_ref
        j = i % half
        to[j, flat : flat + qc, :] = dq_ref[aligned(device, qc), :]
        to[j, flat + qc : flat + qc + dc, :] = db_ref[aligned(device, dc), :]
        at = aligned(device, kc)
        for b in range(n):
            start = 2 * kc * moved_block(n, i, b)
            lanes = slice(tokens * b, tokens * (b + 1))
            to[j, start : start + kc, :] = dk_ref[at, lanes]
            to[j, start + kc : start + 2 * kc, :] = dv_ref[at, lanes]


def attention_backward(me, starts, sums, g, hidden, gains, out_pieces, saved, cosine, sine, n):
    q_rot, k_rot, v_low, att, lse = saved
    query_width, tokens = q_rot.shape
    width = hidden.shape[1]
    key_width, length = k_rot.shape
    rows = 2 * key_width + (query_width + width) // n

    def body(*refs):
        attention_backward_kernel(*refs, n=n)

    return kernel_call(
        body,
        "attention_backward",
        [((tokens, width), F32), ((n // 2, rows, tokens), BF)] + [((rows, tokens), BF)] * (n // 2),
        [me, starts, *sums, g, hidden, gains, q_rot, k_rot, v_low, att, lse, cosine, sine, *out_pieces],
        scratch=[
            ((query_width, tokens), BF), ((width, tokens), BF), ((query_width, tokens), BF),
            ((key_width, length), BF), ((key_width, length), BF), ((length, tokens), F32),
            ((n // 2, rows, tokens), BF), ((width, query_width), BF),
        ],
        scalars=2,
    )


def pair_kernel(same_ref, *refs, flat):
    half, rows = same_ref.shape[:2]
    others, outs = refs[:half], refs[half:]
    more = rows - flat
    for j in reversed(range(half)):
        other = others[j][...]
        both = same_ref[j, :flat, :].astype(F32) + other[:flat].astype(F32)
        outs[j][:flat, :] = both.astype(BF)
        outs[j][flat : flat + more, :] = same_ref[j, flat:, :]
        outs[j][flat + more :, :] = other[flat:]


def pair(same, others, flat):
    half, rows, tokens = same.shape

    def body(*refs):
        pair_kernel(*refs, flat=flat)

    return kernel_call(
        body, "pair", [((2 * rows - flat, tokens), BF)] * half, [same, *others]
    )


def input_grads_kernel(level_ref, *refs, n, depth, cols):
    qc, kc, dc = cols
    half = n // 2
    got, a_refs, x_refs = refs[:half], refs[half : half + n], refs[half + n : half + 2 * n]
    gains_ref, weight_t_ref = refs[half + 2 * n : half + 2 * n + 2]
    at = half + 2 * n + 2
    part_two_ref, other_ref = refs[at : at + 2]
    same_refs = refs[at + 2 : at + 2 + half]
    level_refs = refs[at + 2 + half : -5]
    d_ref, b_ref, last_ref, row_ref, normed_ref = refs[-5:]
    tokens = x_refs[0].shape[0]
    flat = 2 * kc * n
    total = got[0][:flat, :].astype(F32)
    for r in got[1:]:
        total = total + r[:flat, :].astype(F32)
    total = total.astype(BF)
    for i in range(n):
        lanes = slice(tokens * i, tokens * (i + 1))
        start = flat + (qc + dc) * (i // half)
        source = got[i % half]
        d_ref[:qc, lanes] = source[start : start + qc, :]
        d_ref[qc:, lanes] = total[2 * kc * i : 2 * kc * (i + 1)]
        b_ref[:, lanes] = source[start + qc : start + qc + dc, :]
    width = x_refs[0].shape[1]
    part = jnp.zeros((1, width), F32)
    for i in (*range(half, n), *range(half)):
        lanes = slice(tokens * i, tokens * (i + 1))
        d_normed = dot(d_ref[:, lanes], weight_t_ref[...], 0, 0)
        values = x_refs[i][...].astype(F32)
        normed = values * rms_scale(values)
        part = part + jnp.sum(d_normed * normed, axis=0, keepdims=True)
        normed_ref[tokens * i : tokens * (i + 1), :] = (normed * gains_ref[:1, :]).astype(BF)
        if i < half:
            same_refs[i][...] = d_normed.astype(BF)
        else:
            other_ref[i - half] = d_normed.astype(BF)
    cut = qc + 2 * kc
    last_ref[:, :cut] = dot(normed_ref[...], d_ref[...], 0, 1).astype(BF)
    attended = jnp.concatenate([r[...] for r in a_refs], axis=0)
    last_ref[:, cut:] = dot(attended, b_ref[...], 0, 1).astype(BF)
    rows, wide = width // depth, row_ref.shape[2]
    both = jnp.concatenate([part, part_two_ref[:1, :], jnp.zeros((14, width), F32)], axis=0)
    for t in range(depth):
        row_ref[t, :, :rows] = both[:, rows * t : rows * (t + 1)]
        row_ref[t, :, rows:] = jnp.zeros((16, wide - rows), F32)
    for k in range(depth):
        piece = [last_ref[aligned(level_ref[0] ^ k, rows), :], row_ref[level_ref[0] ^ k].astype(BF)]
        store_level(level_refs, k, jnp.concatenate(piece, axis=0))


def input_grads(level, got, attended, x_blocks, gains, weight_t, part_two, n, depth, qc, kc, dc):
    half = n // 2
    tokens, width = x_blocks[0].shape
    length = n * tokens
    cols = qc + 2 * kc + dc

    def body(*refs):
        input_grads_kernel(*refs, n=n, depth=depth, cols=(qc, kc, dc))

    return kernel_call(
        body,
        "input_grads",
        [((half, tokens, width), BF)]
        + [((tokens, width), BF)] * half
        + level_shapes((width // depth + 16, cols), depth),
        [level, *got, *attended, *x_blocks, gains, weight_t, part_two],
        scratch=[
            ((qc + 2 * kc, length), BF), ((dc, length), BF), ((width, cols), BF), ((depth, 16, cols), F32),
            ((length, width), BF),
        ],
        scalars=1,
    )


def summed(parts, tokens):
    total = parts[0].astype(F32)
    for part in parts[1:]:
        total = total + part[:tokens].astype(F32)
    return total


def finish_kernel(*refs, half, terms, cuts):
    sums, y_sums = refs[: half + 1], refs[half + 1 : 2 * half + 2]
    at = 2 * half + 2
    pieces, downs = refs[at : at + terms[0]], refs[at + terms[0] : at + sum(terms)]
    at += sum(terms)
    gu_ref, hidden_ref, dh_ref, x_ref, gains_ref = refs[at : at + 5]
    y_ref, out_ref, down_ref, gate_ref, up_ref = refs[at + 5 : at + 10]
    fc = gate_ref.shape[1]
    gate_ref[...] = gu_ref[:, :fc].astype(F32)
    up_ref[...] = gu_ref[:, fc:].astype(F32)
    y_ref[...] = (
        hidden_ref[...]
        + summed([y_sums[0][0], y_sums[1][0], *(r[...] for r in y_sums[2:])], x_ref.shape[0])
    ).astype(BF)
    total = downs[0][...].astype(F32)
    for r in downs[1:]:
        total = total + r[...].astype(F32)
    down_ref[...] = total
    d_normed = summed([sums[0][...], sums[1][0], *(r[...] for r in sums[2:])], x_ref.shape[0])
    values = x_ref[...].astype(F32)
    scale = rms_scale(values)
    normed = values * scale
    scaled = d_normed * gains_ref[0:1, :]
    out_ref[...] = (
        dh_ref[...]
        + scale * (scaled - normed * jnp.mean(scaled * normed, axis=-1, keepdims=True))
    ).astype(BF)
    total = pieces[0][...].astype(F32)
    for r in pieces[1:]:
        total = total + r[...].astype(F32)
    turned = total[: total.shape[0] - 16].T
    for grad_ref, start, stop in zip(refs[at + 10 :], cuts[:-1], cuts[1:]):
        grad_ref[...] = turned[start:stop]


def finish(sums, y_sums, pieces, downs, gate_up, hidden, d_hidden, x, gains, cuts):
    height = pieces[0].shape[0]

    def body(*refs):
        finish_kernel(*refs, half=len(sums) - 1, terms=(len(pieces), len(downs)), cuts=cuts)

    return kernel_call(
        body,
        "finish",
        [(x.shape, BF), (x.shape, BF), (downs[0].shape, F32)]
        + [((gate_up.shape[0], gate_up.shape[1] // 2), F32)] * 2
        + [((stop - start, height - 16), F32) for start, stop in zip(cuts[:-1], cuts[1:])],
        [*sums, *y_sums, *pieces, *downs, gate_up, hidden, d_hidden, x, gains],
    )


def pair_sums(same, far):
    return [
        (same[j].astype(F32) + far[j].astype(F32)).astype(BF) for j in range(1, far.shape[0])
    ]


def column_slice(weight, index, width):
    return lax.dynamic_slice_in_dim(weight, index * width, width, axis=1)


def local(
    tokens_in,
    doc_starts,
    attn_gain,
    query_weight,
    key_weight,
    value_weight,
    output_weight,
    ffn_gain,
    gate_weight,
    up_weight,
    down_weight,
    out_cotangent,
):
    n = lax.axis_size("ctx")
    depth = lax.axis_size("fsdp")
    tokens, width = tokens_in.shape[1:]
    query_width, key_width = query_weight.shape[1], key_weight.shape[1]
    qc, kc, dc = query_width // n, key_width // n, width // n
    rows = query_weight.shape[0]
    hidden_units = gate_weight.shape[1]
    fc = hidden_units // n
    down_rows = down_weight.shape[0] // n
    per_row = width // fc
    operands = (
        tokens_in, doc_starts, attn_gain, query_weight, key_weight, value_weight, output_weight,
        ffn_gain, gate_weight, up_weight, down_weight, out_cotangent,
    )
    if n > 8 or tokens != LANES or any(size % 16 for size in (qc, kc, dc, rows, down_rows)):
        return local_gathered(*operands)
    half = n // 2
    me = lax.axis_index("ctx")
    level = lax.axis_index("fsdp")
    me_1, level_1 = me[None], level[None]
    x, g = tokens_in[0], out_cotangent[0]

    x_same = gather_chips(x, n)
    x_blocks = x_same + [hop(after(block, x_same[1]), "ctx", 1) for block in x_same]

    columns = jnp.concatenate(
        [
            column_slice(query_weight, me, qc),
            column_slice(key_weight, me, kc),
            column_slice(value_weight, me, kc),
            column_slice(output_weight, me, dc),
        ],
        axis=1,
    )
    gain_rows = jnp.pad(
        jnp.stack([attn_gain, ffn_gain]), ((0, 14), (0, columns.shape[1] - rows))
    )
    first = jnp.concatenate([columns, gain_rows], axis=0)
    first_pieces = [first] + [hop(first, "fsdp", k) for k in range(1, depth)]
    down_piece = lax.dynamic_slice_in_dim(down_weight, me * down_rows, down_rows, axis=0)
    shard = jnp.concatenate(
        [
            column_slice(gate_weight, me, fc),
            column_slice(up_weight, me, fc),
            jnp.concatenate(
                [down_piece[:, fc * i : fc * (i + 1)] for i in range(per_row)], axis=0
            ),
        ],
        axis=1,
    )
    ffn_weights = lax.all_gather(after(shard, *first_pieces[1:], *x_blocks[1:half]), "fsdp", axis=0, tiled=True)

    devices = jnp.asarray(np.array(relative_ids(n), np.int32)) ^ me
    row_ids = (devices[:, None] * tokens + jnp.arange(tokens, dtype=jnp.int32)[None, :]).reshape(1, -1)
    positions = stored_position(row_ids, tokens, n)
    starts = doc_starts[0][:, None]
    begins = jnp.max(jnp.where(starts <= positions, starts, 0), axis=0, keepdims=True)
    inv_freq = jnp.exp(-math.log(BASE) * 2.0 * jnp.arange(HALF, dtype=F32) / HEAD_SIZE)
    angles = inv_freq[:, None] * (positions - begins).astype(F32)
    cosine, sine = jnp.cos(angles), jnp.sin(angles)

    weight_t, out_t_own, gains, *messages = project(
        level_1, x_blocks, first_pieces, n, depth, qc, kc
    )
    same = [messages[0]] + [hop(messages[j], "ctx", 2 * j) for j in range(1, half)]
    other = [hop(message, "ctx", 1) for message in same]
    g_blocks = gather_blocks(after(g, x_blocks[half - 1]), n)
    attended, att, lse, q_rot, k_rot, v_low = attention_forward(
        me_1, after(doc_starts, *g_blocks[:half]), same, other, cosine, sine,
        n, query_width, key_width,
    )

    out_same = [out_t_own] + [
        hop(after(out_t_own, same[1]), "ctx", 2 * j) for j in range(1, half)
    ]
    out_other = [hop(after(piece, attended), "ctx", 1) for piece in out_same]
    share = n // depth
    downs = []
    for t in range(depth):
        chunk = lax.dynamic_slice(
            ffn_weights, (((me % depth) ^ t) * rows, 2 * fc), (rows, fc)
        )
        downs.append(
            lax.ppermute(
                after(chunk, *out_other), "ctx", [(i, ((i % depth) ^ t) * share + i // depth) for i in range(n)]
            )
        )

    a_same = [attended] + [hop(attended, "ctx", 2 * j) for j in range(1, half)]
    a_blocks = a_same + [hop(after(block, *downs), "ctx", 1) for block in a_same]
    d_same, d_other, y_same, y_other, ffn_in, act, d_gate_up, gain_part, hidden = feed_forward(
        me_1, out_same + out_other, downs, ffn_weights, gains, x_blocks, a_blocks, g_blocks, n, depth
    )
    d_far = hop(d_other, "ctx", 1)
    d_pairs = pair_sums(d_same, d_far)
    gate_up_grad, *packed = ffn_grads(
        me_1, after(ffn_in, *d_pairs), act, d_gate_up, g_blocks, n
    )
    sums = [d_same[0], d_far]
    for j in range(1, half):
        sums.append(hop(d_pairs[j - 1], "ctx", 2 * j))
    gate_up_sum = lax.psum_scatter(gate_up_grad, "fsdp", scatter_dimension=0, tiled=True)
    y_far = hop(y_other, "ctx", 1)
    y_pairs = [jnp.pad(block, ((0, 16), (0, 0))) for block in pair_sums(y_same, y_far)]

    d_hidden, own_messages, *other_messages = attention_backward(
        me_1, after(doc_starts, *packed, *y_pairs), sums, g, hidden, gains, out_same + out_other,
        (q_rot, k_rot, v_low, att, lse), cosine, sine, n,
    )

    packed = [packed[0]] + [
        hop(after(packed[j], *sums[2:]), "ctx", 2 * j) for j in range(1, half)
    ]
    y_sums = [y_same, y_far] + [
        hop(after(y_pairs[j - 1], packed[0], *sums[2:]), "ctx", 2 * j)
        for j in range(1, min(half, 3))
    ]
    down_far = [hop(after(piece, d_hidden, *y_sums[2:]), "ctx", 1) for piece in packed]
    onward = pair(
        after(own_messages, *down_far), [hop(m, "ctx", 1) for m in other_messages], 2 * kc * n
    )
    down_pieces = unpack_down(me_1, level_1, packed, down_far, n, depth)
    onward = [after(block, down_pieces[0]) for block in onward]
    down_terms = [down_pieces[0]] + [hop(down_pieces[k], "fsdp", k) for k in range(1, depth)]
    weight_t = after(weight_t, *down_terms[1:])

    got = [onward[0]] + [hop(onward[j], "ctx", 2 * j) for j in range(1, half)]
    rest = input_grads(
        level_1, got, a_blocks, x_blocks, gains, weight_t, gain_part, n, depth, qc, kc, dc
    )
    n_other, n_same, level_pieces = rest[0], rest[1 : half + 1], rest[half + 1 :]
    pieces = sum_levels(level_pieces)
    n_far = hop(n_other, "ctx", 1)
    n_pairs = [
        (n_same[j].astype(F32) + n_far[j].astype(F32)).astype(BF) for j in range(1, half)
    ]
    n_sums = [n_same[0], n_far]
    for j in range(1, half):
        sent = after(n_pairs[j - 1], n_sums[2], gate_up_sum) if j == 3 else n_pairs[j - 1]
        n_sums.append(hop(sent, "ctx", 2 * j))
    y_sums += [hop(after(y_pairs[j - 1], n_sums[2]), "ctx", 2 * j) for j in range(3, half)]
    cuts = [0, qc, qc + kc, qc + 2 * kc, qc + 2 * kc + dc]
    (
        layer_out, tokens_grad, down_sum, gate_grad, up_grad,
        query_grad, key_grad, value_grad, output_grad,
    ) = finish(n_sums, y_sums, pieces, down_terms, gate_up_sum, hidden, d_hidden, x, gains, cuts)
    gain_rows = sum(piece[rows : rows + 2].astype(F32) for piece in after(pieces, *n_sums[2:]))
    gain_rows = gain_rows + hop(gain_rows, "ctx", 1)
    gain_rows = gain_rows + sum(
        after(hop(gain_rows, "ctx", 2 * j), tokens_grad) for j in range(1, half)
    )
    gain_own = gain_rows[:2, :rows]
    return (
        layer_out[None],
        tokens_grad[None],
        gain_own[0],
        query_grad.T,
        key_grad.T,
        value_grad.T,
        output_grad.T,
        gain_own[1],
        gate_grad,
        up_grad,
        down_sum.T,
    )


def rotate_half(values, cosine_table, sine_table, heads, forward):
    count = values.shape[0]
    half = HEAD_SIZE // 2
    shaped = values.reshape(count, heads, HEAD_SIZE)
    first_half = shaped[..., :half]
    second_half = shaped[..., half:]
    cos_rows = cosine_table[:, None, :]
    sin_rows = sine_table[:, None, :]
    if forward:
        lower = first_half * cos_rows - second_half * sin_rows
        upper = second_half * cos_rows + first_half * sin_rows
    else:
        lower = first_half * cos_rows + second_half * sin_rows
        upper = second_half * cos_rows - first_half * sin_rows
    return jnp.concatenate([lower, upper], axis=-1).reshape(count, heads * HEAD_SIZE)


def local_gathered(
    tokens_in,
    doc_starts,
    attn_gain,
    query_weight,
    key_weight,
    value_weight,
    output_weight,
    ffn_gain,
    gate_weight,
    up_weight,
    down_weight,
    out_cotangent,
):
    present_rows = tokens_in.shape[1]
    devices_ctx = lax.axis_size("ctx")
    group_size = QUERY_HEADS // KEY_VALUE_HEADS
    scale = HEAD_SIZE ** (-0.5)
    inputs_f = tokens_in[0].astype(jnp.float32)
    gain_one, query_full, key_full, value_full, output_full = (
        lax.all_gather(attn_gain, "fsdp", axis=0, tiled=True),
        lax.all_gather(query_weight, "fsdp", axis=0, tiled=True),
        lax.all_gather(key_weight, "fsdp", axis=0, tiled=True),
        lax.all_gather(value_weight, "fsdp", axis=0, tiled=True),
        lax.all_gather(output_weight, "fsdp", axis=0, tiled=True),
    )
    gain_one = gain_one.astype(jnp.float32)
    scale_one = rms_scale(inputs_f)
    normed_one = inputs_f * scale_one
    normalized_input = (normed_one * gain_one).astype(jnp.bfloat16)
    query_raw = jnp.dot(normalized_input, query_full, preferred_element_type=jnp.float32)
    key_unrotated = jnp.dot(normalized_input, key_full, preferred_element_type=jnp.float32)
    value_raw = jnp.dot(normalized_input, value_full, preferred_element_type=jnp.float32)
    local_rows = lax.axis_index("ctx") * present_rows + jnp.arange(present_rows, dtype=jnp.int32)
    token_pos = stored_position(local_rows, present_rows, devices_ctx)
    starts_row = doc_starts[0]
    doc_begin = jnp.max(
        jnp.where(starts_row[None, :] <= token_pos[:, None], starts_row[None, :], 0), axis=1
    )
    relative = (token_pos - doc_begin).astype(jnp.float32)
    inv_freq = jnp.exp(
        -math.log(BASE) * 2.0 * jnp.arange(HEAD_SIZE // 2, dtype=jnp.float32) / HEAD_SIZE
    )
    angles = relative[:, None] * inv_freq[None, :]
    cosine_table = jnp.cos(angles)
    sine_table = jnp.sin(angles)
    rotated_queries = rotate_half(query_raw, cosine_table, sine_table, QUERY_HEADS, True).astype(
        jnp.bfloat16
    )
    rotated_keys = rotate_half(
        key_unrotated, cosine_table, sine_table, KEY_VALUE_HEADS, True
    ).astype(jnp.bfloat16)
    reduced_values = value_raw.astype(jnp.bfloat16)
    key_gathered, value_gathered = (
        lax.all_gather(rotated_keys, "ctx", axis=0, tiled=True),
        lax.all_gather(reduced_values, "ctx", axis=0, tiled=True),
    )
    stream_len = key_gathered.shape[0]
    block_index = min(512, stream_len)
    block_count = stream_len // block_index
    key_block_list = key_gathered.reshape(block_count, block_index, KEY_VALUE_HEADS, HEAD_SIZE)
    value_block_list = value_gathered.reshape(block_count, block_index, KEY_VALUE_HEADS, HEAD_SIZE)
    key_positions = stored_position(
        jnp.arange(stream_len, dtype=jnp.int32), present_rows, devices_ctx
    )
    position_blocks = key_positions.reshape(block_count, block_index)
    grouped_queries = rotated_queries.reshape(present_rows, KEY_VALUE_HEADS, group_size, HEAD_SIZE)

    def scores_of(key_block, key_pos):
        raw = jnp.einsum(
            "tkgd,skd->kgts", grouped_queries, key_block, preferred_element_type=jnp.float32
        )
        visible = (key_pos[None, :] >= doc_begin[:, None]) & (
            key_pos[None, :] <= token_pos[:, None]
        )
        return (jnp.where(visible[None, None], raw * scale, NEGATIVE_FILL), visible)

    def stats_step(carry, items):
        running_max, running_sum = carry
        key_block, key_pos = items
        scores, visible = scores_of(key_block, key_pos)
        new_max = jnp.maximum(running_max, jnp.max(scores, axis=-1))
        weights = jnp.where(visible[None, None], jnp.exp(scores - new_max[..., None]), 0.0)
        running_sum = running_sum * jnp.exp(running_max - new_max) + jnp.sum(weights, axis=-1)
        return ((new_max, running_sum), None)

    stat_init = (
        jnp.full((KEY_VALUE_HEADS, group_size, present_rows), NEGATIVE_FILL, jnp.float32),
        jnp.zeros((KEY_VALUE_HEADS, group_size, present_rows), jnp.float32),
    )
    (row_max, row_sum), unused = lax.scan(stats_step, stat_init, (key_block_list, position_blocks))
    log_total = row_max + jnp.log(row_sum)

    def probs_of(key_block, key_pos):
        scores, visible = scores_of(key_block, key_pos)
        return jnp.where(visible[None, None], jnp.exp(scores - log_total[..., None]), 0.0)

    def value_step(carry, items):
        key_block, value_block, key_pos = items
        probs_low = probs_of(key_block, key_pos).astype(jnp.bfloat16)
        return (
            carry
            + jnp.einsum(
                "kgts,skd->tkgd", probs_low, value_block, preferred_element_type=jnp.float32
            ),
            None,
        )

    attn_rows, unused = lax.scan(
        value_step,
        jnp.zeros((present_rows, KEY_VALUE_HEADS, group_size, HEAD_SIZE), jnp.float32),
        (key_block_list, value_block_list, position_blocks),
    )
    query_width = rotated_queries.shape[1]
    attended_low = attn_rows.reshape(present_rows, query_width).astype(jnp.bfloat16)
    hidden_in = inputs_f + jnp.dot(attended_low, output_full, preferred_element_type=jnp.float32)
    gain_two, gate_full, up_full, down_full = (
        lax.all_gather(ffn_gain, "fsdp", axis=0, tiled=True),
        lax.all_gather(gate_weight, "fsdp", axis=0, tiled=True),
        lax.all_gather(up_weight, "fsdp", axis=0, tiled=True),
        lax.all_gather(down_weight, "fsdp", axis=0, tiled=True),
    )
    gain_two = gain_two.astype(jnp.float32)
    scale_two = rms_scale(hidden_in)
    normed_two = hidden_in * scale_two
    ffn_in = (normed_two * gain_two).astype(jnp.bfloat16)
    gate = jnp.dot(ffn_in, gate_full, preferred_element_type=jnp.float32)
    upper = jnp.dot(ffn_in, up_full, preferred_element_type=jnp.float32)
    sigma = jax.nn.sigmoid(gate)
    act_low = (gate * sigma * upper).astype(jnp.bfloat16)
    layer_out = (
        hidden_in + jnp.dot(act_low, down_full, preferred_element_type=jnp.float32)
    ).astype(jnp.bfloat16)
    cot_rows = out_cotangent[0]
    cot_f = cot_rows.astype(jnp.float32)
    down_local = jnp.dot(act_low.T, cot_rows, preferred_element_type=jnp.float32)
    d_act = jnp.dot(cot_rows, down_full.T, preferred_element_type=jnp.float32)
    d_gate = (d_act * upper * sigma * (1.0 + gate * (1.0 - sigma))).astype(jnp.bfloat16)
    d_up = (d_act * gate * sigma).astype(jnp.bfloat16)
    gate_local = jnp.dot(ffn_in.T, d_gate, preferred_element_type=jnp.float32)
    up_local = jnp.dot(ffn_in.T, d_up, preferred_element_type=jnp.float32)
    d_ffn_in = jnp.dot(d_gate, gate_full.T, preferred_element_type=jnp.float32) + jnp.dot(
        d_up, up_full.T, preferred_element_type=jnp.float32
    )
    gain_two_local = jnp.sum(d_ffn_in * normed_two, axis=0)
    scaled_two = d_ffn_in * gain_two
    d_hidden = cot_f + scale_two * (
        scaled_two - normed_two * jnp.mean(scaled_two * normed_two, axis=-1, keepdims=True)
    )
    d_branch = d_hidden.astype(jnp.bfloat16)
    output_local = jnp.dot(attended_low.T, d_branch, preferred_element_type=jnp.float32)
    attended_gradient = jnp.dot(d_branch, output_full.T, preferred_element_type=jnp.float32).astype(
        jnp.bfloat16
    )
    grouped_output_gradient = attended_gradient.reshape(
        present_rows, KEY_VALUE_HEADS, group_size, HEAD_SIZE
    )
    delta = jnp.einsum("tkgd,tkgd->kgt", grouped_output_gradient.astype(jnp.float32), attn_rows)

    def grad_step(carry, items):
        key_block, value_block, key_pos = items
        probs = probs_of(key_block, key_pos)
        d_probs = jnp.einsum(
            "tkgd,skd->kgts",
            grouped_output_gradient,
            value_block,
            preferred_element_type=jnp.float32,
        )
        d_score = (probs * (d_probs - delta[..., None]) * scale).astype(jnp.bfloat16)
        carry = carry + jnp.einsum(
            "kgts,skd->tkgd", d_score, key_block, preferred_element_type=jnp.float32
        )
        d_key_block = jnp.einsum(
            "kgts,tkgd->skd", d_score, grouped_queries, preferred_element_type=jnp.float32
        )
        d_value_block = jnp.einsum(
            "kgts,tkgd->skd",
            probs.astype(jnp.bfloat16),
            grouped_output_gradient,
            preferred_element_type=jnp.float32,
        )
        return (carry, (d_key_block, d_value_block))

    d_query_rot, (d_key_parts, d_value_parts) = lax.scan(
        grad_step,
        jnp.zeros((present_rows, KEY_VALUE_HEADS, group_size, HEAD_SIZE), jnp.float32),
        (key_block_list, value_block_list, position_blocks),
    )
    key_width = rotated_keys.shape[1]
    d_key_all = d_key_parts.reshape(stream_len, key_width)
    d_value_all = d_value_parts.reshape(stream_len, key_width)
    rotated_key_gradient, d_value = (
        lax.psum_scatter(d_key_all, "ctx", scatter_dimension=0, tiled=True),
        lax.psum_scatter(d_value_all, "ctx", scatter_dimension=0, tiled=True),
    )
    d_query = rotate_half(
        d_query_rot.reshape(present_rows, query_width), cosine_table, sine_table, QUERY_HEADS, False
    ).astype(jnp.bfloat16)
    key_gradient = rotate_half(
        rotated_key_gradient, cosine_table, sine_table, KEY_VALUE_HEADS, False
    ).astype(jnp.bfloat16)
    d_value_low = d_value.astype(jnp.bfloat16)
    query_local = jnp.dot(normalized_input.T, d_query, preferred_element_type=jnp.float32)
    key_local = jnp.dot(normalized_input.T, key_gradient, preferred_element_type=jnp.float32)
    value_local = jnp.dot(normalized_input.T, d_value_low, preferred_element_type=jnp.float32)
    d_normed = (
        jnp.dot(d_query, query_full.T, preferred_element_type=jnp.float32)
        + jnp.dot(key_gradient, key_full.T, preferred_element_type=jnp.float32)
        + jnp.dot(d_value_low, value_full.T, preferred_element_type=jnp.float32)
    )
    gain_one_local = jnp.sum(d_normed * normed_one, axis=0)
    scaled_one = d_normed * gain_one
    tokens_grad = d_hidden + scale_one * (
        scaled_one - normed_one * jnp.mean(scaled_one * normed_one, axis=-1, keepdims=True)
    )
    column_sums = (
        lax.psum_scatter(query_local, "ctx", scatter_dimension=1, tiled=True),
        lax.psum_scatter(key_local, "ctx", scatter_dimension=1, tiled=True),
        lax.psum_scatter(value_local, "ctx", scatter_dimension=1, tiled=True),
        lax.psum_scatter(output_local, "ctx", scatter_dimension=1, tiled=True),
        lax.psum_scatter(gate_local, "ctx", scatter_dimension=1, tiled=True),
        lax.psum_scatter(up_local, "ctx", scatter_dimension=1, tiled=True),
        lax.psum_scatter(down_local, "ctx", scatter_dimension=1, tiled=True),
    )
    gain_totals = lax.psum((gain_one_local, gain_two_local), "ctx")
    finals = (
        lax.psum_scatter(
            gain_totals[0].astype(jnp.bfloat16), "fsdp", scatter_dimension=0, tiled=True
        ).astype(jnp.float32),
        lax.psum_scatter(
            column_sums[0].astype(jnp.bfloat16), "fsdp", scatter_dimension=0, tiled=True
        ).astype(jnp.float32),
        lax.psum_scatter(
            column_sums[1].astype(jnp.bfloat16), "fsdp", scatter_dimension=0, tiled=True
        ).astype(jnp.float32),
        lax.psum_scatter(
            column_sums[2].astype(jnp.bfloat16), "fsdp", scatter_dimension=0, tiled=True
        ).astype(jnp.float32),
        lax.psum_scatter(
            column_sums[3].astype(jnp.bfloat16), "fsdp", scatter_dimension=0, tiled=True
        ).astype(jnp.float32),
        lax.psum_scatter(
            gain_totals[1].astype(jnp.bfloat16), "fsdp", scatter_dimension=0, tiled=True
        ).astype(jnp.float32),
        lax.psum_scatter(
            column_sums[4].astype(jnp.bfloat16), "fsdp", scatter_dimension=0, tiled=True
        ).astype(jnp.float32),
        lax.psum_scatter(
            column_sums[5].astype(jnp.bfloat16), "fsdp", scatter_dimension=0, tiled=True
        ).astype(jnp.float32),
        lax.psum_scatter(
            column_sums[6].astype(jnp.bfloat16), "fsdp", scatter_dimension=0, tiled=True
        ).astype(jnp.float32),
    )
    gain_one_grad = finals[0]
    gain_two_grad = finals[5]
    matrices = (finals[1], finals[2], finals[3], finals[4], finals[6], finals[7], finals[8])
    return (
        layer_out[None],
        tokens_grad.astype(jnp.bfloat16)[None],
        gain_one_grad,
        matrices[0],
        matrices[1],
        matrices[2],
        matrices[3],
        gain_two_grad,
        matrices[4],
        matrices[5],
        matrices[6],
    )


def solution(mesh):
    return jax.shard_map(
        local,
        mesh=mesh,
        in_specs=(
            P("fsdp", "ctx", None),
            P("fsdp", None),
            P("fsdp"),
            P("fsdp", None),
            P("fsdp", None),
            P("fsdp", None),
            P("fsdp", None),
            P("fsdp"),
            P("fsdp", None),
            P("fsdp", None),
            P("fsdp", None),
            P("fsdp", "ctx", None),
        ),
        out_specs=(
            P("fsdp", "ctx", None),
            P("fsdp", "ctx", None),
            P("fsdp"),
            P("fsdp", "ctx"),
            P("fsdp", "ctx"),
            P("fsdp", "ctx"),
            P("fsdp", "ctx"),
            P("fsdp"),
            P("fsdp", "ctx"),
            P("fsdp", "ctx"),
            P("fsdp", "ctx"),
        ),
        check_vma=False,
    )
```
